32 devices in a mesh: batch: 4 (over x, core), var: 8 (over z, y).
Axes of the slice: x: 2, y: 2, z: 4, core: 2. Of those that a mesh axis runs over, the one named last changes fastest.
Arguments:
- inputs: bfloat16 [16, 2560, 512], P('batch', 'var'), may hold values from -6 to 6
- w_query: bfloat16 [512, 512], replicated, may hold values from -0.25 to 0.25
- w_key: bfloat16 [512, 512], replicated, may hold values from -0.25 to 0.25
- w_value: bfloat16 [512, 512], replicated, may hold values from -0.25 to 0.25
- w_out: bfloat16 [512, 512], replicated, may hold values from -4 to 4
- b_query: bfloat16 [512], replicated, may hold values from -3 to 3
- b_value: bfloat16 [512], replicated, may hold values from -1.1953125 to 1.1953125
- b_out: bfloat16 [512], replicated, may hold values from -3 to 3
- gain_one: bfloat16 [512], replicated, may hold values from 0.5 to 1.5
- shift_one: bfloat16 [512], replicated, may hold values from -1.796875 to 1.796875
- w_up: bfloat16 [512, 2048], replicated, may hold values from -0.25 to 0.25
- b_up: bfloat16 [2048], replicated, may hold values from -3 to 3
- w_down: bfloat16 [2048, 512], replicated, may hold values from -0.125 to 0.125
- b_down: bfloat16 [512], replicated, may hold values from -3 to 3
- gain_two: bfloat16 [512], replicated, may hold values from 0.5 to 1.5
- shift_two: bfloat16 [512], replicated, may hold values from -1.796875 to 1.796875
- cotangent: bfloat16 [16, 2560, 512], P('batch', 'var'), may hold values from -6 to 6
- valid_mask: int32 [2560], replicated, may hold values from 0 to 1, as said below
Outputs:
- activations: bfloat16 [16, 2560, 512], P('batch', 'var')
- grad_inputs: bfloat16 [16, 2560, 512], P('batch', 'var')
- grad_w_query: float32 [512, 512], replicated
- grad_w_key: float32 [512, 512], replicated
- grad_w_value: float32 [512, 512], replicated
- grad_w_out: float32 [512, 512], replicated
- grad_b_query: float32 [512], replicated
- grad_b_value: float32 [512], replicated
- grad_b_out: float32 [512], replicated
- grad_gain_one: float32 [512], replicated
- grad_shift_one: float32 [512], replicated
- grad_w_up: float32 [512, 2048], replicated
- grad_b_up: float32 [2048], replicated
- grad_w_down: float32 [2048, 512], replicated
- grad_b_down: float32 [512], replicated
- grad_gain_two: float32 [512], replicated
- grad_shift_two: float32 [512], replicated
The draws below stay inside these ranges and needn't reach their ends.
Inputs may be any that keep to these rules, and one draw needn't show every extreme that they name: `valid_mask`: exactly 2352 of the 2560 slots are 1, the rest 0; which slots is drawn from the seed.
All inputs are finite; a program needn't handle non-finite values.
Results may differ from the reference program's by a relative error of at most 0.015.
Values may be sent and summed in bfloat16 or wider, within the bound.
A program may use at most 640 MiB of HBM per device.

```python
import jax
import jax.numpy as jnp
from jax import lax

D = 512
HEADS = 8
FF = 2048
V = 2560
VALID = 2352
WINDOWS = 16


def draw_valid_mask(key, part):
    key = jax.random.fold_in(key, 5)
    order = jax.random.permutation(key, V)
    return (order < VALID).astype(jnp.int32)


def level_of(stream_key, dims, split, low, largest):
    factor_of, own = 1.0, jax.random.fold_in(stream_key, 6)
    for axis_at, blocks in split:
        steps = jnp.exp(jax.random.uniform(jax.random.fold_in(own, axis_at), (blocks,), jnp.float32, low / len(split), largest / len(split)))
        factor_of = factor_of * jnp.repeat(steps, dims[axis_at] // blocks).reshape([-1 if axis == axis_at else 1 for axis in range(len(dims))])
    return factor_of


def scatter_about(rng, shape, scale, bound, split=(), dtype=jnp.bfloat16):
    values = jax.random.normal(rng, shape, jnp.float32) * scale
    if len(split) > 0:
        values = level_of(rng, shape, split, -0.22, 0.18) * values
    return jnp.clip(values, min=-bound, max=bound).astype(dtype)


def setup_inputs(seed: int = 0) -> dict:
    arg_keys = jax.random.split(jax.random.key(seed), 19)
    inputs = scatter_about(arg_keys[0], (WINDOWS, V, D), 1.0, 6.0, ((0, 4), (1, 8)))
    w_query = scatter_about(arg_keys[1], (D, D), D ** -0.5, 0.25)
    w_key = scatter_about(arg_keys[2], (D, D), D ** -0.5, 0.25)
    w_value = scatter_about(arg_keys[3], (D, D), D ** -0.5, 0.25)
    w_out = scatter_about(arg_keys[4], (D, D), 2 ** -0.5, 4.0)
    b_query = scatter_about(arg_keys[5], (D,), 0.5, 3.0)
    b_value = scatter_about(arg_keys[6], (D,), 0.2, 1.1953125)
    b_out = scatter_about(arg_keys[7], (D,), 0.5, 3.0)
    gain_one = jnp.clip(1.0 + 0.1 * jax.random.normal(arg_keys[8], (D,), jnp.float32), 0.5, 1.5).astype(jnp.bfloat16)
    shift_one = scatter_about(arg_keys[9], (D,), 0.3, 1.796875)
    w_up = scatter_about(arg_keys[10], (D, FF), D ** -0.5, 0.25)
    b_up = scatter_about(arg_keys[11], (FF,), 0.5, 3.0)
    w_down = scatter_about(arg_keys[12], (FF, D), FF ** -0.5, 0.125)
    b_down = scatter_about(arg_keys[13], (D,), 0.5, 3.0)
    gain_two = jnp.clip(1.0 + 0.1 * jax.random.normal(arg_keys[14], (D,), jnp.float32), 0.5, 1.5).astype(jnp.bfloat16)
    shift_two = scatter_about(arg_keys[15], (D,), 0.3, 1.796875)
    cotangent = scatter_about(arg_keys[16], (WINDOWS, V, D), 1.0, 6.0, ((0, 4), (1, 8)))
    valid_mask = draw_valid_mask(jax.random.fold_in(arg_keys[18], 71), 0)
    return {"inputs": inputs, "w_query": w_query, "w_key": w_key, "w_value": w_value, "w_out": w_out, "b_query": b_query, "b_value": b_value, "b_out": b_out, "gain_one": gain_one, "shift_one": shift_one, "w_up": w_up, "b_up": b_up, "w_down": w_down, "b_down": b_down, "gain_two": gain_two, "shift_two": shift_two, "cotangent": cotangent, "valid_mask": valid_mask}


@jax.custom_vjp
def low(v):
    return lax.optimization_barrier(v.astype(jnp.bfloat16)).astype(jnp.float32)

@jax.custom_vjp
def low_back(v):
    return v

def low_keep(v):
    return (low(v), None)

def low_pass(kept, grad):
    return (grad,)

def back_keep(v):
    return (v, None)

def back_low(kept, grad):
    return (low(grad),)
low.defvjp(low_keep, low_pass)
low_back.defvjp(back_keep, back_low)

def normalize(rows, gain, shift):
    center = rows - lax.optimization_barrier(jnp.mean(rows, axis=-1, keepdims=True))
    spread = lax.optimization_barrier(jnp.mean(center * center, axis=-1, keepdims=True))
    return center * lax.rsqrt(spread + 1e-05) * gain + shift

def layer(params, block, allowed):
    w_query, w_key, w_value, w_out, b_query, b_value, b_out, gain_one, shift_one, w_up, b_up, w_down, b_down, gain_two, shift_two = params
    groups, slots, width = block.shape
    head_dim = width // HEADS
    highest = lax.Precision.HIGHEST

    def project(rows, weight):
        return jnp.einsum('gvd,de->gve', rows, weight, precision=highest)
    query = low_back(low(project(block, w_query) + b_query)).reshape(groups, slots, HEADS, head_dim)
    keys = low_back(low(project(block, w_key))).reshape(groups, slots, HEADS, head_dim)
    values = low_back(low(project(block, w_value) + b_value)).reshape(groups, slots, HEADS, head_dim)
    score = low_back(jnp.einsum('gqhc,gkhc->ghqk', query, keys, precision=highest) * head_dim ** (-0.5))
    score = jnp.where(allowed[None, None, None, :], score, -1e+30)
    top = lax.optimization_barrier(jnp.max(score, axis=-1, keepdims=True))
    expo = jnp.exp(score - top)
    prob = expo / lax.optimization_barrier(jnp.sum(expo, axis=-1, keepdims=True))
    attended = jnp.einsum('ghqk,gkhc->gqhc', low(prob), values, precision=highest)
    attended = low_back(low(attended)).reshape(groups, slots, width)
    branch = low_back(project(attended, w_out) + b_out)
    middle = normalize(block + branch, gain_one, shift_one)
    hidden_pre = low_back(project(low(middle), w_up) + b_up)
    act = jax.nn.gelu(hidden_pre, approximate=False)
    second = middle + low_back(project(low(act), w_down) + b_down)
    return normalize(second, gain_two, shift_two)

def reference(inputs, w_query, w_key, w_value, w_out, b_query, b_value, b_out, gain_one, shift_one, w_up, b_up, w_down, b_down, gain_two, shift_two, cotangent, valid_mask):
    params = tuple((p.astype(jnp.float32) for p in (w_query, w_key, w_value, w_out, b_query, b_value, b_out, gain_one, shift_one, w_up, b_up, w_down, b_down, gain_two, shift_two)))
    windows, slots, width = inputs.shape
    grouped = inputs.astype(jnp.float32).reshape(windows, 1, slots, width)
    allowed = valid_mask > 0
    checked = jax.checkpoint(layer)

    def whole(weights, data):

        def step(carry, block):
            return (carry, checked(weights, block, allowed))
        _, result = lax.scan(step, jnp.zeros((), jnp.float32), data)
        return result
    result, pullback = jax.vjp(whole, params, grouped)
    grads, d_inputs = pullback(cotangent.astype(jnp.float32).reshape(grouped.shape))
    return (result.reshape(windows, slots, width).astype(jnp.bfloat16), d_inputs.reshape(windows, slots, width).astype(jnp.bfloat16), grads[0], grads[1], grads[2], grads[3], grads[4], grads[5], grads[6], grads[7], grads[8], grads[9], grads[10], grads[11], grads[12], grads[13], grads[14])
```

```python
import functools

import jax
import jax.numpy as jnp
from jax import lax
from jax.experimental import pallas as pl
from jax.experimental.pallas import tpu as pltpu
from jax.sharding import PartitionSpec as P

HEADS = 8
LANES = 128
LOW = jnp.bfloat16
F32 = jnp.float32
MESH = pl.DeviceIdType.MESH
DMA = pltpu.SemaphoreType.DMA
VM = pl.BlockSpec(memory_space=pltpu.VMEM)
VMEM_BYTES = 60 << 20


def mm(left, right):
    return jnp.dot(left, right, preferred_element_type=F32)


def mm_nt(left, right):
    return lax.dot_general(left, right, (((1,), (1,)), ((), ())), preferred_element_type=F32)


def mm_tn(left, right):
    return lax.dot_general(left, right, (((0,), (0,)), ((), ())), preferred_element_type=F32)


def lane_of(shape):
    return lax.broadcasted_iota(jnp.int32, shape, len(shape) - 1)


def three_parts(value):
    high = value.astype(LOW)
    rest = value - high.astype(F32)
    mid = rest.astype(LOW)
    tail = (rest - mid.astype(F32)).astype(LOW)
    return high, mid, tail


class Plan:
    def __init__(self, mesh, inputs_shape):
        windows, slots, width = inputs_shape
        self.nv = mesh.shape["var"]
        self.nb = mesh.shape["batch"]
        self.nw = windows // self.nb
        self.local = slots // self.nv
        self.slots = slots
        self.width = width
        self.hd = width // HEADS
        self.cpw = self.nv // (2 * self.nw)
        self.groups = 2 * self.cpw
        self.hpd = HEADS // self.groups
        self.gw = self.hpd * self.hd
        self.rows = self.nw * self.local

    def here(self):
        b = lax.axis_index("batch")
        v = lax.axis_index("var")
        core = lax.rem(b, 2)
        window = v // self.cpw
        parity = window // self.nw
        slot = lax.rem(window, self.nw)
        group = lax.rem(v, self.cpw) * 2 + core
        return b, v, core, parity, slot, group


def loop(low, high, step):
    def run(index, carry):
        step(index)
        return carry

    lax.fori_loop(low, high, run, 0)


def enter(plan, b, v, core):
    barrier = pltpu.get_barrier_semaphore()
    partner = b + 1 - 2 * core

    def greet_same(o):
        pl.semaphore_signal(
            barrier, inc=1, device_id=(b, lax.rem(v + o, plan.nv)), device_id_type=MESH
        )

    def greet_other(o):
        pl.semaphore_signal(
            barrier, inc=1, device_id=(partner, lax.rem(v + o, plan.nv)), device_id_type=MESH
        )

    loop(1, plan.nv, greet_same)
    loop(0, plan.nv, greet_other)
    pl.semaphore_wait(barrier, 2 * plan.nv - 1)


def arrived(ref, sem):
    pltpu.make_async_copy(ref, ref, sem).wait()


def forward_kernel(
    plan, x, wq, wk, wv, bq, bv, mask,
    qa, ka, va, xw, att, got,
    waug, kaug, send, recv, pass_on, a_send, a_recv, local_sem,
):
    nv, nw, loc, hpd, hd = plan.nv, plan.nw, plan.local, plan.hpd, plan.hd
    b, v, core, parity, slot, group = plan.here()
    mine = parity == core
    partner = b + 1 - 2 * core
    owner = b - core + parity
    enter(plan, b, v, core)

    def out_copy(o):
        d = lax.rem(v + o, nv)
        return pltpu.make_async_remote_copy(
            src_ref=x.at[lax.rem(d // plan.cpw, nw)],
            dst_ref=xw.at[v],
            send_sem=send.at[o],
            recv_sem=recv.at[v],
            device_id=(b, d),
            device_id_type=MESH,
        )

    def wanted(o):
        return (lax.rem(v + o, nv) // plan.cpw) // nw == core

    def start_out(o):
        @pl.when(wanted(o))
        def _():
            out_copy(o).start()

    def end_out(o):
        @pl.when(wanted(o))
        def _():
            out_copy(o).wait_send()

    def forward_copy(s):
        return pltpu.make_async_remote_copy(
            src_ref=xw.at[s],
            dst_ref=xw.at[s],
            send_sem=pass_on.at[s],
            recv_sem=recv.at[s],
            device_id=(partner, v),
            device_id_type=MESH,
        )

    loop(1, nv, start_out)

    lane = lane_of((plan.width, LANES))
    base = pl.multiple_of(group * plan.gw, LANES)
    for kind, ref in enumerate((wq, wk, wv)):
        for pair in range(hpd // 2):
            both = ref[:, pl.ds(base + pair * LANES, LANES)].astype(F32)
            turned = pltpu.roll(both, hd, 1)
            at = (kind * hpd + 2 * pair) * LANES
            waug[:, at : at + LANES] = jnp.where(lane < hd, both, 0.0).astype(LOW)
            waug[:, at + LANES : at + 2 * LANES] = jnp.where(lane < hd, turned, 0.0).astype(LOW)

    square = lane_of((LANES, LANES))
    diag = square == lax.broadcasted_iota(jnp.int32, (LANES, LANES), 0)
    ones = jnp.where((square > hd) & (square < hd + 4), 1.0, 0.0)
    for at in range(plan.slots // LANES):
        row = jnp.where(mask[at : at + 1, :] > 0, 0.0, -1e30)
        column = jnp.sum(jnp.where(diag, row, 0.0), axis=1, keepdims=True)
        kaug[at * LANES : (at + 1) * LANES, :] = jnp.where(square == hd, column, ones).astype(LOW)

    tile = lane_of((loc, LANES))

    def bias_of(ref, h):
        pair = ref[:, pl.ds(base + (h // 2) * LANES, LANES)].astype(F32)
        if h % 2:
            pair = pltpu.roll(jnp.broadcast_to(pair, (8, LANES)), hd, 1)[0:1]
        return pair

    def project(s):
        block = xw[s]
        rows = pl.ds(pl.multiple_of(s * loc, 16), loc)
        extra = kaug[rows, :].astype(F32)
        both = mm(block, waug[...])
        for h in range(hpd):
            q = both[:, h * LANES : (h + 1) * LANES] + bias_of(bq, h)
            q = q.astype(LOW).astype(F32) * (hd**-0.5)
            qa[h, rows, :] = jnp.where(
                tile < hd, q, jnp.where(tile == hd, 1.0, 0.0)
            ).astype(LOW)
            k = both[:, (hpd + h) * LANES : (hpd + h + 1) * LANES]
            ka[h, rows, :] = jnp.where(tile < hd, k, extra).astype(LOW)
            val = both[:, (2 * hpd + h) * LANES : (2 * hpd + h + 1) * LANES] + bias_of(bv, h)
            va[h, rows, :] = jnp.where(
                tile < hd, val, jnp.where(tile < hd + 3, 1.0, 0.0)
            ).astype(LOW)

    @pl.when(mine)
    def _():
        own = pltpu.make_async_copy(x.at[slot], xw.at[v], local_sem)
        own.start()
        own.wait()
        forward_copy(v).start()
        project(v)

    def take(o):
        s = lax.rem(v + o, nv)
        arrived(xw.at[s], recv.at[s])

        @pl.when(mine)
        def _():
            forward_copy(s).start()

        project(s)

    loop(1, nv, take)

    @pl.when(jnp.logical_not(mine))
    def _():
        arrived(xw.at[v], recv.at[v])
        project(v)

    def send_copy(d, o):
        return pltpu.make_async_remote_copy(
            src_ref=att.at[d],
            dst_ref=got.at[slot, group],
            send_sem=a_send.at[o],
            recv_sem=a_recv.at[slot, group],
            device_id=(owner, d),
            device_id_type=MESH,
        )

    def own_copy():
        return pltpu.make_async_copy(att.at[v], got.at[slot, group], local_sem)

    def attend(o):
        d = lax.rem(v + o, nv)
        rows = pl.ds(pl.multiple_of(d * loc, 16), loc)
        done = []
        for h in range(hpd):
            q = qa[h, rows, :]
            score = mm_nt(q, ka[h])
            top = jnp.max(score, axis=1, keepdims=True)
            expo = jnp.exp(score - top)
            mixed = mm(expo.astype(LOW), va[h])
            total = mixed[:, hd : hd + 1]
            done.append(mixed / total)
            high, mid, tail = three_parts(-(top + jnp.log(total)))
            qa[h, rows, :] = jnp.where(
                tile == hd + 1,
                high,
                jnp.where(tile == hd + 2, mid, jnp.where(tile == hd + 3, tail, q)),
            )
        for pair in range(hpd // 2):
            att[d, :, pair * LANES : (pair + 1) * LANES] = jnp.where(
                tile < hd, done[2 * pair], pltpu.roll(done[2 * pair + 1], hd, 1)
            ).astype(LOW)

    def attend_and_send(o):
        attend(o)
        send_copy(lax.rem(v + o, nv), o).start()

    loop(1, nv, attend_and_send)
    attend(0)

    @pl.when(mine)
    def _():
        own_copy().start()
        own_copy().wait()

    @pl.when(jnp.logical_not(mine))
    def _():
        send_copy(v, 0).start()

    for w in range(nw):
        for g in range(plan.groups):

            @pl.when(jnp.logical_not(mine & (slot == w) & (group == g)))
            def _():
                arrived(got.at[w, g], a_recv.at[w, g])

    @pl.when(jnp.logical_not(mine))
    def _():
        send_copy(v, 0).wait_send()

    loop(1, nv, lambda o: send_copy(lax.rem(v + o, nv), o).wait_send())

    @pl.when(mine)
    def _():
        loop(0, nv, lambda s: forward_copy(s).wait_send())

    loop(1, nv, end_out)


def gelu_and_slope(pre):
    size = jnp.abs(pre)
    bell = jnp.exp(pre * pre * -0.5)
    t = 1.0 / (1.0 + 0.2316418882663604 * size)
    poly = t * (
        0.127414796
        + t * (-0.142248368 + t * (0.7107068705 + t * (-0.7265760135 + t * 0.5307027145)))
    )
    below = poly * bell
    phi = jnp.where(pre < 0, below, 1.0 - below)
    return pre * phi, phi + pre * bell * 0.3989422804014327


def fold_rows(value):
    rows, width = value.shape
    return jnp.sum(value.reshape(rows // 8, 8, width), axis=0)


def norm_parts(rows):
    center = rows - jnp.mean(rows, axis=-1, keepdims=True)
    spread = jnp.mean(center * center, axis=-1, keepdims=True)
    inverse = lax.rsqrt(spread + 1e-05)
    return center * inverse, inverse


def norm_back(unit, inverse, grad):
    return inverse * (
        grad
        - jnp.mean(grad, axis=-1, keepdims=True)
        - unit * jnp.mean(grad * unit, axis=-1, keepdims=True)
    )


def token_kernel(
    plan, ff, x, got, cot, wo, bo, g1, s1, wu, bu, wd, bd, g2, s2,
    out, d_first, d_att, gwo, gwu, gwd, small, small_up,
    att_s, mid_s, act_s, slope_s, pre_s, branch_s, dout_s, dsend,
    send, recv, local_sem,
):
    nv, nw, loc = plan.nv, plan.nw, plan.local
    b, v, core, parity, slot, group = plan.here()
    enter(plan, b, v, core)
    small[...] = jnp.zeros_like(small)
    small_up[...] = jnp.zeros_like(small_up)
    step = 512

    def up(ref):
        return ref[...].astype(F32)

    def target(w, g):
        return b - core + g % 2, (core * nw + w) * plan.cpw + g // 2

    def is_self(w, g):
        tb, tv = target(w, g)
        return (tb == b) & (tv == v)

    def remote(w, g):
        tb, tv = target(w, g)
        return pltpu.make_async_remote_copy(
            src_ref=dsend.at[w, g],
            dst_ref=d_att.at[v],
            send_sem=send.at[w, g],
            recv_sem=recv.at[v],
            device_id=(tb, tv),
            device_id_type=MESH,
        )

    def local(w, g):
        return pltpu.make_async_copy(dsend.at[w, g], d_att.at[v], local_sem)

    def window(i):
        w = lax.rem(v + i, nw)
        rows = pl.ds(pl.multiple_of(w * loc, 16), loc)
        att = jnp.concatenate([got[w, g] for g in range(plan.groups)], axis=1)
        att_s[rows, :] = att
        first = x[w].astype(F32) + mm(att, wo[...]) + up(bo)
        unit1, inv1 = norm_parts(first)
        middle = unit1 * up(g1) + up(s1)
        mid_low = middle.astype(LOW)
        mid_s[rows, :] = mid_low
        total = middle + up(bd)
        for f in range(0, ff, step):
            pre = mm(mid_low, wu[:, f : f + step]) + bu[:, f : f + step].astype(F32)
            act, slope = gelu_and_slope(pre)
            act_low = act.astype(LOW)
            act_s[rows, f : f + step] = act_low
            slope_s[:, f : f + step] = slope
            total = total + mm(act_low, wd[f : f + step, :])
        unit2, inv2 = norm_parts(total)
        out[w] = (unit2 * up(g2) + up(s2)).astype(LOW)
        grad = cot[w].astype(F32)
        small[0] += fold_rows(grad * unit2)
        small[1] += fold_rows(grad)
        d_second = norm_back(unit2, inv2, grad * up(g2))
        branch = d_second.astype(LOW)
        branch_s[rows, :] = branch
        small[2] += fold_rows(branch.astype(F32))
        d_middle = d_second
        for f in range(0, ff, step):
            d_pre = (mm_nt(branch, wd[f : f + step, :]) * slope_s[:, f : f + step]).astype(LOW)
            pre_s[rows, f : f + step] = d_pre
            small_up[:, f : f + step] += fold_rows(d_pre.astype(F32))
            d_middle = d_middle + mm_nt(d_pre, wu[:, f : f + step])
        small[3] += fold_rows(d_middle * unit1)
        small[4] += fold_rows(d_middle)
        d_one = norm_back(unit1, inv1, d_middle * up(g1))
        d_first[w] = d_one
        d_out = d_one.astype(LOW)
        dout_s[rows, :] = d_out
        small[5] += fold_rows(d_out.astype(F32))
        d_attended = mm_nt(d_out, wo[...]).astype(LOW)
        for g in range(plan.groups):
            dsend[w, g] = d_attended[:, g * plan.gw : (g + 1) * plan.gw]

            @pl.when(is_self(w, g))
            def _():
                local(w, g).start()

            @pl.when(jnp.logical_not(is_self(w, g)))
            def _():
                remote(w, g).start()

    loop(0, nw, window)

    gwo[...] = mm_tn(att_s[...], dout_s[...]).astype(LOW)
    for f in range(0, ff, step):
        gwu[:, f : f + step] = mm_tn(mid_s[...], pre_s[:, f : f + step]).astype(LOW)
        gwd[f : f + step, :] = mm_tn(act_s[:, f : f + step], branch_s[...]).astype(LOW)

    def take(s):
        @pl.when(jnp.logical_not((s == v) & (parity == core)))
        def _():
            arrived(d_att.at[s], recv.at[s])

    loop(0, nv, take)

    def finish(w):
        for g in range(plan.groups):

            @pl.when(is_self(w, g))
            def _():
                local(w, g).wait()

            @pl.when(jnp.logical_not(is_self(w, g)))
            def _():
                remote(w, g).wait_send()

    loop(0, nw, finish)


def backward_kernel(
    plan, qa, ka, va, att, d_att, xw, wq, wk, wv, d_first,
    gi, gwq, gwk, gwv, small,
    da, dqt, dk, dv, dall, part, mate, final, dx,
    p_send, p_recv, send, recv, local_sem,
):
    nv, nw, loc, hpd, hd = plan.nv, plan.nw, plan.local, plan.hpd, plan.hd
    slots, groups = plan.slots, plan.groups
    b, v, core, parity, slot, group = plan.here()
    mine = parity == core
    owner = b - core + parity
    base = pl.multiple_of(group * plan.gw, LANES)
    enter(plan, b, v, core)

    tile = lane_of((loc, LANES))

    def prepare(s):
        rows = pl.ds(pl.multiple_of(s * loc, 16), loc)
        for pair in range(hpd // 2):
            grad = d_att[s, :, pair * LANES : (pair + 1) * LANES].astype(F32)
            prod = grad * att[s, :, pair * LANES : (pair + 1) * LANES].astype(F32)
            for odd in range(2):
                mask = (tile >= hd) if odd else (tile < hd)
                delta = jnp.sum(jnp.where(mask, prod, 0.0), axis=1, keepdims=True)
                high, mid, tail = three_parts(-delta)
                turned = pltpu.roll(grad, hd, 1) if odd else grad
                da[2 * pair + odd, rows, :] = jnp.where(
                    tile < hd,
                    turned,
                    jnp.where(
                        tile == hd,
                        high.astype(F32),
                        jnp.where(
                            tile == hd + 1,
                            mid.astype(F32),
                            jnp.where(tile == hd + 2, tail.astype(F32), 0.0),
                        ),
                    ),
                ).astype(LOW)

    loop(0, nv, prepare)
    dk[...] = jnp.zeros_like(dk)
    dv[...] = jnp.zeros_like(dv)
    qb, kb = 256, slots // 2

    def queries(j):
        rows = pl.ds(pl.multiple_of(j * qb, qb), qb)
        for h in range(hpd):
            q = qa[h, rows, :]
            d = da[h, rows, :]
            total = None
            for i in range(slots // kb):
                keys = slice(i * kb, (i + 1) * kb)
                prob = jnp.exp(mm_nt(ka[h, keys, :], q))
                d_score = (prob * mm_nt(va[h, keys, :], d)).astype(LOW)
                dv[h, keys, :] += mm(prob.astype(LOW), d)
                dk[h, keys, :] += mm(d_score, q)
                piece = mm_tn(ka[h, keys, :], d_score)[:hd, :]
                total = piece if total is None else total + piece
            dqt[h * hd : (h + 1) * hd, rows] = total * (hd**-0.5)

    loop(0, slots // qb, queries)

    wide = lane_of((slots, LANES))
    for pair in range(hpd // 2):
        at = pair * LANES
        dall[:, at : at + LANES] = jnp.transpose(dqt[at : at + LANES, :]).astype(LOW)
        for kind, ref in ((1, dk), (2, dv)):
            to = kind * plan.gw + at
            dall[:, to : to + LANES] = jnp.where(
                wide < hd, ref[2 * pair], pltpu.roll(ref[2 * pair + 1], hd, 1)
            ).astype(LOW)

    def part_of(s):
        rows = pl.ds(pl.multiple_of(s * loc, 16), loc)
        total = mm_nt(dall[rows, 0 : plan.gw], wq[:, pl.ds(base, plan.gw)])
        total += mm_nt(dall[rows, plan.gw : 2 * plan.gw], wk[:, pl.ds(base, plan.gw)])
        total += mm_nt(dall[rows, 2 * plan.gw : 3 * plan.gw], wv[:, pl.ds(base, plan.gw)])
        return total

    share = nv // groups

    def device_of(g):
        return b - core + g % 2, v - lax.rem(v, plan.cpw) + g // 2

    def part_copy(g, i):
        return pltpu.make_async_remote_copy(
            src_ref=part.at[g * share + i],
            dst_ref=mate.at[group, i],
            send_sem=p_send.at[g, i],
            recv_sem=p_recv.at[group, i],
            device_id=device_of(g),
            device_id_type=MESH,
        )

    for g in range(groups):

        @pl.when(g != group)
        def _():
            for i in range(share):
                part[g * share + i] = part_of(g * share + i).astype(LOW)
                part_copy(g, i).start()

    def final_copy(d, i):
        return pltpu.make_async_remote_copy(
            src_ref=final.at[i],
            dst_ref=dx.at[slot],
            send_sem=send.at[i],
            recv_sem=recv.at[slot],
            device_id=(owner, d),
            device_id_type=MESH,
        )

    def is_own(d):
        return mine & (d == v)

    def own_copy(i):
        return pltpu.make_async_copy(final.at[i], dx.at[slot], local_sem)

    def settle(i):
        d = group * share + i
        total = part_of(d)
        for g in range(groups):

            @pl.when(g != group)
            def _():
                arrived(mate.at[g, i], p_recv.at[g, i])

            @pl.when(g == group)
            def _():
                mate[g, i] = jnp.zeros((loc, plan.width), LOW)

        for g in range(groups):
            total = total + mate[g, i].astype(F32)
        final[i] = total.astype(LOW)

        @pl.when(is_own(d))
        def _():
            own_copy(i).start()

        @pl.when(jnp.logical_not(is_own(d)))
        def _():
            final_copy(d, i).start()

    for i in range(share):
        settle(i)

    grads = mm_tn(xw[...], dall[...])
    gwq[...] = grads[:, 0 : plan.gw].astype(LOW)
    gwk[...] = grads[:, plan.gw : 2 * plan.gw].astype(LOW)
    gwv[...] = grads[:, 2 * plan.gw : 3 * plan.gw].astype(LOW)
    small[0] = fold_rows(dall[:, 0 : plan.gw].astype(F32))
    small[1] = fold_rows(dall[:, 2 * plan.gw : 3 * plan.gw].astype(F32))

    for i in range(share):

        @pl.when(is_own(group * share + i))
        def _():
            own_copy(i).wait()

    for w in range(nw):
        self_sent = mine & (slot == w) & (v // share == group)

        @pl.when(jnp.logical_not(self_sent))
        def _():
            arrived(dx.at[w], recv.at[w])

        gi[w] = (d_first[w] + dx[w].astype(F32)).astype(LOW)

    for i in range(share):

        @pl.when(jnp.logical_not(is_own(group * share + i)))
        def _():
            final_copy(group * share + i, i).wait_send()

    for g in range(groups):

        @pl.when(g != group)
        def _():
            for i in range(share):
                part_copy(g, i).wait_send()


def params(number):
    return pltpu.CompilerParams(
        vmem_limit_bytes=VMEM_BYTES, collective_id=number, has_side_effects=True
    )


def body(
    plan,
    inputs, w_query, w_key, w_value, w_out, b_query, b_value, b_out, gain_one, shift_one,
    w_up, b_up, w_down, b_down, gain_two, shift_two, cotangent, valid_mask,
):
    nv, nw, loc, width = plan.nv, plan.nw, plan.local, plan.width
    slots, hpd, hd, gw, groups = plan.slots, plan.hpd, plan.hd, plan.gw, plan.groups
    ff = w_up.shape[1]
    rows = plan.rows
    shape = jax.ShapeDtypeStruct

    def row(value):
        return value.reshape(1, -1)

    heads = shape((hpd, slots, LANES), LOW)
    qa, ka, va, xw, att, got = pl.pallas_call(
        functools.partial(forward_kernel, plan),
        out_shape=(
            heads,
            heads,
            heads,
            shape((nv, loc, width), LOW),
            shape((nv, loc, gw), LOW),
            shape((nw, groups, loc, gw), LOW),
        ),
        in_specs=[VM] * 7,
        out_specs=(VM,) * 6,
        scratch_shapes=[
            pltpu.VMEM((width, 3 * hpd * LANES), LOW),
            pltpu.VMEM((slots, LANES), LOW),
            DMA((nv,)),
            DMA((nv,)),
            DMA((nv,)),
            DMA((nv,)),
            DMA((nw, groups)),
            DMA,
        ],
        compiler_params=params(1),
        name="attention_forward",
    )(
        inputs, w_query, w_key, w_value, row(b_query), row(b_value),
        valid_mask.reshape(slots // LANES, LANES),
    )

    out, d_first, d_att, gwo, gwu, gwd, small, small_up = pl.pallas_call(
        functools.partial(token_kernel, plan, ff),
        out_shape=(
            shape((nw, loc, width), LOW),
            shape((nw, loc, width), F32),
            shape((nv, loc, gw), LOW),
            shape((width, width), LOW),
            shape((width, ff), LOW),
            shape((ff, width), LOW),
            shape((6, 8, width), F32),
            shape((8, ff), F32),
        ),
        in_specs=[VM] * 13,
        out_specs=(VM,) * 8,
        scratch_shapes=[
            pltpu.VMEM((rows, width), LOW),
            pltpu.VMEM((rows, width), LOW),
            pltpu.VMEM((rows, ff), LOW),
            pltpu.VMEM((loc, ff), F32),
            pltpu.VMEM((rows, ff), LOW),
            pltpu.VMEM((rows, width), LOW),
            pltpu.VMEM((rows, width), LOW),
            pltpu.VMEM((nw, groups, loc, gw), LOW),
            DMA((nw, groups)),
            DMA((nv,)),
            DMA,
        ],
        compiler_params=params(2),
        name="token_part",
    )(
        inputs, got, cotangent, w_out, row(b_out), row(gain_one), row(shift_one),
        w_up, row(b_up), w_down, row(b_down), row(gain_two), row(shift_two),
    )

    axes = ("batch", "var")
    gwo, gwu, gwd = lax.psum((gwo, gwu, gwd), axes)

    share = nv // groups
    gi, gwq, gwk, gwv, small_b = pl.pallas_call(
        functools.partial(backward_kernel, plan),
        out_shape=(
            shape((nw, loc, width), LOW),
            shape((width, gw), LOW),
            shape((width, gw), LOW),
            shape((width, gw), LOW),
            shape((2, 8, gw), F32),
        ),
        in_specs=[VM] * 10,
        out_specs=(VM,) * 5,
        scratch_shapes=[
            pltpu.VMEM((hpd, slots, LANES), LOW),
            pltpu.VMEM((gw, slots), F32),
            pltpu.VMEM((hpd, slots, LANES), F32),
            pltpu.VMEM((hpd, slots, LANES), F32),
            pltpu.VMEM((slots, 3 * gw), LOW),
            pltpu.VMEM((nv, loc, width), LOW),
            pltpu.VMEM((groups, share, loc, width), LOW),
            pltpu.VMEM((share, loc, width), LOW),
            pltpu.VMEM((nw, loc, width), LOW),
            DMA((groups, share)),
            DMA((groups, share)),
            DMA((share,)),
            DMA((nw,)),
            DMA,
        ],
        compiler_params=params(3),
        name="attention_backward",
    )(
        qa, ka, va, att, d_att, xw.reshape(slots, width), w_query, w_key, w_value, d_first,
    )

    group = lax.rem(lax.axis_index("var"), plan.cpw) * 2 + lax.rem(lax.axis_index("batch"), 2)
    start = group * gw
    blank = jnp.zeros((3, width, width), LOW)
    blank = lax.dynamic_update_slice(blank, jnp.stack((gwq, gwk, gwv)), (0, 0, start))
    blank_b = jnp.zeros((2, width), F32)
    blank_b = lax.dynamic_update_slice(blank_b, jnp.sum(small_b, axis=1), (0, start))
    vectors = jnp.concatenate(
        [
            jnp.sum(small, axis=1).reshape(-1),
            jnp.sum(small_up, axis=0),
            blank_b.reshape(-1),
        ]
    )
    blank, vectors = lax.psum((blank, vectors.astype(F32)), axes)
    vec = vectors[: 6 * width].reshape(6, width)
    g_up = vectors[6 * width : 6 * width + ff]
    g_b = vectors[6 * width + ff :].reshape(2, width)
    return (
        out,
        gi,
        blank[0].astype(F32),
        blank[1].astype(F32),
        blank[2].astype(F32),
        gwo.astype(F32),
        g_b[0],
        g_b[1],
        vec[5],
        vec[3],
        vec[4],
        gwu.astype(F32),
        g_up,
        gwd.astype(F32),
        vec[2],
        vec[0],
        vec[1],
    )


def solution(mesh):
    data = P("batch", "var", None)

    def run(*args):
        plan = Plan(mesh, args[0].shape)
        return jax.shard_map(
            functools.partial(body, plan),
            mesh=mesh,
            in_specs=(data,) + (P(),) * 15 + (data, P()),
            out_specs=(data, data) + (P(),) * 15,
            check_vma=False,
        )(*args)

    return run
```

```python
import functools

import jax
import jax.numpy as jnp
from jax import lax
from jax.experimental import pallas as pl
from jax.experimental.pallas import tpu as pltpu
from jax.sharding import PartitionSpec as P

HEADS = 8
LANES = 128
LOW = jnp.bfloat16
F32 = jnp.float32
MESH = pl.DeviceIdType.MESH
DMA = pltpu.SemaphoreType.DMA
VM = pl.BlockSpec(memory_space=pltpu.VMEM)
VMEM_BYTES = 60 << 20


def mm(left, right):
    return jnp.dot(left, right, preferred_element_type=F32)


def mm_nt(left, right):
    return lax.dot_general(left, right, (((1,), (1,)), ((), ())), preferred_element_type=F32)


def mm_tn(left, right):
    return lax.dot_general(left, right, (((0,), (0,)), ((), ())), preferred_element_type=F32)


def lane_of(shape):
    return lax.broadcasted_iota(jnp.int32, shape, len(shape) - 1)


def in_half(lane, odd, hd):
    return (lane >= hd) == (odd == 1)


def extra_lane(lane, odd, hd):
    return jnp.where(in_half(lane, odd, hd), -1, lane - hd * (1 - odd))


def vec(ref):
    return ref[...].reshape(1, -1).astype(F32)


def three_parts(value):
    high = value.astype(LOW)
    rest = value - high.astype(F32)
    mid = rest.astype(LOW)
    tail = (rest - mid.astype(F32)).astype(LOW)
    return high, mid, tail


class Plan:
    def __init__(self, mesh, inputs_shape):
        windows, slots, width = inputs_shape
        self.nv = mesh.shape["var"]
        self.nb = mesh.shape["batch"]
        self.nw = windows // self.nb
        self.local = slots // self.nv
        self.slots = slots
        self.width = width
        self.hd = width // HEADS
        self.cpw = self.nv // (2 * self.nw)
        self.groups = 2 * self.cpw
        self.hpd = HEADS // self.groups
        self.pairs = max(self.hpd // 2, 1)
        self.pw = self.pairs * LANES
        self.rows = self.nw * self.local
        unit = 16 * self.nv * self.nb
        self.piece = -(-3 * width // unit) * unit

    def here(self):
        b = lax.axis_index("batch")
        v = lax.axis_index("var")
        core = lax.rem(b, 2)
        window = v // self.cpw
        parity = window // self.nw
        slot = lax.rem(window, self.nw)
        group = lax.rem(v, self.cpw) * 2 + core
        return b, v, core, parity, slot, group

    def odd(self, h, group):
        return lax.rem(group, 2) if self.hpd == 1 else h % 2

    def base(self, group):
        if self.hpd == 1:
            return pl.multiple_of((group // 2) * LANES, LANES)
        return pl.multiple_of(group * self.pw, LANES)


def loop(low, high, step):
    def run(index, carry):
        step(index)
        return carry

    lax.fori_loop(low, high, run, 0)


def enter(plan, b, v, core, across=False):
    barrier = pltpu.get_barrier_semaphore()
    partner = b + 1 - 2 * core

    def greet_same(o):
        pl.semaphore_signal(
            barrier, inc=1, device_id=(b, lax.rem(v + o, plan.nv)), device_id_type=MESH
        )

    def greet_other(o):
        pl.semaphore_signal(
            barrier, inc=1, device_id=(partner, lax.rem(v + o, plan.nv)), device_id_type=MESH
        )

    loop(1, plan.nv, greet_same)
    loop(0, plan.nv, greet_other)
    count = 2 * plan.nv - 1
    if across:
        pl.semaphore_signal(
            barrier, inc=1, device_id=(b + 2 - 4 * (b // 2), v), device_id_type=MESH
        )
        count += 1
    pl.semaphore_wait(barrier, count)


def arrived(ref, sem):
    pltpu.make_async_copy(ref, ref, sem).wait()


def forward_kernel(
    plan, x, wq, wk, wv, bq, bv, mask,
    qa, ka, va, xw, att, got,
    waug, kaug, send, recv, pass_on, a_send, a_recv, local_sem,
):
    nv, nw, loc, hpd, hd = plan.nv, plan.nw, plan.local, plan.hpd, plan.hd
    b, v, core, parity, slot, group = plan.here()
    mine = parity == core
    partner = b + 1 - 2 * core
    owner = b - core + parity
    odds = [plan.odd(h, group) for h in range(hpd)]
    enter(plan, b, v, core)

    def out_copy(o):
        d = lax.rem(v + o, nv)
        return pltpu.make_async_remote_copy(
            src_ref=x.at[lax.rem(d // plan.cpw, nw)],
            dst_ref=xw.at[v],
            send_sem=send.at[o],
            recv_sem=recv.at[v],
            device_id=(b, d),
            device_id_type=MESH,
        )

    def wanted(o):
        return (lax.rem(v + o, nv) // plan.cpw) // nw == core

    def start_out(o):
        @pl.when(wanted(o))
        def _():
            out_copy(o).start()

    def end_out(o):
        @pl.when(wanted(o))
        def _():
            out_copy(o).wait_send()

    def forward_copy(s):
        return pltpu.make_async_remote_copy(
            src_ref=xw.at[s],
            dst_ref=xw.at[s],
            send_sem=pass_on.at[s],
            recv_sem=recv.at[s],
            device_id=(partner, v),
            device_id_type=MESH,
        )

    loop(1, nv, start_out)

    lane = lane_of((plan.width, LANES))
    base = plan.base(group)
    for kind, ref in enumerate((wq, wk, wv)):
        for h in range(hpd):
            both = ref[:, pl.ds(base + (h // 2) * LANES, LANES)].astype(F32)
            at = (kind * hpd + h) * LANES
            waug[:, at : at + LANES] = jnp.where(in_half(lane, odds[h], hd), both, 0.0).astype(LOW)

    square = lane_of((LANES, LANES))
    diag = square == lax.broadcasted_iota(jnp.int32, (LANES, LANES), 0)
    place = lax.rem(square, hd)
    ones = jnp.where((place > 0) & (place < 4), 1.0, 0.0)
    for at in range(plan.slots // LANES):
        row = jnp.where(mask[at : at + 1, :] > 0, 0.0, -1e30)
        column = jnp.sum(jnp.where(diag, row, 0.0), axis=1, keepdims=True)
        kaug[at * LANES : (at + 1) * LANES, :] = jnp.where(place == 0, column, ones).astype(LOW)

    tile = lane_of((loc, LANES))

    def bias_of(ref, h):
        return ref[:, pl.ds(base + (h // 2) * LANES, LANES)].astype(F32)

    def project(s):
        block = xw[s]
        rows = pl.ds(pl.multiple_of(s * loc, 16), loc)
        extra = kaug[rows, :].astype(F32)
        both = mm(block, waug[...])
        for h in range(hpd):
            data = in_half(tile, odds[h], hd)
            column = extra_lane(tile, odds[h], hd)
            q = both[:, h * LANES : (h + 1) * LANES] + bias_of(bq, h)
            q = q.astype(LOW).astype(F32) * (hd**-0.5)
            qa[h, rows, :] = jnp.where(data, q, jnp.where(column == 0, 1.0, 0.0)).astype(LOW)
            k = both[:, (hpd + h) * LANES : (hpd + h + 1) * LANES]
            ka[h, rows, :] = jnp.where(data, k, extra).astype(LOW)
            val = both[:, (2 * hpd + h) * LANES : (2 * hpd + h + 1) * LANES] + bias_of(bv, h)
            va[h, rows, :] = jnp.where(
                data, val, jnp.where((column >= 0) & (column < 3), 1.0, 0.0)
            ).astype(LOW)

    @pl.when(mine)
    def _():
        own = pltpu.make_async_copy(x.at[slot], xw.at[v], local_sem)
        own.start()
        own.wait()
        forward_copy(v).start()
        project(v)

    def take(o):
        s = lax.rem(v + o, nv)
        arrived(xw.at[s], recv.at[s])

        @pl.when(mine)
        def _():
            forward_copy(s).start()

        project(s)

    loop(1, nv, take)

    @pl.when(jnp.logical_not(mine))
    def _():
        arrived(xw.at[v], recv.at[v])
        project(v)

    def send_copy(d, o):
        return pltpu.make_async_remote_copy(
            src_ref=att.at[d],
            dst_ref=got.at[slot, group],
            send_sem=a_send.at[o],
            recv_sem=a_recv.at[slot, group],
            device_id=(owner, d),
            device_id_type=MESH,
        )

    def own_copy():
        return pltpu.make_async_copy(att.at[v], got.at[slot, group], local_sem)

    def attend(o):
        d = lax.rem(v + o, nv)
        rows = pl.ds(pl.multiple_of(d * loc, 16), loc)
        done = []
        for h in range(hpd):
            column = extra_lane(tile, odds[h], hd)
            q = qa[h, rows, :]
            score = mm_nt(q, ka[h])
            top = jnp.max(score, axis=1, keepdims=True)
            expo = jnp.exp(score - top)
            mixed = mm(expo.astype(LOW), va[h])
            if hpd == 1:
                total = jnp.where(odds[h] == 1, mixed[:, 0:1], mixed[:, hd : hd + 1])
            else:
                at = hd * (1 - odds[h])
                total = mixed[:, at : at + 1]
            done.append(mixed / total)
            high, mid, tail = three_parts(-(top + jnp.log(total)))
            qa[h, rows, :] = jnp.where(
                column == 1, high, jnp.where(column == 2, mid, jnp.where(column == 3, tail, q))
            )
        for pair in range(plan.pairs):
            other = 0.0 if hpd == 1 else done[2 * pair + 1]
            att[d, :, pair * LANES : (pair + 1) * LANES] = jnp.where(
                in_half(tile, odds[2 * pair], hd), done[2 * pair], other
            ).astype(LOW)

    def attend_and_send(o):
        attend(o)
        send_copy(lax.rem(v + o, nv), o).start()

    loop(1, nv, attend_and_send)
    attend(0)

    @pl.when(mine)
    def _():
        own_copy().start()
        own_copy().wait()

    @pl.when(jnp.logical_not(mine))
    def _():
        send_copy(v, 0).start()

    for w in range(nw):
        for g in range(plan.groups):

            @pl.when(jnp.logical_not(mine & (slot == w) & (group == g)))
            def _():
                arrived(got.at[w, g], a_recv.at[w, g])

    @pl.when(jnp.logical_not(mine))
    def _():
        send_copy(v, 0).wait_send()

    loop(1, nv, lambda o: send_copy(lax.rem(v + o, nv), o).wait_send())

    @pl.when(mine)
    def _():
        loop(0, nv, lambda s: forward_copy(s).wait_send())

    loop(1, nv, end_out)


def gelu_and_slope(pre):
    size = jnp.abs(pre)
    bell = jnp.exp(pre * pre * -0.5)
    t = 1.0 / (1.0 + 0.2316418882663604 * size)
    poly = t * (
        0.127414796
        + t * (-0.142248368 + t * (0.7107068705 + t * (-0.7265760135 + t * 0.5307027145)))
    )
    below = poly * bell
    phi = jnp.where(pre < 0, below, 1.0 - below)
    return pre * phi, phi + pre * bell * 0.3989422804014327


def fold_rows(value):
    rows, width = value.shape
    return jnp.sum(value.reshape(rows // 8, 8, width), axis=0)


def norm_parts(rows):
    center = rows - jnp.mean(rows, axis=-1, keepdims=True)
    spread = jnp.mean(center * center, axis=-1, keepdims=True)
    inverse = lax.rsqrt(spread + 1e-05)
    return center * inverse, inverse


def norm_back(unit, inverse, grad):
    return inverse * (
        grad
        - jnp.mean(grad, axis=-1, keepdims=True)
        - unit * jnp.mean(grad * unit, axis=-1, keepdims=True)
    )


def token_kernel(
    plan, ff, x, got, cot, wo, bo, g1, s1, wu, bu, wd, bd, g2, s2,
    out, d_first, d_att, pieces, small, small_up,
    att_s, mid_s, act_s, slope_s, pre_s, branch_s, dout_s, dsend,
    send, recv, local_sem,
):
    nv, nw, loc = plan.nv, plan.nw, plan.local
    b, v, core, parity, slot, group = plan.here()
    enter(plan, b, v, core)
    small[...] = jnp.zeros_like(small)
    small_up[...] = jnp.zeros_like(small_up)
    step = 512

    up = vec

    def target(w, g):
        return b - core + g % 2, (core * nw + w) * plan.cpw + g // 2

    def is_self(w, g):
        tb, tv = target(w, g)
        return (tb == b) & (tv == v)

    def remote(w, g):
        tb, tv = target(w, g)
        return pltpu.make_async_remote_copy(
            src_ref=dsend.at[w, g],
            dst_ref=d_att.at[v],
            send_sem=send.at[w, g],
            recv_sem=recv.at[v],
            device_id=(tb, tv),
            device_id_type=MESH,
        )

    def local(w, g):
        return pltpu.make_async_copy(dsend.at[w, g], d_att.at[v], local_sem)

    def window(i):
        w = lax.rem(v + i, nw)
        rows = pl.ds(pl.multiple_of(w * loc, 16), loc)
        if plan.hpd == 1:
            parts = [got[w, g] + got[w, g + 1] for g in range(0, plan.groups, 2)]
        else:
            parts = [got[w, g] for g in range(plan.groups)]
        att = jnp.concatenate(parts, axis=1)
        att_s[rows, :] = att
        first = x[w].astype(F32) + mm(att, wo[...]) + up(bo)
        unit1, inv1 = norm_parts(first)
        middle = unit1 * up(g1) + up(s1)
        mid_low = middle.astype(LOW)
        mid_s[rows, :] = mid_low
        total = middle + up(bd)
        for f in range(0, ff, step):
            pre = mm(mid_low, wu[:, f : f + step]) + bu[f : f + step].reshape(1, -1).astype(F32)
            act, slope = gelu_and_slope(pre)
            act_low = act.astype(LOW)
            act_s[rows, f : f + step] = act_low
            slope_s[:, f : f + step] = slope
            total = total + mm(act_low, wd[f : f + step, :])
        unit2, inv2 = norm_parts(total)
        out[w] = (unit2 * up(g2) + up(s2)).astype(LOW)
        grad = cot[w].astype(F32)
        small[0] += fold_rows(grad * unit2)
        small[1] += fold_rows(grad)
        d_second = norm_back(unit2, inv2, grad * up(g2))
        branch = d_second.astype(LOW)
        branch_s[rows, :] = branch
        small[2] += fold_rows(branch.astype(F32))
        d_middle = d_second
        for f in range(0, ff, step):
            d_pre = (mm_nt(branch, wd[f : f + step, :]) * slope_s[:, f : f + step]).astype(LOW)
            pre_s[rows, f : f + step] = d_pre
            small_up[:, f : f + step] += fold_rows(d_pre.astype(F32))
            d_middle = d_middle + mm_nt(d_pre, wu[:, f : f + step])
        small[3] += fold_rows(d_middle * unit1)
        small[4] += fold_rows(d_middle)
        d_one = norm_back(unit1, inv1, d_middle * up(g1))
        d_first[w] = d_one
        d_out = d_one.astype(LOW)
        dout_s[rows, :] = d_out
        small[5] += fold_rows(d_out.astype(F32))
        d_attended = mm_nt(d_out, wo[...]).astype(LOW)
        for g in range(plan.groups):
            at = (g // 2) * LANES if plan.hpd == 1 else g * plan.pw
            dsend[w, g] = d_attended[:, at : at + plan.pw]

            @pl.when(is_self(w, g))
            def _():
                local(w, g).start()

            @pl.when(jnp.logical_not(is_self(w, g)))
            def _():
                remote(w, g).start()

    loop(0, nw, window)

    if plan.piece > 3 * plan.width:
        pieces[:, 3 * plan.width :, :] = jnp.zeros_like(pieces[:, 3 * plan.width :, :])

    def put(block, value):
        at = (block % 3) * plan.width
        pieces[block // 3, at : at + plan.width, :] = value.astype(LOW)

    blocks = ff // step
    for f in range(blocks):
        put(f, mm_tn(mid_s[...], pre_s[:, f * step : (f + 1) * step]))
        put(blocks + f, mm_tn(act_s[:, f * step : (f + 1) * step], branch_s[...]))
    put(2 * blocks, mm_tn(att_s[...], dout_s[...]))

    def take(s):
        @pl.when(jnp.logical_not((s == v) & (parity == core)))
        def _():
            arrived(d_att.at[s], recv.at[s])

    loop(0, nv, take)

    def finish(w):
        for g in range(plan.groups):

            @pl.when(is_self(w, g))
            def _():
                local(w, g).wait()

            @pl.when(jnp.logical_not(is_self(w, g)))
            def _():
                remote(w, g).wait_send()

    loop(0, nw, finish)


def backward_kernel(
    plan, count, qa, ka, va, att, d_att, xw, wq, wk, wv, d_first, ga, small, small_up,
    gi, sums, vectors,
    da, kt, dqt, dk, dv, dall, wcat, part, mate, final, dx,
    gb, box1, half, box2, box3, fin, vec_mine, vec1, vec2, vec3,
    p_send, p_recv, send, recv, local_sem,
    s0, r0, l0, s1, r1, s2, r2, s3, r3, l3, s4, r4, s5, r5, vs, vr, vs3, vr3,
):
    nv, nw, loc, hpd, hd = plan.nv, plan.nw, plan.local, plan.hpd, plan.hd
    slots, groups, pw, width = plan.slots, plan.groups, plan.pw, plan.width
    b, v, core, parity, slot, group = plan.here()
    mine = parity == core
    owner = b - core + parity
    base = plan.base(group)
    odds = [plan.odd(h, group) for h in range(hpd)]
    xs = b // 2
    core_mate = (b + 1 - 2 * core, v)
    x_mate = (b + 2 - 4 * xs, v)
    enter(plan, b, v, core, across=True)

    half_rows = plan.piece // 2
    quarter = half_rows // 2
    chunk = quarter // nv

    def rows16(start, size):
        return pl.ds(pl.multiple_of(start, 16), size)

    def remote(src, dst, send_sem, recv_sem, device):
        return pltpu.make_async_remote_copy(
            src_ref=src, dst_ref=dst, send_sem=send_sem, recv_sem=recv_sem,
            device_id=device, device_id_type=MESH,
        )

    def core_copy(p, src):
        rows = rows16((1 - core) * half_rows, half_rows)
        return remote(src.at[rows, :], box1.at[p], s0.at[p], r0.at[p], core_mate)

    def half_copy(p, src):
        return pltpu.make_async_copy(
            src.at[rows16(core * half_rows, half_rows), :], half.at[p], l0.at[p]
        )

    def x_copy(p):
        rows = rows16((1 - xs) * quarter, quarter)
        return remote(half.at[p, rows, :], box2.at[p], s1.at[p], r1.at[p], x_mate)

    def var_copy(p, o):
        d = lax.rem(v + o, nv)
        rows = rows16(xs * quarter + d * chunk, chunk)
        return remote(half.at[p, rows, :], box3.at[p, v], s2.at[p, o], r2.at[p, v], (b, d))

    def chunk_at(p, who):
        return sums.at[p, rows16(core * half_rows + xs * quarter + who * chunk, chunk), :]

    def spread_copy(p, o):
        d = lax.rem(v + o, nv)
        return remote(fin.at[p], chunk_at(p, v), s3.at[p, o], r3.at[p, v], (b, d))

    def keep_copy(p):
        return pltpu.make_async_copy(fin.at[p], chunk_at(p, v), l3.at[p])

    def quarter_copy(p):
        at = sums.at[p, rows16(core * half_rows + xs * quarter, quarter), :]
        return remote(at, at, s4.at[p], r4.at[p], x_mate)

    def whole_half_copy(p):
        at = sums.at[p, rows16(core * half_rows, half_rows), :]
        return remote(at, at, s5.at[p], r5.at[p], core_mate)

    def step0(p, src):
        core_copy(p, src).start()
        half_copy(p, src).start()

    def step1(p, src):
        half_copy(p, src).wait()
        arrived(box1.at[p], r0.at[p])
        half[p] = (half[p].astype(F32) + box1[p].astype(F32)).astype(LOW)
        x_copy(p).start()

    def step2(p):
        arrived(box2.at[p], r1.at[p])
        x_copy(p).wait_send()
        rows = rows16(xs * quarter, quarter)
        half[p, rows, :] = (half[p, rows, :].astype(F32) + box2[p].astype(F32)).astype(LOW)
        loop(1, nv, lambda o: var_copy(p, o).start())

    def step3(p):
        def take(o):
            s = lax.rem(v + o, nv)
            arrived(box3.at[p, s], r2.at[p, s])

        loop(1, nv, take)
        total = half[p, rows16(xs * quarter + v * chunk, chunk), :].astype(F32)
        for o in range(1, nv):
            total = total + box3[p, lax.rem(v + o, nv)].astype(F32)
        fin[p] = total.astype(LOW)
        keep_copy(p).start()
        loop(1, nv, lambda o: spread_copy(p, o).start())

    def step4(p):
        def take(o):
            s = lax.rem(v + o, nv)
            arrived(chunk_at(p, s), r3.at[p, s])

        loop(1, nv, take)
        keep_copy(p).wait()
        quarter_copy(p).start()

    def step5(p):
        at = sums.at[p, rows16(core * half_rows + (1 - xs) * quarter, quarter), :]
        arrived(at, r4.at[p])
        whole_half_copy(p).start()

    def step6(p, src):
        at = sums.at[p, rows16((1 - core) * half_rows, half_rows), :]
        arrived(at, r5.at[p])
        core_copy(p, src).wait_send()
        loop(1, nv, lambda o: var_copy(p, o).wait_send())
        loop(1, nv, lambda o: spread_copy(p, o).wait_send())
        quarter_copy(p).wait_send()
        whole_half_copy(p).wait_send()

    def tick(t):
        for at, step in enumerate((
            lambda p: step0(p, ga.at[p]),
            lambda p: step1(p, ga.at[p]),
            step2,
            step3,
            step4,
            step5,
            lambda p: step6(p, ga.at[p]),
        )):
            p = t - at

            @pl.when((p >= 0) & (p < count))
            def _():
                step(p)

    tile = lane_of((loc, LANES))

    def prepare(s):
        rows = rows16(s * loc, loc)
        for h in range(hpd):
            at = (h // 2) * LANES
            data = in_half(tile, odds[h], hd)
            column = extra_lane(tile, odds[h], hd)
            grad = d_att[s, :, at : at + LANES].astype(F32)
            prod = grad * att[s, :, at : at + LANES].astype(F32)
            delta = jnp.sum(jnp.where(data, prod, 0.0), axis=1, keepdims=True)
            high, mid, tail = (part.astype(F32) for part in three_parts(-delta))
            extra = jnp.where(column == 0, high, jnp.where(column == 1, mid, tail))
            da[h, rows, :] = jnp.where(
                data, grad, jnp.where((column >= 0) & (column < 3), extra, 0.0)
            ).astype(LOW)

    loop(0, nv, prepare)
    for h in range(hpd):
        turned = jnp.transpose(ka[h])
        if hpd == 1:
            kt[h] = jnp.where(odds[h] == 1, turned[hd:], turned[:hd])
        else:
            kt[h] = turned[odds[h] * hd : (odds[h] + 1) * hd]
    for kind, ref in enumerate((wq, wk, wv)):
        wcat[:, kind * pw : (kind + 1) * pw] = ref[:, pl.ds(base, pw)]
    dk[...] = jnp.zeros_like(dk)
    dv[...] = jnp.zeros_like(dv)
    if hpd == 1:
        dqt[...] = jnp.zeros_like(dqt)
    qb, kb = 256, slots // 2
    key_lane = lane_of((kb, LANES))

    def queries(j):
        tick(j)
        rows = pl.ds(pl.multiple_of(j * qb, qb), qb)
        for pair in range(plan.pairs):
            heads = range(2 * pair, min(2 * pair + 2, hpd))
            totals = {h: None for h in heads}
            for i in range(slots // kb):
                keys = slice(i * kb, (i + 1) * kb)
                key_parts, value_parts = [], []
                for h in heads:
                    q = qa[h, rows, :]
                    d = da[h, rows, :]
                    prob = jnp.exp(mm_nt(ka[h, keys, :], q))
                    d_score = (prob * mm_nt(va[h, keys, :], d)).astype(LOW)
                    value_parts.append(mm(prob.astype(LOW), d))
                    key_parts.append(mm(d_score, q))
                    piece = mm(kt[h, :, keys], d_score)
                    totals[h] = piece if totals[h] is None else totals[h] + piece
                if hpd == 1:
                    key_parts.append(jnp.zeros_like(key_parts[0]))
                    value_parts.append(jnp.zeros_like(value_parts[0]))
                first = in_half(key_lane, odds[2 * pair], hd)
                dv[pair, keys, :] += jnp.where(first, value_parts[0], value_parts[1])
                dk[pair, keys, :] += jnp.where(first, key_parts[0], key_parts[1])
            for h in heads:
                at = pl.ds(pair * LANES + odds[h] * hd, hd)
                dqt[at, rows] = totals[h] * (hd**-0.5)

    loop(0, slots // qb, queries)

    for pair in range(plan.pairs):
        at = pair * LANES
        dall[:, at : at + LANES] = jnp.transpose(dqt[at : at + LANES, :]).astype(LOW)
        dall[:, pw + at : pw + at + LANES] = dk[pair].astype(LOW)
        dall[:, 2 * pw + at : 2 * pw + at + LANES] = dv[pair].astype(LOW)

    def part_of(s):
        return mm_nt(dall[rows16(s * loc, loc), :], wcat[...])

    share = nv // groups

    def device_of(g):
        return b - core + g % 2, v - lax.rem(v, plan.cpw) + g // 2

    def part_copy(g, i):
        return remote(
            part.at[g * share + i], mate.at[group, i], p_send.at[g, i], p_recv.at[group, i],
            device_of(g),
        )

    for g in range(groups):

        @pl.when(g != group)
        def _():
            for i in range(share):
                part[g * share + i] = part_of(g * share + i).astype(LOW)
                part_copy(g, i).start()

    gb[...] = jnp.zeros_like(gb)
    last = count
    for kind in range(3):
        grads = mm_tn(xw[...], dall[:, kind * pw : (kind + 1) * pw])
        gb[kind * width : (kind + 1) * width, pl.ds(base, pw)] = grads.astype(LOW)
    step0(last, gb)

    vec_mine[...] = jnp.zeros_like(vec_mine)
    for at in range(6):
        vec_mine[at : at + 1, :] = jnp.sum(small[at], axis=0, keepdims=True)
    ups = small_up.shape[1] // width
    for at in range(ups):
        vec_mine[6 + at : 7 + at, :] = jnp.sum(
            small_up[:, at * width : (at + 1) * width], axis=0, keepdims=True
        )
    for at, kind in enumerate((0, 2)):
        vec_mine[6 + ups + at : 7 + ups + at, pl.ds(base, pw)] = jnp.sum(
            dall[:, kind * pw : (kind + 1) * pw].astype(F32), axis=0, keepdims=True
        )

    def vec_copy(at, dst, device):
        return remote(vec_mine, dst, vs.at[at], vr.at[at], device)

    vec_copy(0, vec1, core_mate).start()

    def final_copy(d, i):
        return remote(final.at[i], dx.at[slot], send.at[i], recv.at[slot], (owner, d))

    def is_own(d):
        return mine & (d == v)

    def own_copy(i):
        return pltpu.make_async_copy(final.at[i], dx.at[slot], local_sem)

    def settle(i):
        d = group * share + i
        total = part_of(d)
        for g in range(groups):

            @pl.when(g != group)
            def _():
                arrived(mate.at[g, i], p_recv.at[g, i])

            @pl.when(g == group)
            def _():
                mate[g, i] = jnp.zeros((loc, width), LOW)

        for g in range(groups):
            total = total + mate[g, i].astype(F32)
        final[i] = total.astype(LOW)

        @pl.when(is_own(d))
        def _():
            own_copy(i).start()

        @pl.when(jnp.logical_not(is_own(d)))
        def _():
            final_copy(d, i).start()

    for i in range(share):
        settle(i)

    step1(last, gb)
    arrived(vec1, vr.at[0])
    vec_copy(0, vec1, core_mate).wait_send()
    vec_mine[...] = vec_mine[...] + vec1[...]
    vec_copy(1, vec2, x_mate).start()
    step2(last)
    arrived(vec2, vr.at[1])
    vec_copy(1, vec2, x_mate).wait_send()
    vec_mine[...] = vec_mine[...] + vec2[...]

    def vec_spread(o):
        d = lax.rem(v + o, nv)
        return remote(vec_mine, vec3.at[v], vs3.at[o], vr3.at[v], (b, d))

    loop(1, nv, lambda o: vec_spread(o).start())
    vec3[v] = vec_mine[...]
    step3(last)

    for i in range(share):

        @pl.when(is_own(group * share + i))
        def _():
            own_copy(i).wait()

    for w in range(nw):
        self_sent = mine & (slot == w) & (v // share == group)

        @pl.when(jnp.logical_not(self_sent))
        def _():
            arrived(dx.at[w], recv.at[w])

        gi[w] = (d_first[w] + dx[w].astype(F32)).astype(LOW)

    step4(last)

    def vec_take(o):
        s = lax.rem(v + o, nv)
        arrived(vec3.at[s], vr3.at[s])

    loop(1, nv, vec_take)
    total = vec3[0]
    for s in range(1, nv):
        total = total + vec3[s]
    vectors[...] = total
    step5(last)

    for i in range(share):

        @pl.when(jnp.logical_not(is_own(group * share + i)))
        def _():
            final_copy(group * share + i, i).wait_send()

    for g in range(groups):

        @pl.when(g != group)
        def _():
            for i in range(share):
                part_copy(g, i).wait_send()

    loop(1, nv, lambda o: vec_spread(o).wait_send())
    step6(last, gb)


def params(number):
    return pltpu.CompilerParams(
        vmem_limit_bytes=VMEM_BYTES, collective_id=number, has_side_effects=True
    )


def body(
    plan,
    inputs, w_query, w_key, w_value, w_out, b_query, b_value, b_out, gain_one, shift_one,
    w_up, b_up, w_down, b_down, gain_two, shift_two, cotangent, valid_mask,
):
    nv, nw, loc, width = plan.nv, plan.nw, plan.local, plan.width
    slots, hpd, hd, pw, groups = plan.slots, plan.hpd, plan.hd, plan.pw, plan.groups
    ff = w_up.shape[1]
    rows = plan.rows
    piece = plan.piece
    shape = jax.ShapeDtypeStruct
    ANY = pl.BlockSpec(memory_space=pl.ANY)

    heads = shape((hpd, slots, LANES), LOW)
    qa, ka, va, xw, att, got = pl.pallas_call(
        functools.partial(forward_kernel, plan),
        out_shape=(
            heads,
            heads,
            heads,
            shape((nv, loc, width), LOW),
            shape((nv, loc, pw), LOW),
            shape((nw, groups, loc, pw), LOW),
        ),
        in_specs=[VM] * 7,
        out_specs=(VM,) * 6,
        scratch_shapes=[
            pltpu.VMEM((width, 3 * hpd * LANES), LOW),
            pltpu.VMEM((slots, LANES), LOW),
            DMA((nv,)),
            DMA((nv,)),
            DMA((nv,)),
            DMA((nv,)),
            DMA((nw, groups)),
            DMA,
        ],
        compiler_params=params(1),
        name="attention_forward",
    )(
        inputs, w_query, w_key, w_value, b_query.reshape(1, width), b_value.reshape(1, width),
        valid_mask.reshape(slots // LANES, LANES),
    )

    count = (2 * ff // width + 1) // 3
    out, d_first, d_att, ga, small, small_up = pl.pallas_call(
        functools.partial(token_kernel, plan, ff),
        out_shape=(
            shape((nw, loc, width), LOW),
            shape((nw, loc, width), F32),
            shape((nv, loc, pw), LOW),
            shape((count, piece, width), LOW),
            shape((6, 8, width), F32),
            shape((8, ff), F32),
        ),
        in_specs=[VM] * 13,
        out_specs=(VM,) * 6,
        scratch_shapes=[
            pltpu.VMEM((rows, width), LOW),
            pltpu.VMEM((rows, width), LOW),
            pltpu.VMEM((rows, ff), LOW),
            pltpu.VMEM((loc, ff), F32),
            pltpu.VMEM((rows, ff), LOW),
            pltpu.VMEM((rows, width), LOW),
            pltpu.VMEM((rows, width), LOW),
            pltpu.VMEM((nw, groups, loc, pw), LOW),
            DMA((nw, groups)),
            DMA((nv,)),
            DMA,
        ],
        compiler_params=params(2),
        name="token_part",
    )(
        inputs, got, cotangent, w_out, b_out, gain_one, shift_one,
        w_up, b_up, w_down, b_down, gain_two, shift_two,
    )

    share = nv // groups
    every = count + 1
    gi, sums, vectors = pl.pallas_call(
        functools.partial(backward_kernel, plan, count),
        out_shape=(
            shape((nw, loc, width), LOW),
            shape((every, piece, width), LOW),
            shape((16, width), F32),
        ),
        in_specs=[VM] * 10 + [ANY, VM, VM],
        out_specs=(VM, ANY, VM),
        scratch_shapes=[
            pltpu.VMEM((hpd, slots, LANES), LOW),
            pltpu.VMEM((hpd, hd, slots), LOW),
            pltpu.VMEM((pw, slots), F32),
            pltpu.VMEM((plan.pairs, slots, LANES), F32),
            pltpu.VMEM((plan.pairs, slots, LANES), F32),
            pltpu.VMEM((slots, 3 * pw), LOW),
            pltpu.VMEM((width, 3 * pw), LOW),
            pltpu.VMEM((nv, loc, width), LOW),
            pltpu.VMEM((groups, share, loc, width), LOW),
            pltpu.VMEM((share, loc, width), LOW),
            pltpu.VMEM((nw, loc, width), LOW),
            pltpu.VMEM((piece, width), LOW),
            pltpu.VMEM((every, piece // 2, width), LOW),
            pltpu.VMEM((every, piece // 2, width), LOW),
            pltpu.VMEM((every, piece // 4, width), LOW),
            pltpu.VMEM((every, nv, piece // 4 // nv, width), LOW),
            pltpu.VMEM((every, piece // 4 // nv, width), LOW),
            pltpu.VMEM((16, width), F32),
            pltpu.VMEM((16, width), F32),
            pltpu.VMEM((16, width), F32),
            pltpu.VMEM((nv, 16, width), F32),
            DMA((groups, share)),
            DMA((groups, share)),
            DMA((share,)),
            DMA((nw,)),
            DMA,
            DMA((every,)),
            DMA((every,)),
            DMA((every,)),
            DMA((every,)),
            DMA((every,)),
            DMA((every, nv)),
            DMA((every, nv)),
            DMA((every, nv)),
            DMA((every, nv)),
            DMA((every,)),
            DMA((every,)),
            DMA((every,)),
            DMA((every,)),
            DMA((every,)),
            DMA((2,)),
            DMA((2,)),
            DMA((nv,)),
            DMA((nv,)),
        ],
        compiler_params=params(3),
        name="attention_backward",
    )(
        qa, ka, va, att, d_att, xw.reshape(slots, width), w_query, w_key, w_value, d_first,
        ga, small, small_up,
    )

    flat = sums[:, : 3 * width].reshape(every * 3, width, width).astype(F32)
    blocks = ff // width
    ups = vectors[6 : 6 + blocks].reshape(ff)
    return (
        out,
        gi,
        flat[3 * count],
        flat[3 * count + 1],
        flat[3 * count + 2],
        flat[2 * blocks],
        vectors[6 + blocks],
        vectors[7 + blocks],
        vectors[5],
        vectors[3],
        vectors[4],
        flat[:blocks].transpose(1, 0, 2).reshape(width, ff),
        ups,
        flat[blocks : 2 * blocks].reshape(ff, width),
        vectors[2],
        vectors[0],
        vectors[1],
    )


def solution(mesh):
    data = P("batch", "var", None)

    def run(*args):
        plan = Plan(mesh, args[0].shape)
        return jax.shard_map(
            functools.partial(body, plan),
            mesh=mesh,
            in_specs=(data,) + (P(),) * 15 + (data, P()),
            out_specs=(data, data) + (P(),) * 15,
            check_vma=False,
        )(*args)

    return run
```

```python
import functools

import jax
import jax.numpy as jnp
from jax import lax
from jax.experimental import pallas as pl
from jax.experimental.pallas import tpu as pltpu
from jax.sharding import PartitionSpec as P

HEADS = 8
LANES = 128
LOW = jnp.bfloat16
F32 = jnp.float32
MESH = pl.DeviceIdType.MESH
DMA = pltpu.SemaphoreType.DMA
VM = pl.BlockSpec(memory_space=pltpu.VMEM)
VMEM_BYTES = 62 << 20


def mm(left, right):
    return jnp.dot(left, right, preferred_element_type=F32)


def mm_nt(left, right):
    return lax.dot_general(left, right, (((1,), (1,)), ((), ())), preferred_element_type=F32)


def mm_tn(left, right):
    return lax.dot_general(left, right, (((0,), (0,)), ((), ())), preferred_element_type=F32)


def lane_of(shape):
    return lax.broadcasted_iota(jnp.int32, shape, len(shape) - 1)


def in_half(lane, odd, hd):
    return (lane >= hd) == (odd == 1)


def extra_lane(lane, odd, hd):
    return jnp.where(in_half(lane, odd, hd), -1, lane - hd * (1 - odd))


def vec(ref):
    return ref[...].reshape(1, -1).astype(F32)


def three_parts(value):
    high = value.astype(LOW)
    rest = value - high.astype(F32)
    mid = rest.astype(LOW)
    tail = (rest - mid.astype(F32)).astype(LOW)
    return high, mid, tail


class Plan:
    def __init__(self, mesh, inputs_shape):
        windows, slots, width = inputs_shape
        self.nv = mesh.shape["var"]
        self.nb = mesh.shape["batch"]
        self.nw = windows // self.nb
        self.local = slots // self.nv
        self.slots = slots
        self.width = width
        self.hd = width // HEADS
        self.cpw = self.nv // (2 * self.nw)
        self.groups = 2 * self.cpw
        self.hpd = HEADS // self.groups
        self.pairs = max(self.hpd // 2, 1)
        self.pw = self.pairs * LANES
        self.rows = self.nw * self.local
        self.sub = next(
            n for n in (5, 4, 2, 1)
            if self.local % (16 * n) == 0 and slots % (LANES * n) == 0
        )
        self.sr = self.local // self.sub
        self.st = self.nv * self.sr
        unit = 16 * self.nv * self.nb
        self.piece = -(-3 * width // unit) * unit

    def here(self):
        b = lax.axis_index("batch")
        v = lax.axis_index("var")
        core = lax.rem(b, 2)
        window = v // self.cpw
        parity = window // self.nw
        slot = lax.rem(window, self.nw)
        group = lax.rem(v, self.cpw) * 2 + core
        return b, v, core, parity, slot, group

    def odd(self, h, group):
        return lax.rem(group, 2) if self.hpd == 1 else h % 2

    def base(self, group):
        if self.hpd == 1:
            return pl.multiple_of((group // 2) * LANES, LANES)
        return pl.multiple_of(group * self.pw, LANES)


def loop(low, high, step):
    def run(index, carry):
        step(index)
        return carry

    lax.fori_loop(low, high, run, 0)


def enter(plan, b, v, core, across=False):
    barrier = pltpu.get_barrier_semaphore()
    partner = b + 1 - 2 * core

    def greet_same(o):
        pl.semaphore_signal(
            barrier, inc=1, device_id=(b, lax.rem(v + o, plan.nv)), device_id_type=MESH
        )

    def greet_other(o):
        pl.semaphore_signal(
            barrier, inc=1, device_id=(partner, lax.rem(v + o, plan.nv)), device_id_type=MESH
        )

    loop(1, plan.nv, greet_same)
    loop(0, plan.nv, greet_other)
    count = 2 * plan.nv - 1

    def greet_across(o):
        pl.semaphore_signal(
            barrier, inc=1, device_id=(b + 2 - 4 * (b // 2), lax.rem(v + o, plan.nv)),
            device_id_type=MESH,
        )

    if across:
        loop(0, plan.nv, greet_across)
        count += plan.nv
    pl.semaphore_wait(barrier, count)


def arrived(ref, sem):
    pltpu.make_async_copy(ref, ref, sem).wait()


def gelu_and_slope(pre):
    size = jnp.abs(pre)
    bell = jnp.exp(pre * pre * -0.5)
    t = 1.0 / (1.0 + 0.2316418882663604 * size)
    poly = t * (
        0.127414796
        + t * (-0.142248368 + t * (0.7107068705 + t * (-0.7265760135 + t * 0.5307027145)))
    )
    below = poly * bell
    phi = jnp.where(pre < 0, below, 1.0 - below)
    return pre * phi, phi + pre * bell * 0.3989422804014327


def fold_rows(value):
    rows, width = value.shape
    return jnp.sum(value.reshape(rows // 8, 8, width), axis=0)


def norm_parts(rows):
    center = rows - jnp.mean(rows, axis=-1, keepdims=True)
    spread = jnp.mean(center * center, axis=-1, keepdims=True)
    inverse = lax.rsqrt(spread + 1e-05)
    return center * inverse, inverse


def norm_back(unit, inverse, grad):
    return inverse * (
        grad
        - jnp.mean(grad, axis=-1, keepdims=True)
        - unit * jnp.mean(grad * unit, axis=-1, keepdims=True)
    )


def remote(src, dst, send_sem, recv_sem, device):
    return pltpu.make_async_remote_copy(
        src_ref=src, dst_ref=dst, send_sem=send_sem, recv_sem=recv_sem,
        device_id=device, device_id_type=MESH,
    )


def rows16(start, size):
    return pl.ds(pl.multiple_of(start, 16), size)


TOP = 8


def forward_kernel(
    plan, ff, x, wq, wk, wv, bq, bv, mask, cot, wo, bo, g1, s1, wu, bu, wd, bd, g2, s2,
    qa, ka, va, xw, att, out, d_first, d_att, pieces, small, small_up,
    waug, kaug, bias, acc, got, att_s, mid_s, act_s, slope_s, pre_s, branch_s, dout_s, dsend, stage,
    send, recv, pass_on, a_send, a_recv, a_local, d_send, d_recv, d_local, local_sem, stage_sem,
):
    nv, nw, hpd, hd, pw = plan.nv, plan.nw, plan.hpd, plan.hd, plan.pw
    sub, sr, st, width, groups = plan.sub, plan.sr, plan.st, plan.width, plan.groups
    b, v, core, parity, slot, group = plan.here()
    mine = parity == core
    partner = b + 1 - 2 * core
    owner = b - core + parity
    odds = [plan.odd(h, group) for h in range(hpd)]
    enter(plan, b, v, core)

    def out_copy(i, o):
        d = lax.rem(v + o, nv)
        return remote(
            x.at[lax.rem(d // plan.cpw, nw), i], xw.at[i, v], send.at[i, o], recv.at[i, v], (b, d)
        )

    def wanted(o):
        return (lax.rem(v + o, nv) // plan.cpw) // nw == core

    def start_out(n):
        @pl.when(wanted(lax.rem(n, nv)) & (lax.rem(n, nv) > 0))
        def _():
            out_copy(n // nv, lax.rem(n, nv)).start()

    def end_out(n):
        @pl.when(wanted(lax.rem(n, nv)) & (lax.rem(n, nv) > 0))
        def _():
            out_copy(n // nv, lax.rem(n, nv)).wait_send()

    def own_x():
        return pltpu.make_async_copy(x.at[slot], xw.at[:, v], local_sem)

    def forward_copy(i, s):
        at = xw.at[i, s]
        return remote(at, at, pass_on.at[i, s], recv.at[i, s], (partner, v))

    loop(0, sub * nv, start_out)

    @pl.when(mine)
    def _():
        own_x().start()

    lane = lane_of((width, LANES))
    base = plan.base(group)
    for kind, ref in enumerate((wq, wk, wv)):
        for h in range(hpd):
            both = ref[:, pl.ds(base + (h // 2) * LANES, LANES)].astype(F32)
            at = (kind * hpd + h) * LANES
            waug[:, at : at + LANES] = jnp.where(in_half(lane, odds[h], hd), both, 0.0).astype(LOW)
    bias[0:1, :] = vec(bq)
    bias[1:2, :] = vec(bv)

    square = lane_of((LANES, LANES))
    diag = square == lax.broadcasted_iota(jnp.int32, (LANES, LANES), 0)
    place = lax.rem(square, hd)
    ones = jnp.where((place > 0) & (place < 4), 1.0, 0.0)
    for at in range(plan.slots // LANES):
        row = jnp.where(mask[at : at + 1, :] > 0, 0.0, -1e30)
        column = jnp.sum(jnp.where(diag, row, 0.0), axis=1, keepdims=True)
        kaug[at * LANES : (at + 1) * LANES, :] = jnp.where(place == 0, column, ones).astype(LOW)

    tile = lane_of((st, LANES))
    data = [in_half(tile, odd, hd) for odd in odds]
    column = [extra_lane(tile, odd, hd) for odd in odds]

    def extra_column(value, h, at):
        if hpd == 1:
            return jnp.where(
                odds[h] == 1, value[:, at : at + 1], value[:, hd + at : hd + at + 1]
            )
        at += hd * (1 - odds[h])
        return value[:, at : at + 1]

    small[...] = jnp.zeros_like(small)
    small_up[...] = jnp.zeros_like(small_up)

    def bias_of(kind, h):
        return bias[kind : kind + 1, pl.ds(base + (h // 2) * LANES, LANES)]

    def project(i):
        rows = rows16(i * st, st)
        extra = kaug[rows, :].astype(F32)
        both = mm(xw[i].reshape(st, width), waug[...])
        for h in range(hpd):
            q = both[:, h * LANES : (h + 1) * LANES] + bias_of(0, h)
            q = q.astype(LOW).astype(F32) * (hd**-0.5)
            qa[h, rows, :] = jnp.where(data[h], q, jnp.where(column[h] == 0, 1.0, 0.0)).astype(LOW)
            k = both[:, (hpd + h) * LANES : (hpd + h + 1) * LANES]
            ka[h, rows, :] = jnp.where(data[h], k, extra).astype(LOW)
            val = both[:, (2 * hpd + h) * LANES : (2 * hpd + h + 1) * LANES] + bias_of(1, h)
            va[h, rows, :] = jnp.where(
                data[h], val, jnp.where((column[h] >= 0) & (column[h] < 3), 1.0, 0.0)
            ).astype(LOW)

    early = (sub + 1) // 2

    def attend(i, low, high, merge):
        rows = rows16(i * st, st)
        keys = slice(low * st, high * st)
        score = mm_nt(qa[0, rows, :], ka[0, keys, :])
        states = []
        for h in range(hpd):
            if h + 1 < hpd:
                ahead = mm_nt(qa[h + 1, rows, :], ka[h + 1, keys, :])
            top = jnp.max(score, axis=1, keepdims=True)
            if merge:
                state = acc[h, rows, :]
                old = extra_column(state, h, TOP)
                top = jnp.maximum(old, top)
            expo = jnp.exp(score - top)
            mixed = mm(expo.astype(LOW), va[h, keys, :])
            if merge:
                mixed = state * jnp.exp(old - top) + mixed
            states.append((top, mixed))
            score = ahead if h + 1 < hpd else None
        return states

    def attend_early(i):
        for h, (top, mixed) in enumerate(attend(i, 0, early, False)):
            acc[h, rows16(i * st, st), :] = jnp.where(column[h] == TOP, top, mixed)

    def att_copy(i, o):
        d = lax.rem(v + o, nv)
        return remote(
            att.at[i, d], got.at[slot, group, i], a_send.at[i, o], a_recv.at[slot, group, i],
            (owner, d),
        )

    def att_own(i):
        return pltpu.make_async_copy(att.at[i, v], got.at[slot, group, i], a_local.at[i])

    def settle(i, states):
        rows = rows16(i * st, st)
        done = []
        for h, (top, mixed) in enumerate(states):
            total = extra_column(mixed, h, 0)
            done.append(mixed / total)
            high, mid, tail = three_parts(-(top + jnp.log(total)))
            at = column[h]
            qa[h, rows, :] = jnp.where(
                at == 1, high, jnp.where(at == 2, mid, jnp.where(at == 3, tail, qa[h, rows, :]))
            )
        for pair in range(plan.pairs):
            other = 0.0 if hpd == 1 else done[2 * pair + 1]
            att[i, :, :, pair * LANES : (pair + 1) * LANES] = (
                jnp.where(data[2 * pair], done[2 * pair], other)
                .astype(LOW)
                .reshape(nv, sr, LANES)
            )
        loop(1, nv, lambda o: att_copy(i, o).start())

        @pl.when(mine)
        def _():
            att_own(i).start()

        @pl.when(jnp.logical_not(mine))
        def _():
            att_copy(i, 0).start()

    def arrive(i):
        def take(o):
            s = lax.rem(v + o, nv)
            arrived(xw.at[i, s], recv.at[i, s])

            @pl.when(mine)
            def _():
                forward_copy(i, s).start()

        loop(1, nv, take)

        @pl.when(jnp.logical_not(mine))
        def _():
            arrived(xw.at[i, v], recv.at[i, v])

        project(i)

    @pl.when(mine)
    def _():
        own_x().wait()
        loop(0, sub, lambda n: forward_copy(n, v).start())

    loop(0, early, arrive)

    def first_part(i):
        attend_early(i)

        @pl.when(early + i < sub)
        def _():
            arrive(early + i)

    if early < sub:
        loop(0, early, first_part)
        loop(0, early, lambda i: settle(i, attend(i, early, sub, True)))
    loop(early if early < sub else 0, sub, lambda i: settle(i, attend(i, 0, sub, False)))

    step = 512
    cr = nw * sr

    def target(w, g):
        return b - core + g % 2, (core * nw + w) * plan.cpw + g // 2

    def is_self(w, g):
        tb, tv = target(w, g)
        return (tb == b) & (tv == v)

    def grad_copy(i, w, g):
        return remote(
            dsend.at[i, w, g], d_att.at[i, v], d_send.at[i, w, g], d_recv.at[i, v], target(w, g)
        )

    def grad_own(i, w, g):
        return pltpu.make_async_copy(dsend.at[i, w, g], d_att.at[i, v], d_local.at[i])

    def tokens(i):
        for w in range(nw):
            for g in range(groups):
                own = mine & (slot == w) & (group == g)

                @pl.when(own)
                def _():
                    att_own(i).wait()

                @pl.when(jnp.logical_not(own))
                def _():
                    arrived(got.at[w, g, i], a_recv.at[w, g, i])

        rows = rows16(i * cr, cr)
        if hpd == 1:
            parts = [got[:, g, i] + got[:, g + 1, i] for g in range(0, groups, 2)]
        else:
            parts = [got[:, g, i] for g in range(groups)]
        attended = jnp.concatenate([part.reshape(cr, pw) for part in parts], axis=1)
        att_s[rows, :] = attended
        first = x[:, i].reshape(cr, width).astype(F32) + mm(attended, wo[...]) + vec(bo)
        unit1, inv1 = norm_parts(first)
        middle = unit1 * vec(g1) + vec(s1)
        mid_low = middle.astype(LOW)
        mid_s[rows, :] = mid_low
        total = middle + vec(bd)
        for f in range(0, ff, step):
            pre = mm(mid_low, wu[:, f : f + step]) + bu[f : f + step].reshape(1, -1).astype(F32)
            act, slope = gelu_and_slope(pre)
            act_low = act.astype(LOW)
            act_s[rows, f : f + step] = act_low
            slope_s[:, f : f + step] = slope
            total = total + mm(act_low, wd[f : f + step, :])
        unit2, inv2 = norm_parts(total)
        out[:, i] = (unit2 * vec(g2) + vec(s2)).astype(LOW).reshape(nw, sr, width)
        grad = cot[:, i].reshape(cr, width).astype(F32)
        small[0] += fold_rows(grad * unit2)
        small[1] += fold_rows(grad)
        d_second = norm_back(unit2, inv2, grad * vec(g2))
        branch = d_second.astype(LOW)
        branch_s[rows, :] = branch
        small[2] += fold_rows(branch.astype(F32))
        d_middle = d_second
        for f in range(0, ff, step):
            d_pre = (mm_nt(branch, wd[f : f + step, :]) * slope_s[:, f : f + step]).astype(LOW)
            pre_s[rows, f : f + step] = d_pre
            small_up[:, f : f + step] += fold_rows(d_pre.astype(F32))
            d_middle = d_middle + mm_nt(d_pre, wu[:, f : f + step])
        small[3] += fold_rows(d_middle * unit1)
        small[4] += fold_rows(d_middle)
        d_one = norm_back(unit1, inv1, d_middle * vec(g1))
        d_first[:, i] = d_one.reshape(nw, sr, width)
        d_out = d_one.astype(LOW)
        dout_s[rows, :] = d_out
        small[5] += fold_rows(d_out.astype(F32))
        d_attended = mm_nt(d_out, wo[...]).astype(LOW).reshape(nw, sr, width)
        for w in range(nw):
            for g in range(groups):
                at = (g // 2) * LANES if hpd == 1 else g * pw
                dsend[i, w, g] = d_attended[w, :, at : at + pw]

                @pl.when(is_self(w, g))
                def _():
                    grad_own(i, w, g).start()

                @pl.when(jnp.logical_not(is_self(w, g)))
                def _():
                    grad_copy(i, w, g).start()

    loop(0, sub, tokens)

    blocks = 2 * ff // step + 1
    spare = plan.piece - 3 * width

    def stage_copy(n):
        at = (n % 3) * width
        return pltpu.make_async_copy(
            stage.at[n % 2], pieces.at[n // 3, at : at + width, :], stage_sem.at[n % 2]
        )

    def put(n, value):
        if n >= 2:
            stage_copy(n - 2).wait()
        stage[n % 2] = value.astype(LOW)
        stage_copy(n).start()

    for f in range(ff // step):
        put(2 * f, mm_tn(mid_s[...], pre_s[:, f * step : (f + 1) * step]))
        put(2 * f + 1, mm_tn(act_s[:, f * step : (f + 1) * step], branch_s[...]))
    put(blocks - 1, mm_tn(att_s[...], dout_s[...]))
    stage_copy(blocks - 2).wait()
    stage_copy(blocks - 1).wait()
    if spare > 0:
        stage[0] = jnp.zeros_like(stage[0])
        for n in range(pieces.shape[0]):
            for at in range(0, spare, width):
                size = min(width, spare - at)
                pad = pltpu.make_async_copy(
                    stage.at[0, 0:size, :],
                    pieces.at[n, 3 * width + at : 3 * width + at + size, :],
                    stage_sem.at[0],
                )
                pad.start()
                pad.wait()

    def take(n):
        i, s = n // nv, lax.rem(n, nv)

        @pl.when(jnp.logical_not((s == v) & mine))
        def _():
            arrived(d_att.at[i, s], d_recv.at[i, s])

    loop(0, sub * nv, take)

    def finish(i):
        for w in range(nw):
            for g in range(groups):

                @pl.when(is_self(w, g))
                def _():
                    grad_own(i, w, g).wait()

                @pl.when(jnp.logical_not(is_self(w, g)))
                def _():
                    grad_copy(i, w, g).wait_send()

        @pl.when(jnp.logical_not(mine))
        def _():
            att_copy(i, 0).wait_send()

        loop(1, nv, lambda o: att_copy(i, o).wait_send())

        @pl.when(mine)
        def _():
            loop(0, nv, lambda s: forward_copy(i, s).wait_send())

    loop(0, sub, finish)
    loop(0, sub * nv, end_out)


class Sums:
    def __init__(self, plan, source, sums, box1, half, box2, box3, box4, fin, pair_sems, many_sems):
        self.plan, self.source, self.sums = plan, source, sums
        self.box1, self.half, self.box2, self.box3 = box1, half, box2, box3
        self.box4, self.fin = box4, fin
        self.s, self.m = pair_sems, many_sems
        b, v = lax.axis_index("batch"), lax.axis_index("var")
        self.b, self.v = b, v
        self.core, self.xs, self.lo, self.hi = lax.rem(b, 2), b // 2, lax.rem(v, 2), v // 2
        self.nh = plan.nv // 2
        self.half_rows = plan.piece // 2
        self.quarter, self.eighth = plan.piece // 4, plan.piece // 8
        self.chunk = self.eighth // self.nh

    def mate(self, p, first):
        over_x = (p % 2 == 0) if first else (p % 2 == 1)
        db, dv = self.b + 2 - 4 * self.xs, self.v + 1 - 2 * self.lo
        return jnp.where(over_x, db, self.b), jnp.where(over_x, self.v, dv)

    def coords(self, p):
        even = p % 2 == 0
        return jnp.where(even, self.xs, self.lo), jnp.where(even, self.lo, self.xs)

    def pair(self, p, at, src, dst, device):
        return remote(src, dst, self.s.at[0, at, p], self.s.at[1, at, p], device)

    def core_copy(self, p):
        rows = rows16((1 - self.core) * self.half_rows, self.half_rows)
        device = (self.b + 1 - 2 * self.core, self.v)
        return self.pair(p, 0, self.source(p).at[rows, :], self.box1.at[p], device)

    def own_copy(self, p):
        rows = rows16(self.core * self.half_rows, self.half_rows)
        return pltpu.make_async_copy(
            self.source(p).at[rows, :], self.half.at[p], self.s.at[0, 6, p]
        )

    def first_copy(self, p):
        c1, _ = self.coords(p)
        rows = rows16((1 - c1) * self.quarter, self.quarter)
        return self.pair(p, 1, self.half.at[p, rows, :], self.box2.at[p], self.mate(p, True))

    def second_copy(self, p):
        c1, c2 = self.coords(p)
        rows = rows16(c1 * self.quarter + (1 - c2) * self.eighth, self.eighth)
        return self.pair(p, 2, self.half.at[p, rows, :], self.box3.at[p], self.mate(p, False))

    def peer(self, o):
        return lax.rem(self.hi + o, self.nh)

    def many_copy(self, p, o):
        d = self.peer(o)
        c1, c2 = self.coords(p)
        rows = rows16(c1 * self.quarter + c2 * self.eighth + d * self.chunk, self.chunk)
        return remote(
            self.half.at[p, rows, :], self.box4.at[p, self.hi],
            self.m.at[0, 0, p, o], self.m.at[1, 0, p, self.hi], (self.b, d * 2 + self.lo),
        )

    def region(self, p, start, size):
        return self.sums.at[p, rows16(self.core * self.half_rows + start, size), :]

    def chunk_at(self, p, who):
        c1, c2 = self.coords(p)
        start = c1 * self.quarter + c2 * self.eighth + who * self.chunk
        return self.region(p, start, self.chunk)

    def spread_copy(self, p, o):
        return remote(
            self.fin.at[p], self.chunk_at(p, self.hi),
            self.m.at[0, 1, p, o], self.m.at[1, 1, p, self.hi],
            (self.b, self.peer(o) * 2 + self.lo),
        )

    def keep_copy(self, p):
        return pltpu.make_async_copy(
            self.fin.at[p], self.chunk_at(p, self.hi), self.s.at[0, 7, p]
        )

    def back_second(self, p):
        c1, c2 = self.coords(p)
        at = self.region(p, c1 * self.quarter + c2 * self.eighth, self.eighth)
        return self.pair(p, 3, at, at, self.mate(p, False))

    def back_first(self, p):
        c1, _ = self.coords(p)
        at = self.region(p, c1 * self.quarter, self.quarter)
        return self.pair(p, 4, at, at, self.mate(p, True))

    def back_core(self, p):
        at = self.region(p, 0, self.half_rows)
        return self.pair(p, 5, at, at, (self.b + 1 - 2 * self.core, self.v))

    def came(self, p, at, ref):
        arrived(ref, self.s.at[1, at, p])

    def step0(self, p):
        self.core_copy(p).start()
        self.own_copy(p).start()

    def step1(self, p):
        self.own_copy(p).wait()
        self.came(p, 0, self.box1.at[p])
        self.half[p] = (self.half[p].astype(F32) + self.box1[p].astype(F32)).astype(LOW)
        self.first_copy(p).start()

    def add(self, p, start, size, other):
        rows = rows16(start, size)
        total = self.half[p, rows, :].astype(F32) + other.astype(F32)
        self.half[p, rows, :] = total.astype(LOW)

    def step2(self, p):
        c1, _ = self.coords(p)
        self.came(p, 1, self.box2.at[p])
        self.first_copy(p).wait_send()
        self.add(p, c1 * self.quarter, self.quarter, self.box2[p])
        self.second_copy(p).start()

    def step3(self, p):
        c1, c2 = self.coords(p)
        self.came(p, 2, self.box3.at[p])
        self.second_copy(p).wait_send()
        self.add(p, c1 * self.quarter + c2 * self.eighth, self.eighth, self.box3[p])
        loop(1, self.nh, lambda o: self.many_copy(p, o).start())

    def step4(self, p):
        def take(o):
            s = self.peer(o)
            arrived(self.box4.at[p, s], self.m.at[1, 0, p, s])

        loop(1, self.nh, take)
        c1, c2 = self.coords(p)
        rows = rows16(c1 * self.quarter + c2 * self.eighth + self.hi * self.chunk, self.chunk)
        total = self.half[p, rows, :].astype(F32)
        for o in range(1, self.nh):
            total = total + self.box4[p, self.peer(o)].astype(F32)
        self.fin[p] = total.astype(LOW)
        self.keep_copy(p).start()
        loop(1, self.nh, lambda o: self.spread_copy(p, o).start())

    def step5(self, p):
        def take(o):
            s = self.peer(o)
            arrived(self.chunk_at(p, s), self.m.at[1, 1, p, s])

        loop(1, self.nh, take)
        self.keep_copy(p).wait()
        self.back_second(p).start()

    def step6(self, p):
        c1, c2 = self.coords(p)
        self.came(p, 3, self.region(p, c1 * self.quarter + (1 - c2) * self.eighth, self.eighth))
        self.back_first(p).start()

    def step7(self, p):
        c1, _ = self.coords(p)
        self.came(p, 4, self.region(p, (1 - c1) * self.quarter, self.quarter))
        self.back_core(p).start()

    def step8(self, p):
        rows = rows16((1 - self.core) * self.half_rows, self.half_rows)
        self.came(p, 5, self.sums.at[p, rows, :])
        self.core_copy(p).wait_send()
        loop(1, self.nh, lambda o: self.many_copy(p, o).wait_send())
        loop(1, self.nh, lambda o: self.spread_copy(p, o).wait_send())
        self.back_second(p).wait_send()
        self.back_first(p).wait_send()
        self.back_core(p).wait_send()

    DUE = (0, 2, 10, 15, 22, 29, 34, 42, 45)
    LAG = 3

    def at(self, tile, count):
        steps = (
            self.step0, self.step1, self.step2, self.step3, self.step4,
            self.step5, self.step6, self.step7, self.step8,
        )
        for due, step in reversed(tuple(zip(self.DUE, steps))):
            late = tile - due

            @pl.when((late >= 0) & (lax.rem(late, self.LAG) == 0) & (late < self.LAG * count))
            def _():
                step(late // self.LAG)

    def end(self, count):
        return self.DUE[-1] + self.LAG * (count - 1) + 1


class ShortSums:
    def __init__(self, plan, source, sums, box1, half, box2, fin, pair_sems, many_sems):
        self.plan, self.source, self.sums = plan, source, sums
        self.box1, self.half, self.box2, self.fin = box1, half, box2, fin
        self.s, self.m = pair_sems, many_sems
        b, v = lax.axis_index("batch"), lax.axis_index("var")
        self.b, self.v, self.core = b, v, lax.rem(b, 2)
        self.peers = 2 * plan.nv
        self.me = (b // 2) * plan.nv + v
        self.half_rows = plan.piece // 2
        self.chunk = self.half_rows // self.peers

    def peer(self, o):
        return lax.rem(self.me + o, self.peers)

    def device(self, j):
        return (j // self.plan.nv) * 2 + self.core, lax.rem(j, self.plan.nv)

    def core_copy(self, p):
        rows = rows16((1 - self.core) * self.half_rows, self.half_rows)
        return remote(
            self.source.at[p, rows, :], self.box1.at[p], self.s.at[0, 0, p], self.s.at[1, 0, p],
            (self.b + 1 - 2 * self.core, self.v),
        )

    def many_copy(self, p, o):
        j = self.peer(o)
        return remote(
            self.half.at[p, rows16(j * self.chunk, self.chunk), :], self.box2.at[p, self.me],
            self.m.at[0, 0, p, o], self.m.at[1, 0, p, self.me], self.device(j),
        )

    def chunk_at(self, p, j):
        rows = rows16(self.core * self.half_rows + j * self.chunk, self.chunk)
        return self.sums.at[p, rows, :]

    def spread_copy(self, p, o):
        return remote(
            self.fin.at[p], self.chunk_at(p, self.me),
            self.m.at[0, 1, p, o], self.m.at[1, 1, p, self.me], self.device(self.peer(o)),
        )

    def keep_copy(self, p):
        return pltpu.make_async_copy(
            self.fin.at[p], self.chunk_at(p, self.me), self.s.at[0, 2, p]
        )

    def back_core(self, p):
        at = self.sums.at[p, rows16(self.core * self.half_rows, self.half_rows), :]
        return remote(
            at, at, self.s.at[0, 1, p], self.s.at[1, 1, p],
            (self.b + 1 - 2 * self.core, self.v),
        )

    def step0(self, p):
        self.core_copy(p).start()

    def step1(self, p):
        arrived(self.box1.at[p], self.s.at[1, 0, p])
        rows = rows16(self.core * self.half_rows, self.half_rows)
        total = self.source[p, rows, :].astype(F32) + self.box1[p].astype(F32)
        self.half[p] = total.astype(LOW)
        loop(1, self.peers, lambda o: self.many_copy(p, o).start())

    def step2(self, p):
        def take(o):
            j = self.peer(o)
            arrived(self.box2.at[p, j], self.m.at[1, 0, p, j])

        loop(1, self.peers, take)
        total = self.half[p, rows16(self.me * self.chunk, self.chunk), :].astype(F32)
        for o in range(1, self.peers):
            total = total + self.box2[p, self.peer(o)].astype(F32)
        self.fin[p] = total.astype(LOW)
        self.keep_copy(p).start()
        loop(1, self.peers, lambda o: self.spread_copy(p, o).start())

    def step3(self, p):
        def take(o):
            j = self.peer(o)
            arrived(self.chunk_at(p, j), self.m.at[1, 1, p, j])

        loop(1, self.peers, take)
        self.keep_copy(p).wait()
        self.back_core(p).start()

    def step4(self, p):
        rows = rows16((1 - self.core) * self.half_rows, self.half_rows)
        arrived(self.sums.at[p, rows, :], self.s.at[1, 1, p])
        self.core_copy(p).wait_send()
        loop(1, self.peers, lambda o: self.many_copy(p, o).wait_send())
        loop(1, self.peers, lambda o: self.spread_copy(p, o).wait_send())
        self.back_core(p).wait_send()


def backward_kernel(
    plan, count, qa, ka, va, att, d_att, xw, wq, wk, wv, d_first, ga, small, small_up,
    gi, sums, sums_b, vectors,
    da, kt, dqt, dk, dv, dall, wcat, part, mate, own, final, dx, gacc, gb,
    box1, half, box2, box3, box4, fin, box1b, halfb, box2b, finb,
    vec_mine, vec1, vec2, xs, firsts,
    p_send, p_recv, send, recv, local_sem, sa, ma, sb, mb, vs, vs2, load,
):
    nv, nw, hpd, hd = plan.nv, plan.nw, plan.hpd, plan.hd
    sub, sr, st, pairs = plan.sub, plan.sr, plan.st, plan.pairs
    slots, groups, pw, width = plan.slots, plan.groups, plan.pw, plan.width
    b, v, core, parity, slot, group = plan.here()
    mine = parity == core
    owner = b - core + parity
    base = plan.base(group)
    odds = [plan.odd(h, group) for h in range(hpd)]
    core_mate = (b + 1 - 2 * core, v)
    x_copy = pltpu.make_async_copy(xw, xs, load.at[0])
    first_copy = pltpu.make_async_copy(d_first, firsts, load.at[1])
    x_copy.start()
    first_copy.start()
    enter(plan, b, v, core, across=True)
    tokens = Sums(
        plan, lambda p: ga.at[p], sums, box1, half, box2, box3, box4, fin, sa, ma
    )
    projections = ShortSums(plan, gb, sums_b, box1b, halfb, box2b, finb, sb, mb)

    tile = lane_of((st, LANES))

    def prepare(i):
        rows = rows16(i * st, st)
        for h in range(hpd):
            at = (h // 2) * LANES
            data = in_half(tile, odds[h], hd)
            column = extra_lane(tile, odds[h], hd)
            grad = d_att[i, :, :, at : at + LANES].reshape(st, LANES).astype(F32)
            prod = grad * att[i, :, :, at : at + LANES].reshape(st, LANES).astype(F32)
            delta = jnp.sum(jnp.where(data, prod, 0.0), axis=1, keepdims=True)
            high, mid, tail = (term.astype(F32) for term in three_parts(-delta))
            extra = jnp.where(column == 0, high, jnp.where(column == 1, mid, tail))
            da[h, rows, :] = jnp.where(
                data, grad, jnp.where((column >= 0) & (column < 3), extra, 0.0)
            ).astype(LOW)

    tokens.step0(0)
    loop(0, sub, prepare)
    for h in range(hpd):
        turned = jnp.transpose(ka[h])
        if hpd == 1:
            kt[h] = jnp.where(odds[h] == 1, turned[hd:], turned[:hd])
        else:
            kt[h] = turned[odds[h] * hd : (odds[h] + 1) * hd]
    for kind, ref in enumerate((wq, wk, wv)):
        wcat[:, kind * pw : (kind + 1) * pw] = ref[:, pl.ds(base, pw)]
    dk[...] = jnp.zeros_like(dk)
    dv[...] = jnp.zeros_like(dv)
    dqt[...] = jnp.zeros_like(dqt)
    gacc[...] = jnp.zeros_like(gacc)

    def attend(pair, qi, ki):
        rows, keys = pl.ds(pl.multiple_of(qi * st, st), st), pl.ds(pl.multiple_of(ki * st, st), st)
        key_parts, value_parts = [], []
        for h in range(2 * pair, min(2 * pair + 2, hpd)):
            q = qa[h, rows, :]
            d = da[h, rows, :]
            prob = jnp.exp(mm_nt(ka[h, keys, :], q))
            d_score = (prob * mm_nt(va[h, keys, :], d)).astype(LOW)
            value_parts.append(mm(prob.astype(LOW), d))
            key_parts.append(mm(d_score, q))
            dqt[pl.ds(pair * LANES + odds[h] * hd, hd), rows] += mm(kt[h, :, keys], d_score)
        if hpd == 1:
            key_parts.append(jnp.zeros_like(key_parts[0]))
            value_parts.append(jnp.zeros_like(value_parts[0]))
        first = in_half(tile, odds[2 * pair], hd)
        dv[pair, keys, :] += jnp.where(first, value_parts[0], value_parts[1])
        dk[pair, keys, :] += jnp.where(first, key_parts[0], key_parts[1])

    def gather_pair(pair, i):
        rows = rows16(i * st, st)
        at = pair * LANES
        dq = jnp.transpose(dqt[at : at + LANES, pl.ds(pl.multiple_of(i * st, st), st)])
        terms = (dq * (hd**-0.5), dk[pair, rows, :], dv[pair, rows, :])
        for kind, term in enumerate(terms):
            dall[rows, kind * pw + at : kind * pw + at + LANES] = term.astype(LOW)
        block = xs[rows, :]
        for kind, term in enumerate(terms):
            gacc[:, kind * LANES : (kind + 1) * LANES] += mm_tn(block, term.astype(LOW))

    lanes = gb.shape[-1]

    def put_pair(pair):
        if plan.piece > 3 * width or lanes > LANES:
            gb[pair] = jnp.zeros_like(gb[pair])
        at = base if hpd == 1 else pl.multiple_of(group * LANES, LANES)
        for kind in range(3):
            gb[pair, kind * width : (kind + 1) * width, pl.ds(at, LANES)] = gacc[
                :, kind * LANES : (kind + 1) * LANES
            ].astype(LOW)

    x_copy.wait()

    for pair in range(pairs - 1):

        def square(t):
            tokens.at(pair * sub * sub + t + 1, count)
            attend(pair, t // sub, lax.rem(t, sub))

        loop(0, sub * sub, square)
        loop(0, sub, lambda i: gather_pair(pair, i))
        put_pair(pair)
        projections.step0(pair)
        gacc[...] = jnp.zeros_like(gacc)

    last = pairs - 1
    before = last * sub * sub
    share = nv // groups
    mine_rows = share * sr

    def device_of(g):
        return b - core + g % 2, v - lax.rem(v, plan.cpw) + g // 2

    def part_copy(i, g):
        return remote(
            part.at[i, g * mine_rows : (g + 1) * mine_rows, :], mate.at[i, group],
            p_send.at[i, g], p_recv.at[i, group], device_of(g),
        )

    def send_parts(i):
        rows = rows16(i * st, st)
        total = mm_nt(dall[rows, :], wcat[...])
        part[i] = total.astype(LOW)
        own[i % 2] = total
        for g in range(groups):

            @pl.when(g != group)
            def _():
                part_copy(i, g).start()

    def final_copy(i, n):
        d = group * share + n
        return remote(
            final.at[i, n], dx.at[slot, i], send.at[i, n], recv.at[slot, i], (owner, d)
        )

    def is_own(n):
        return mine & (group * share + n == v)

    def own_copy(i, n):
        return pltpu.make_async_copy(final.at[i, n], dx.at[slot, i], local_sem.at[i])

    def send_final(i):
        total = own[i % 2, rows16(group * mine_rows, mine_rows), :]
        for g in range(groups):

            @pl.when(g != group)
            def _():
                arrived(mate.at[i, g], p_recv.at[i, g])

            @pl.when(g == group)
            def _():
                mate[i, g] = jnp.zeros((mine_rows, width), LOW)

        for g in range(groups):
            total = total + mate[i, g].astype(F32)
        final[i] = total.astype(LOW).reshape(share, sr, width)
        for n in range(share):

            @pl.when(is_own(n))
            def _():
                own_copy(i, n).start()

            @pl.when(jnp.logical_not(is_own(n)))
            def _():
                final_copy(i, n).start()

    def shrink(i):
        start = i * (2 * sub - i)

        def angle(t):
            done = start + t
            tokens.at(before + done + 1, count)
            if last > 0:
                for due, step in ((2, projections.step1), (12, projections.step2), (22, projections.step3)):

                    @pl.when(done == due)
                    def _():
                        step(last - 1)

            n = sub - i
            attend(
                last, jnp.where(t < n, i, i + 1 + t - n), jnp.where(t < n, i + t, i)
            )

        loop(0, 2 * (sub - i) - 1, angle)
        gather_pair(last, i)

        @pl.when(i == sub - 1)
        def _():
            put_pair(last)
            projections.step0(last)

        send_parts(i)

        @pl.when(i > 0)
        def _():
            send_final(i - 1)

    loop(0, sub, shrink)
    tiles = before + sub * sub
    loop(tiles + 1, max(tiles + 1, tokens.end(count)), lambda t: tokens.at(t, count))

    vec_mine[...] = jnp.zeros_like(vec_mine)
    for at in range(6):
        vec_mine[at : at + 1, :] = jnp.sum(small[at], axis=0, keepdims=True)
    ups = small_up.shape[1] // width
    for at in range(ups):
        vec_mine[6 + at : 7 + at, :] = jnp.sum(
            small_up[:, at * width : (at + 1) * width], axis=0, keepdims=True
        )
    for at, kind in enumerate((0, 2)):
        vec_mine[6 + ups + at : 7 + ups + at, pl.ds(base, pw)] = jnp.sum(
            dall[:, kind * pw : (kind + 1) * pw].astype(F32), axis=0, keepdims=True
        )

    core_vec = remote(vec_mine, vec1, vs.at[0], vs.at[1], core_mate)
    core_vec.start()
    send_final(sub - 1)
    projections.step1(last)
    arrived(vec1, vs.at[1])
    core_vec.wait_send()
    vec_mine[...] = vec_mine[...] + vec1[...]

    def vec_spread(o):
        return remote(
            vec_mine, vec2.at[projections.me], vs2.at[0, o], vs2.at[1, projections.me],
            projections.device(projections.peer(o)),
        )

    loop(1, 2 * nv, lambda o: vec_spread(o).start())
    vec2[projections.me] = vec_mine[...]
    first_copy.wait()

    def finish(i):
        for n in range(share):

            @pl.when(is_own(n))
            def _():
                own_copy(i, n).wait()

        for w in range(nw):
            self_sent = mine & (slot == w) & (v // share == group)

            @pl.when(jnp.logical_not(self_sent))
            def _():
                arrived(dx.at[w, i], recv.at[w, i])

        gi[:, i] = (firsts[:, i] + dx[:, i].astype(F32)).astype(LOW)

    loop(0, sub - 1, finish)
    if last > 0:
        projections.step4(last - 1)
    projections.step2(last)

    def vec_take(o):
        j = projections.peer(o)
        arrived(vec2.at[j], vs2.at[1, j])

    loop(1, 2 * nv, vec_take)
    total = vec2[0]
    for j in range(1, 2 * nv):
        total = total + vec2[j]
    vectors[...] = total
    loop(sub - 1, sub, finish)
    projections.step3(last)

    def close(i):
        for n in range(share):

            @pl.when(jnp.logical_not(is_own(n)))
            def _():
                final_copy(i, n).wait_send()

        for g in range(groups):

            @pl.when(g != group)
            def _():
                part_copy(i, g).wait_send()

    loop(0, sub, close)
    loop(1, 2 * nv, lambda o: vec_spread(o).wait_send())
    projections.step4(last)


def output_kernel(
    plan, ff, sums, sums_b, vectors,
    gq, gk, gv, go, gu, gd, bq, bv, bo, g1, s1, bu, bd, g2, s2,
):
    width = plan.width
    blocks = ff // width

    def block(n):
        at = (n % 3) * width
        return sums[n // 3, at : at + width, :].astype(F32)

    for f in range(blocks):
        gu[:, f * width : (f + 1) * width] = block(2 * f)
        gd[f * width : (f + 1) * width, :] = block(2 * f + 1)
    go[...] = block(2 * blocks)
    groups = sums_b.shape[-1] // LANES
    for kind, ref in enumerate((gq, gk, gv)):
        for pair in range(plan.pairs):
            for group in range(groups):
                at = (group * plan.pairs + pair) * LANES
                ref[:, at : at + LANES] = sums_b[
                    pair, kind * width : (kind + 1) * width, group * LANES : (group + 1) * LANES
                ].astype(F32)
    for n, ref in enumerate((g2, s2, bd, g1, s1, bo)):
        ref[...] = vectors[n]
    for f in range(blocks):
        bu[f * width : (f + 1) * width] = vectors[6 + f]
    bq[...] = vectors[6 + blocks]
    bv[...] = vectors[7 + blocks]


def params(number):
    return pltpu.CompilerParams(
        vmem_limit_bytes=VMEM_BYTES, collective_id=number, has_side_effects=True
    )


def sum_scratch(plan, number, lanes):
    piece = plan.piece
    nh = plan.nv // 2
    return [
        pltpu.VMEM((number, piece // 2, lanes), LOW),
        pltpu.VMEM((number, piece // 2, lanes), LOW),
        pltpu.VMEM((number, piece // 4, lanes), LOW),
        pltpu.VMEM((number, piece // 8, lanes), LOW),
        pltpu.VMEM((number, nh, piece // 8 // nh, lanes), LOW),
        pltpu.VMEM((number, piece // 8 // nh, lanes), LOW),
    ]


def short_scratch(plan, number, lanes):
    piece = plan.piece
    peers = 2 * plan.nv
    return [
        pltpu.VMEM((number, piece // 2, lanes), LOW),
        pltpu.VMEM((number, piece // 2, lanes), LOW),
        pltpu.VMEM((number, peers, piece // 2 // peers, lanes), LOW),
        pltpu.VMEM((number, piece // 2 // peers, lanes), LOW),
    ]


def sum_sems(number, steps, peers):
    return [DMA((2, steps, number)), DMA((2, 2, number, peers))]


def body(
    plan,
    inputs, w_query, w_key, w_value, w_out, b_query, b_value, b_out, gain_one, shift_one,
    w_up, b_up, w_down, b_down, gain_two, shift_two, cotangent, valid_mask,
):
    nv, nw, width = plan.nv, plan.nw, plan.width
    slots, hpd, hd, pw, groups = plan.slots, plan.hpd, plan.hd, plan.pw, plan.groups
    sub, sr, st, pairs = plan.sub, plan.sr, plan.st, plan.pairs
    ff = w_up.shape[1]
    rows, cr = plan.rows, nw * sr
    piece = plan.piece
    shape = jax.ShapeDtypeStruct
    ANY = pl.BlockSpec(memory_space=pl.ANY)
    count = (2 * ff // width + 1) // 3

    heads = shape((hpd, slots, LANES), LOW)
    blocked = (nw, sub, sr, width)
    mask = valid_mask.reshape(nv, sub, sr).transpose(1, 0, 2).reshape(slots // LANES, LANES)
    qa, ka, va, xw, att, out, d_first, d_att, ga, small, small_up = pl.pallas_call(
        functools.partial(forward_kernel, plan, ff),
        out_shape=(
            heads,
            heads,
            heads,
            shape((sub, nv, sr, width), LOW),
            shape((sub, nv, sr, pw), LOW),
            shape(blocked, LOW),
            shape(blocked, F32),
            shape((sub, nv, sr, pw), LOW),
            shape((count, piece, width), LOW),
            shape((6, 8, width), F32),
            shape((8, ff), F32),
        ),
        in_specs=[VM] * 18,
        out_specs=(VM,) * 8 + (ANY, VM, VM),
        scratch_shapes=[
            pltpu.VMEM((width, 3 * hpd * LANES), LOW),
            pltpu.VMEM((slots, LANES), LOW),
            pltpu.VMEM((8, width), F32),
            pltpu.VMEM((hpd, (sub + 1) // 2 * st, LANES), F32),
            pltpu.VMEM((nw, groups, sub, sr, pw), LOW),
            pltpu.VMEM((rows, width), LOW),
            pltpu.VMEM((rows, width), LOW),
            pltpu.VMEM((rows, ff), LOW),
            pltpu.VMEM((cr, ff), F32),
            pltpu.VMEM((rows, ff), LOW),
            pltpu.VMEM((rows, width), LOW),
            pltpu.VMEM((rows, width), LOW),
            pltpu.VMEM((sub, nw, groups, sr, pw), LOW),
            pltpu.VMEM((2, width, width), LOW),
            DMA((sub, nv)),
            DMA((sub, nv)),
            DMA((sub, nv)),
            DMA((sub, nv)),
            DMA((nw, groups, sub)),
            DMA((sub,)),
            DMA((sub, nw, groups)),
            DMA((sub, nv)),
            DMA((sub,)),
            DMA,
            DMA((2,)),
        ],
        compiler_params=params(1),
        name="forward_and_tokens",
    )(
        inputs.reshape(blocked), w_query, w_key, w_value, b_query, b_value, mask,
        cotangent.reshape(blocked), w_out, b_out, gain_one, shift_one,
        w_up, b_up, w_down, b_down, gain_two, shift_two,
    )

    share = nv // groups
    lanes = width // pairs
    gi, sums, sums_b, vectors = pl.pallas_call(
        functools.partial(backward_kernel, plan, count),
        out_shape=(
            shape(blocked, LOW),
            shape((count, piece, width), LOW),
            shape((pairs, piece, lanes), LOW),
            shape((16, width), F32),
        ),
        in_specs=[VM] * 5 + [ANY] + [VM] * 3 + [ANY, ANY, VM, VM],
        out_specs=(VM, ANY, ANY, VM),
        scratch_shapes=[
            pltpu.VMEM((hpd, slots, LANES), LOW),
            pltpu.VMEM((hpd, hd, slots), LOW),
            pltpu.VMEM((pw, slots), F32),
            pltpu.VMEM((pairs, slots, LANES), F32),
            pltpu.VMEM((pairs, slots, LANES), F32),
            pltpu.VMEM((slots, 3 * pw), LOW),
            pltpu.VMEM((width, 3 * pw), LOW),
            pltpu.VMEM((sub, st, width), LOW),
            pltpu.VMEM((sub, groups, share * sr, width), LOW),
            pltpu.VMEM((2, st, width), F32),
            pltpu.VMEM((sub, share, sr, width), LOW),
            pltpu.VMEM((nw, sub, sr, width), LOW),
            pltpu.VMEM((width, 3 * LANES), F32),
            pltpu.VMEM((pairs, piece, lanes), LOW),
        ]
        + sum_scratch(plan, count, width)
        + short_scratch(plan, pairs, lanes)
        + [
            pltpu.VMEM((16, width), F32),
            pltpu.VMEM((16, width), F32),
            pltpu.VMEM((2 * nv, 16, width), F32),
            pltpu.VMEM((slots, width), LOW),
            pltpu.VMEM(blocked, F32),
            DMA((sub, groups)),
            DMA((sub, groups)),
            DMA((sub, share)),
            DMA((nw, sub)),
            DMA((sub,)),
        ]
        + sum_sems(count, 8, nv // 2)
        + sum_sems(pairs, 3, 2 * nv)
        + [DMA((2,)), DMA((2, 2 * nv)), DMA((2,))],
        compiler_params=params(2),
        name="attention_backward",
    )(
        qa, ka, va, att, d_att, xw.reshape(slots, width), w_query, w_key, w_value, d_first,
        ga, small, small_up,
    )

    square = shape((width, width), F32)
    one = shape((width,), F32)
    gq, gk, gv, go, gu, gd, bq, bv, bo, g1, s1, bu, bd, g2, s2 = pl.pallas_call(
        functools.partial(output_kernel, plan, ff),
        out_shape=(square,) * 4
        + (shape((width, ff), F32), shape((ff, width), F32))
        + (one,) * 5
        + (shape((ff,), F32),)
        + (one,) * 3,
        in_specs=[VM] * 3,
        out_specs=(VM,) * 15,
        compiler_params=pltpu.CompilerParams(vmem_limit_bytes=VMEM_BYTES),
        name="outputs",
    )(sums, sums_b, vectors)
    return (
        out.reshape(inputs.shape), gi.reshape(inputs.shape),
        gq, gk, gv, go, bq, bv, bo, g1, s1, gu, bu, gd, bd, g2, s2,
    )


def solution(mesh):
    data = P("batch", "var", None)

    def run(*args):
        plan = Plan(mesh, args[0].shape)
        return jax.shard_map(
            functools.partial(body, plan),
            mesh=mesh,
            in_specs=(data,) + (P(),) * 15 + (data, P()),
            out_specs=(data, data) + (P(),) * 15,
            check_vma=False,
        )(*args)

    return run
```

```python
import functools

import jax
import jax.numpy as jnp
from jax import lax
from jax.experimental import pallas as pl
from jax.experimental.pallas import tpu as pltpu
from jax.sharding import PartitionSpec as P

HEADS = 8
LANES = 128
LOW = jnp.bfloat16
F32 = jnp.float32
MESH = pl.DeviceIdType.MESH
DMA = pltpu.SemaphoreType.DMA
VM = pl.BlockSpec(memory_space=pltpu.VMEM)
VMEM_BYTES = 62 << 20


def mm(left, right):
    return jnp.dot(left, right, preferred_element_type=F32)


def mm_nt(left, right):
    return lax.dot_general(left, right, (((1,), (1,)), ((), ())), preferred_element_type=F32)


def mm_tn(left, right):
    return lax.dot_general(left, right, (((0,), (0,)), ((), ())), preferred_element_type=F32)


def lane_of(shape):
    return lax.broadcasted_iota(jnp.int32, shape, len(shape) - 1)


def in_half(lane, odd, hd):
    return (lane >= hd) == (odd == 1)


def extra_lane(lane, odd, hd):
    return jnp.where(in_half(lane, odd, hd), -1, lane - hd * (1 - odd))


def vec(ref):
    return ref[...].reshape(1, -1).astype(F32)


def three_parts(value):
    high = value.astype(LOW)
    rest = value - high.astype(F32)
    mid = rest.astype(LOW)
    tail = (rest - mid.astype(F32)).astype(LOW)
    return high, mid, tail


class Plan:
    def __init__(self, mesh, inputs_shape):
        windows, slots, width = inputs_shape
        self.nv = mesh.shape["var"]
        self.nb = mesh.shape["batch"]
        self.nw = windows // self.nb
        self.local = slots // self.nv
        self.slots = slots
        self.width = width
        self.hd = width // HEADS
        self.cpw = self.nv // (2 * self.nw)
        self.groups = 2 * self.cpw
        self.hpd = HEADS // self.groups
        self.pairs = max(self.hpd // 2, 1)
        self.pw = self.pairs * LANES
        self.rows = self.nw * self.local
        self.sub = next(
            n for n in (5, 4, 2, 1)
            if self.local % (16 * n) == 0 and slots % (LANES * n) == 0
        )
        self.sr = self.local // self.sub
        self.st = self.nv * self.sr
        unit = 16 * self.nv * self.nb
        self.piece = -(-3 * width // unit) * unit

    def here(self):
        b = lax.axis_index("batch")
        v = lax.axis_index("var")
        core = lax.rem(b, 2)
        window = v // self.cpw
        parity = window // self.nw
        slot = lax.rem(window, self.nw)
        group = lax.rem(v, self.cpw) * 2 + core
        return b, v, core, parity, slot, group

    def odd(self, h, group):
        return lax.rem(group, 2) if self.hpd == 1 else h % 2

    def base(self, group):
        if self.hpd == 1:
            return pl.multiple_of((group // 2) * LANES, LANES)
        return pl.multiple_of(group * self.pw, LANES)


def loop(low, high, step):
    def run(index, carry):
        step(index)
        return carry

    lax.fori_loop(low, high, run, 0)


def enter(plan, b, v, core, across=False):
    barrier = pltpu.get_barrier_semaphore()
    partner = b + 1 - 2 * core

    def greet_same(o):
        pl.semaphore_signal(
            barrier, inc=1, device_id=(b, lax.rem(v + o, plan.nv)), device_id_type=MESH
        )

    def greet_other(o):
        pl.semaphore_signal(
            barrier, inc=1, device_id=(partner, lax.rem(v + o, plan.nv)), device_id_type=MESH
        )

    loop(1, plan.nv, greet_same)
    loop(0, plan.nv, greet_other)
    count = 2 * plan.nv - 1

    def greet_across(o):
        pl.semaphore_signal(
            barrier, inc=1, device_id=(b + 2 - 4 * (b // 2), lax.rem(v + o, plan.nv)),
            device_id_type=MESH,
        )

    if across:
        loop(0, plan.nv, greet_across)
        count += plan.nv
    pl.semaphore_wait(barrier, count)


def arrived(ref, sem):
    pltpu.make_async_copy(ref, ref, sem).wait()


def gelu_and_slope(pre):
    size = jnp.abs(pre)
    bell = jnp.exp(pre * pre * -0.5)
    t = 1.0 / (1.0 + 0.2316418882663604 * size)
    poly = t * (
        0.127414796
        + t * (-0.142248368 + t * (0.7107068705 + t * (-0.7265760135 + t * 0.5307027145)))
    )
    below = poly * bell
    phi = jnp.where(pre < 0, below, 1.0 - below)
    return pre * phi, phi + pre * bell * 0.3989422804014327


def fold_rows(value):
    rows, width = value.shape
    return jnp.sum(value.reshape(rows // 8, 8, width), axis=0)


def norm_parts(rows):
    center = rows - jnp.mean(rows, axis=-1, keepdims=True)
    spread = jnp.mean(center * center, axis=-1, keepdims=True)
    inverse = lax.rsqrt(spread + 1e-05)
    return center * inverse, inverse


def norm_back(unit, inverse, grad):
    return inverse * (
        grad
        - jnp.mean(grad, axis=-1, keepdims=True)
        - unit * jnp.mean(grad * unit, axis=-1, keepdims=True)
    )


def remote(src, dst, send_sem, recv_sem, device):
    return pltpu.make_async_remote_copy(
        src_ref=src, dst_ref=dst, send_sem=send_sem, recv_sem=recv_sem,
        device_id=device, device_id_type=MESH,
    )


def rows16(start, size):
    return pl.ds(pl.multiple_of(start, 16), size)


TOP = 8


def forward_kernel(
    plan, ff, x, wq, wk, wv, bq, bv, mask, cot, wo, bo, g1, s1, wu, bu, wd, bd, g2, s2,
    qa_out, ka_out, va_out, xw_out, att_out, out_out, first_out, d_att, pieces, small, small_up,
    qa, ka, va, xw, att, out, d_first, cot_s, wo_s, wu_s, wd_s,
    waug, kaug, bias, acc, got, att_s, mid_s, act_s, slope_s, pre_s, branch_s, dout_s, dsend, stage,
    send, recv, pass_on, a_send, a_recv, a_local, d_send, d_recv, d_local, local_sem, stage_sem,
    load, store,
):
    nv, nw, hpd, hd, pw = plan.nv, plan.nw, plan.hpd, plan.hd, plan.pw
    sub, sr, st, width, groups = plan.sub, plan.sr, plan.st, plan.width, plan.groups
    b, v, core, parity, slot, group = plan.here()
    mine = parity == core
    partner = b + 1 - 2 * core
    owner = b - core + parity
    odds = [plan.odd(h, group) for h in range(hpd)]
    loads = [
        pltpu.make_async_copy(src, dst, load.at[n])
        for n, (src, dst) in enumerate(((wo, wo_s), (wu, wu_s), (wd, wd_s), (cot, cot_s)))
    ]
    stores = [
        pltpu.make_async_copy(src, dst, store.at[n])
        for n, (src, dst) in enumerate((
            (xw, xw_out), (ka, ka_out), (va, va_out), (qa, qa_out), (att, att_out),
            (d_first, first_out), (out, out_out),
        ))
    ]
    enter(plan, b, v, core)

    def out_copy(i, o):
        d = lax.rem(v + o, nv)
        return remote(
            x.at[lax.rem(d // plan.cpw, nw), i], xw.at[i, v], send.at[i, o], recv.at[i, v], (b, d)
        )

    def wanted(o):
        return (lax.rem(v + o, nv) // plan.cpw) // nw == core

    def start_out(n):
        @pl.when(wanted(lax.rem(n, nv)) & (lax.rem(n, nv) > 0))
        def _():
            out_copy(n // nv, lax.rem(n, nv)).start()

    def end_out(n):
        @pl.when(wanted(lax.rem(n, nv)) & (lax.rem(n, nv) > 0))
        def _():
            out_copy(n // nv, lax.rem(n, nv)).wait_send()

    def own_x():
        return pltpu.make_async_copy(x.at[slot], xw.at[:, v], local_sem)

    def forward_copy(i, s):
        at = xw.at[i, s]
        return remote(at, at, pass_on.at[i, s], recv.at[i, s], (partner, v))

    loop(0, sub * nv, start_out)
    for copy in loads:
        copy.start()

    @pl.when(mine)
    def _():
        own_x().start()

    lane = lane_of((width, LANES))
    base = plan.base(group)
    for kind, ref in enumerate((wq, wk, wv)):
        for h in range(hpd):
            both = ref[:, pl.ds(base + (h // 2) * LANES, LANES)].astype(F32)
            at = (kind * hpd + h) * LANES
            waug[:, at : at + LANES] = jnp.where(in_half(lane, odds[h], hd), both, 0.0).astype(LOW)
    bias[0:1, :] = vec(bq)
    bias[1:2, :] = vec(bv)

    square = lane_of((LANES, LANES))
    diag = square == lax.broadcasted_iota(jnp.int32, (LANES, LANES), 0)
    place = lax.rem(square, hd)
    ones = jnp.where((place > 0) & (place < 4), 1.0, 0.0)
    for at in range(plan.slots // LANES):
        row = jnp.where(mask[at : at + 1, :] > 0, 0.0, -1e30)
        column = jnp.sum(jnp.where(diag, row, 0.0), axis=1, keepdims=True)
        kaug[at * LANES : (at + 1) * LANES, :] = jnp.where(place == 0, column, ones).astype(LOW)

    tile = lane_of((st, LANES))
    data = [in_half(tile, odd, hd) for odd in odds]
    column = [extra_lane(tile, odd, hd) for odd in odds]

    def extra_column(value, h, at):
        if hpd == 1:
            return jnp.where(
                odds[h] == 1, value[:, at : at + 1], value[:, hd + at : hd + at + 1]
            )
        at += hd * (1 - odds[h])
        return value[:, at : at + 1]

    small[...] = jnp.zeros_like(small)
    small_up[...] = jnp.zeros_like(small_up)

    def bias_of(kind, h):
        return bias[kind : kind + 1, pl.ds(base + (h // 2) * LANES, LANES)]

    def project(i):
        rows = rows16(i * st, st)
        extra = kaug[rows, :].astype(F32)
        both = mm(xw[i].reshape(st, width), waug[...])
        for h in range(hpd):
            q = both[:, h * LANES : (h + 1) * LANES] + bias_of(0, h)
            q = q.astype(LOW).astype(F32) * (hd**-0.5)
            qa[h, rows, :] = jnp.where(data[h], q, jnp.where(column[h] == 0, 1.0, 0.0)).astype(LOW)
            k = both[:, (hpd + h) * LANES : (hpd + h + 1) * LANES]
            ka[h, rows, :] = jnp.where(data[h], k, extra).astype(LOW)
            val = both[:, (2 * hpd + h) * LANES : (2 * hpd + h + 1) * LANES] + bias_of(1, h)
            va[h, rows, :] = jnp.where(
                data[h], val, jnp.where((column[h] >= 0) & (column[h] < 3), 1.0, 0.0)
            ).astype(LOW)

    early = (sub + 1) // 2

    def attend(i, low, high, merge):
        rows = rows16(i * st, st)
        keys = slice(low * st, high * st)
        score = mm_nt(qa[0, rows, :], ka[0, keys, :])
        states = []
        for h in range(hpd):
            if h + 1 < hpd:
                ahead = mm_nt(qa[h + 1, rows, :], ka[h + 1, keys, :])
            top = jnp.max(score, axis=1, keepdims=True)
            if merge:
                state = acc[h, rows, :]
                old = extra_column(state, h, TOP)
                top = jnp.maximum(old, top)
            expo = jnp.exp(score - top)
            mixed = mm(expo.astype(LOW), va[h, keys, :])
            if merge:
                mixed = state * jnp.exp(old - top) + mixed
            states.append((top, mixed))
            score = ahead if h + 1 < hpd else None
        return states

    def attend_early(i):
        for h, (top, mixed) in enumerate(attend(i, 0, early, False)):
            acc[h, rows16(i * st, st), :] = jnp.where(column[h] == TOP, top, mixed)

    def att_copy(i, o):
        d = lax.rem(v + o, nv)
        return remote(
            att.at[i, d], got.at[slot, group, i], a_send.at[i, o], a_recv.at[slot, group, i],
            (owner, d),
        )

    def att_own(i):
        return pltpu.make_async_copy(att.at[i, v], got.at[slot, group, i], a_local.at[i])

    def settle(i, states):
        rows = rows16(i * st, st)
        done = []
        for h, (top, mixed) in enumerate(states):
            total = extra_column(mixed, h, 0)
            done.append(mixed / total)
            high, mid, tail = three_parts(-(top + jnp.log(total)))
            at = column[h]
            qa[h, rows, :] = jnp.where(
                at == 1, high, jnp.where(at == 2, mid, jnp.where(at == 3, tail, qa[h, rows, :]))
            )
        for pair in range(plan.pairs):
            other = 0.0 if hpd == 1 else done[2 * pair + 1]
            att[i, :, :, pair * LANES : (pair + 1) * LANES] = (
                jnp.where(data[2 * pair], done[2 * pair], other)
                .astype(LOW)
                .reshape(nv, sr, LANES)
            )
        loop(1, nv, lambda o: att_copy(i, o).start())

        @pl.when(mine)
        def _():
            att_own(i).start()

        @pl.when(jnp.logical_not(mine))
        def _():
            att_copy(i, 0).start()

    def arrive(i):
        def take(o):
            s = lax.rem(v + o, nv)
            arrived(xw.at[i, s], recv.at[i, s])

            @pl.when(mine)
            def _():
                forward_copy(i, s).start()

        loop(1, nv, take)

        @pl.when(jnp.logical_not(mine))
        def _():
            arrived(xw.at[i, v], recv.at[i, v])

        project(i)

    @pl.when(mine)
    def _():
        own_x().wait()
        loop(0, sub, lambda n: forward_copy(n, v).start())

    loop(0, early, arrive)

    def first_part(i):
        attend_early(i)

        @pl.when(early + i < sub)
        def _():
            arrive(early + i)

    if early < sub:
        loop(0, early, first_part)
    for copy in stores[:3]:
        copy.start()
    if early < sub:
        loop(0, early, lambda i: settle(i, attend(i, early, sub, True)))
    loop(early if early < sub else 0, sub, lambda i: settle(i, attend(i, 0, sub, False)))

    for copy in stores[3:5]:
        copy.start()
    for copy in loads:
        copy.wait()

    step = 512
    cr = nw * sr

    def target(w, g):
        return b - core + g % 2, (core * nw + w) * plan.cpw + g // 2

    def is_self(w, g):
        tb, tv = target(w, g)
        return (tb == b) & (tv == v)

    def grad_copy(i, w, g):
        return remote(
            dsend.at[i, w, g], d_att.at[i, v], d_send.at[i, w, g], d_recv.at[i, v], target(w, g)
        )

    def grad_own(i, w, g):
        return pltpu.make_async_copy(dsend.at[i, w, g], d_att.at[i, v], d_local.at[i])

    def tokens(i):
        for w in range(nw):
            for g in range(groups):
                own = mine & (slot == w) & (group == g)

                @pl.when(own)
                def _():
                    att_own(i).wait()

                @pl.when(jnp.logical_not(own))
                def _():
                    arrived(got.at[w, g, i], a_recv.at[w, g, i])

        rows = rows16(i * cr, cr)
        if hpd == 1:
            parts = [got[:, g, i] + got[:, g + 1, i] for g in range(0, groups, 2)]
        else:
            parts = [got[:, g, i] for g in range(groups)]
        attended = jnp.concatenate([part.reshape(cr, pw) for part in parts], axis=1)
        att_s[rows, :] = attended
        first = x[:, i].reshape(cr, width).astype(F32) + mm(attended, wo_s[...]) + vec(bo)
        unit1, inv1 = norm_parts(first)
        middle = unit1 * vec(g1) + vec(s1)
        mid_low = middle.astype(LOW)
        mid_s[rows, :] = mid_low
        total = middle + vec(bd)

        def before(f):
            return mm(mid_low, wu_s[:, f : f + step]) + bu[f : f + step].reshape(1, -1).astype(F32)

        pre = before(0)
        for f in range(0, ff, step):
            ahead = before(f + step) if f + step < ff else None
            act, slope = gelu_and_slope(pre)
            act_low = act.astype(LOW)
            act_s[rows, f : f + step] = act_low
            slope_s[:, f : f + step] = slope
            total = total + mm(act_low, wd_s[f : f + step, :])
            pre = ahead
        unit2, inv2 = norm_parts(total)
        out[:, i] = (unit2 * vec(g2) + vec(s2)).astype(LOW).reshape(nw, sr, width)
        grad = cot_s[:, i].reshape(cr, width).astype(F32)
        small[0] += fold_rows(grad * unit2)
        small[1] += fold_rows(grad)
        d_second = norm_back(unit2, inv2, grad * vec(g2))
        branch = d_second.astype(LOW)
        branch_s[rows, :] = branch
        small[2] += fold_rows(branch.astype(F32))
        d_middle = d_second

        def back(f):
            return mm_nt(branch, wd_s[f : f + step, :])

        d_act = back(0)
        for f in range(0, ff, step):
            ahead = back(f + step) if f + step < ff else None
            d_pre = (d_act * slope_s[:, f : f + step]).astype(LOW)
            pre_s[rows, f : f + step] = d_pre
            small_up[:, f : f + step] += fold_rows(d_pre.astype(F32))
            d_middle = d_middle + mm_nt(d_pre, wu_s[:, f : f + step])
            d_act = ahead
        small[3] += fold_rows(d_middle * unit1)
        small[4] += fold_rows(d_middle)
        d_one = norm_back(unit1, inv1, d_middle * vec(g1))
        d_first[:, i] = d_one.reshape(nw, sr, width)
        d_out = d_one.astype(LOW)
        dout_s[rows, :] = d_out
        small[5] += fold_rows(d_out.astype(F32))
        d_attended = mm_nt(d_out, wo_s[...]).astype(LOW).reshape(nw, sr, width)
        for w in range(nw):
            for g in range(groups):
                at = (g // 2) * LANES if hpd == 1 else g * pw
                dsend[i, w, g] = d_attended[w, :, at : at + pw]

                @pl.when(is_self(w, g))
                def _():
                    grad_own(i, w, g).start()

                @pl.when(jnp.logical_not(is_self(w, g)))
                def _():
                    grad_copy(i, w, g).start()

    loop(0, sub, tokens)
    for copy in stores[5:]:
        copy.start()

    blocks = 2 * ff // step + 1
    spare = plan.piece - 3 * width

    half = width // 2

    def stage_copies(n):
        at = (n % 3) * width
        return [
            pltpu.make_async_copy(
                stage.at[n % 2, :, side * half : (side + 1) * half],
                pieces.at[2 * (n // 3) + side, at : at + width, :],
                stage_sem.at[n % 2, side],
            )
            for side in range(2)
        ]

    def put(n, value):
        if n >= 2:
            for copy in stage_copies(n - 2):
                copy.wait()
        stage[n % 2] = value.astype(LOW)
        for copy in stage_copies(n):
            copy.start()

    for f in range(ff // step):
        put(2 * f, mm_tn(mid_s[...], pre_s[:, f * step : (f + 1) * step]))
        put(2 * f + 1, mm_tn(act_s[:, f * step : (f + 1) * step], branch_s[...]))
    put(blocks - 1, mm_tn(att_s[...], dout_s[...]))
    for n in (blocks - 2, blocks - 1):
        for copy in stage_copies(n):
            copy.wait()
    if spare > 0:
        stage[0] = jnp.zeros_like(stage[0])
        for n in range(pieces.shape[0]):
            for at in range(0, spare, width):
                size = min(width, spare - at)
                pad = pltpu.make_async_copy(
                    stage.at[0, 0:size, 0:half],
                    pieces.at[n, 3 * width + at : 3 * width + at + size, :],
                    stage_sem.at[0, 0],
                )
                pad.start()
                pad.wait()

    def take(n):
        i, s = n // nv, lax.rem(n, nv)

        @pl.when(jnp.logical_not((s == v) & mine))
        def _():
            arrived(d_att.at[i, s], d_recv.at[i, s])

    loop(0, sub * nv, take)

    def finish(i):
        for w in range(nw):
            for g in range(groups):

                @pl.when(is_self(w, g))
                def _():
                    grad_own(i, w, g).wait()

                @pl.when(jnp.logical_not(is_self(w, g)))
                def _():
                    grad_copy(i, w, g).wait_send()

        @pl.when(jnp.logical_not(mine))
        def _():
            att_copy(i, 0).wait_send()

        loop(1, nv, lambda o: att_copy(i, o).wait_send())

        @pl.when(mine)
        def _():
            loop(0, nv, lambda s: forward_copy(i, s).wait_send())

    loop(0, sub, finish)
    loop(0, sub * nv, end_out)
    for copy in stores:
        copy.wait()


class Sums:
    def __init__(self, plan, source, sums, box1, half, box2, box3, box4, fin, pair_sems, many_sems):
        self.plan, self.source, self.sums = plan, source, sums
        self.box1, self.half, self.box2, self.box3 = box1, half, box2, box3
        self.box4, self.fin = box4, fin
        self.s, self.m = pair_sems, many_sems
        b, v = lax.axis_index("batch"), lax.axis_index("var")
        self.b, self.v = b, v
        self.core, self.xs, self.lo, self.hi = lax.rem(b, 2), b // 2, lax.rem(v, 2), v // 2
        self.nh = plan.nv // 2
        self.half_rows = plan.piece // 2
        self.quarter, self.eighth = plan.piece // 4, plan.piece // 8
        self.chunk = self.eighth // self.nh

    def mate(self, p, first):
        over_x = (p % 2 == 0) if first else (p % 2 == 1)
        db, dv = self.b + 2 - 4 * self.xs, self.v + 1 - 2 * self.lo
        return jnp.where(over_x, db, self.b), jnp.where(over_x, self.v, dv)

    def coords(self, p):
        even = p % 2 == 0
        return jnp.where(even, self.xs, self.lo), jnp.where(even, self.lo, self.xs)

    def pair(self, p, at, src, dst, device):
        return remote(src, dst, self.s.at[0, at, p], self.s.at[1, at, p], device)

    def core_copy(self, p):
        rows = rows16((1 - self.core) * self.half_rows, self.half_rows)
        device = (self.b + 1 - 2 * self.core, self.v)
        return self.pair(p, 0, self.source(p).at[rows, :], self.box1.at[p], device)

    def own_copy(self, p):
        rows = rows16(self.core * self.half_rows, self.half_rows)
        return pltpu.make_async_copy(
            self.source(p).at[rows, :], self.half.at[p], self.s.at[0, 6, p]
        )

    def first_copy(self, p):
        c1, _ = self.coords(p)
        rows = rows16((1 - c1) * self.quarter, self.quarter)
        return self.pair(p, 1, self.half.at[p, rows, :], self.box2.at[p], self.mate(p, True))

    def second_copy(self, p):
        c1, c2 = self.coords(p)
        rows = rows16(c1 * self.quarter + (1 - c2) * self.eighth, self.eighth)
        return self.pair(p, 2, self.half.at[p, rows, :], self.box3.at[p], self.mate(p, False))

    def peer(self, o):
        return lax.rem(self.hi + o, self.nh)

    def many_copy(self, p, o):
        d = self.peer(o)
        c1, c2 = self.coords(p)
        rows = rows16(c1 * self.quarter + c2 * self.eighth + d * self.chunk, self.chunk)
        return remote(
            self.half.at[p, rows, :], self.box4.at[p, self.hi],
            self.m.at[0, 0, p, o], self.m.at[1, 0, p, self.hi], (self.b, d * 2 + self.lo),
        )

    def region(self, p, start, size):
        return self.sums.at[p, rows16(self.core * self.half_rows + start, size), :]

    def chunk_at(self, p, who):
        c1, c2 = self.coords(p)
        start = c1 * self.quarter + c2 * self.eighth + who * self.chunk
        return self.region(p, start, self.chunk)

    def spread_copy(self, p, o):
        return remote(
            self.fin.at[p], self.chunk_at(p, self.hi),
            self.m.at[0, 1, p, o], self.m.at[1, 1, p, self.hi],
            (self.b, self.peer(o) * 2 + self.lo),
        )

    def keep_copy(self, p):
        return pltpu.make_async_copy(
            self.fin.at[p], self.chunk_at(p, self.hi), self.s.at[0, 7, p]
        )

    def back_second(self, p):
        c1, c2 = self.coords(p)
        at = self.region(p, c1 * self.quarter + c2 * self.eighth, self.eighth)
        return self.pair(p, 3, at, at, self.mate(p, False))

    def back_first(self, p):
        c1, _ = self.coords(p)
        at = self.region(p, c1 * self.quarter, self.quarter)
        return self.pair(p, 4, at, at, self.mate(p, True))

    def back_core(self, p):
        at = self.region(p, 0, self.half_rows)
        return self.pair(p, 5, at, at, (self.b + 1 - 2 * self.core, self.v))

    def came(self, p, at, ref):
        arrived(ref, self.s.at[1, at, p])

    def step0(self, p):
        self.core_copy(p).start()
        self.own_copy(p).start()

    def step1(self, p):
        self.own_copy(p).wait()
        self.came(p, 0, self.box1.at[p])
        self.half[p] = (self.half[p].astype(F32) + self.box1[p].astype(F32)).astype(LOW)
        self.first_copy(p).start()

    def add(self, p, start, size, other):
        rows = rows16(start, size)
        total = self.half[p, rows, :].astype(F32) + other.astype(F32)
        self.half[p, rows, :] = total.astype(LOW)

    def step2(self, p):
        c1, _ = self.coords(p)
        self.came(p, 1, self.box2.at[p])
        self.first_copy(p).wait_send()
        self.add(p, c1 * self.quarter, self.quarter, self.box2[p])
        self.second_copy(p).start()

    def step3(self, p):
        c1, c2 = self.coords(p)
        self.came(p, 2, self.box3.at[p])
        self.second_copy(p).wait_send()
        self.add(p, c1 * self.quarter + c2 * self.eighth, self.eighth, self.box3[p])
        loop(1, self.nh, lambda o: self.many_copy(p, o).start())

    def step4(self, p):
        def take(o):
            s = self.peer(o)
            arrived(self.box4.at[p, s], self.m.at[1, 0, p, s])

        loop(1, self.nh, take)
        c1, c2 = self.coords(p)
        rows = rows16(c1 * self.quarter + c2 * self.eighth + self.hi * self.chunk, self.chunk)
        total = self.half[p, rows, :].astype(F32)
        for o in range(1, self.nh):
            total = total + self.box4[p, self.peer(o)].astype(F32)
        self.fin[p] = total.astype(LOW)
        self.keep_copy(p).start()
        loop(1, self.nh, lambda o: self.spread_copy(p, o).start())

    def step5(self, p):
        def take(o):
            s = self.peer(o)
            arrived(self.chunk_at(p, s), self.m.at[1, 1, p, s])

        loop(1, self.nh, take)
        self.keep_copy(p).wait()
        self.back_second(p).start()

    def step6(self, p):
        c1, c2 = self.coords(p)
        self.came(p, 3, self.region(p, c1 * self.quarter + (1 - c2) * self.eighth, self.eighth))
        self.back_first(p).start()

    def step7(self, p):
        c1, _ = self.coords(p)
        self.came(p, 4, self.region(p, (1 - c1) * self.quarter, self.quarter))
        self.back_core(p).start()

    def step8(self, p):
        rows = rows16((1 - self.core) * self.half_rows, self.half_rows)
        self.came(p, 5, self.sums.at[p, rows, :])
        self.core_copy(p).wait_send()
        loop(1, self.nh, lambda o: self.many_copy(p, o).wait_send())
        loop(1, self.nh, lambda o: self.spread_copy(p, o).wait_send())
        self.back_second(p).wait_send()
        self.back_first(p).wait_send()
        self.back_core(p).wait_send()

    DUE = (0, 2, 8, 14, 20, 26, 30, 36, 38)
    LAG = 2

    def at(self, tile, count):
        steps = (
            self.step0, self.step1, self.step2, self.step3, self.step4,
            self.step5, self.step6, self.step7, self.step8,
        )
        @pl.when((tile & 1) == 0)
        def _():
            for due, step in reversed(tuple(zip(self.DUE, steps))):
                piece = (tile - due) >> 1

                @pl.when((piece >= 0) & (piece < count))
                def _():
                    step(piece)

    def end(self, count):
        return self.DUE[-1] + self.LAG * (count - 1) + 1


class ShortSums:
    def __init__(self, plan, source, sums, box1, half, box2, fin, pair_sems, many_sems):
        self.plan, self.source, self.sums = plan, source, sums
        self.box1, self.half, self.box2, self.fin = box1, half, box2, fin
        self.s, self.m = pair_sems, many_sems
        b, v = lax.axis_index("batch"), lax.axis_index("var")
        self.b, self.v, self.core = b, v, lax.rem(b, 2)
        self.peers = 2 * plan.nv
        self.me = (b // 2) * plan.nv + v
        self.half_rows = source.shape[1] // 2
        self.chunk = self.half_rows // self.peers

    def peer(self, o):
        return lax.rem(self.me + o, self.peers)

    def device(self, j):
        return (j // self.plan.nv) * 2 + self.core, lax.rem(j, self.plan.nv)

    def core_copy(self, p):
        rows = rows16((1 - self.core) * self.half_rows, self.half_rows)
        return remote(
            self.source.at[p, rows, :], self.box1.at[p], self.s.at[0, 0, p], self.s.at[1, 0, p],
            (self.b + 1 - 2 * self.core, self.v),
        )

    def many_copy(self, p, o):
        j = self.peer(o)
        return remote(
            self.half.at[p, rows16(j * self.chunk, self.chunk), :], self.box2.at[p, self.me],
            self.m.at[0, 0, p, o], self.m.at[1, 0, p, self.me], self.device(j),
        )

    def chunk_at(self, p, j):
        rows = rows16(self.core * self.half_rows + j * self.chunk, self.chunk)
        return self.sums.at[p, rows, :]

    def spread_copy(self, p, o):
        return remote(
            self.fin.at[p], self.chunk_at(p, self.me),
            self.m.at[0, 1, p, o], self.m.at[1, 1, p, self.me], self.device(self.peer(o)),
        )

    def keep_copy(self, p):
        return pltpu.make_async_copy(
            self.fin.at[p], self.chunk_at(p, self.me), self.s.at[0, 2, p]
        )

    def back_core(self, p):
        at = self.sums.at[p, rows16(self.core * self.half_rows, self.half_rows), :]
        return remote(
            at, at, self.s.at[0, 1, p], self.s.at[1, 1, p],
            (self.b + 1 - 2 * self.core, self.v),
        )

    def step0(self, p):
        self.core_copy(p).start()

    def step1(self, p):
        arrived(self.box1.at[p], self.s.at[1, 0, p])
        rows = rows16(self.core * self.half_rows, self.half_rows)
        total = self.source[p, rows, :].astype(F32) + self.box1[p].astype(F32)
        self.half[p] = total.astype(LOW)
        loop(1, self.peers, lambda o: self.many_copy(p, o).start())

    def step2(self, p):
        def take(o):
            j = self.peer(o)
            arrived(self.box2.at[p, j], self.m.at[1, 0, p, j])

        loop(1, self.peers, take)
        total = self.half[p, rows16(self.me * self.chunk, self.chunk), :].astype(F32)
        for o in range(1, self.peers):
            total = total + self.box2[p, self.peer(o)].astype(F32)
        self.fin[p] = total.astype(LOW)
        self.keep_copy(p).start()
        loop(1, self.peers, lambda o: self.spread_copy(p, o).start())

    def step3(self, p):
        def take(o):
            j = self.peer(o)
            arrived(self.chunk_at(p, j), self.m.at[1, 1, p, j])

        loop(1, self.peers, take)
        self.keep_copy(p).wait()
        self.back_core(p).start()

    def step4(self, p):
        rows = rows16((1 - self.core) * self.half_rows, self.half_rows)
        arrived(self.sums.at[p, rows, :], self.s.at[1, 1, p])
        self.core_copy(p).wait_send()
        loop(1, self.peers, lambda o: self.many_copy(p, o).wait_send())
        loop(1, self.peers, lambda o: self.spread_copy(p, o).wait_send())
        self.back_core(p).wait_send()


def backward_kernel(
    plan, count, qa_in, ka_in, va_in, att, d_att, xw, wq, wk, wv, d_first, ga, small, small_up,
    gi, sums, first_sums, last_sums, vectors,
    qa, ka, va,
    da, kt, dqt, dk, dv, dall, wcat, part, mate, own, final, dx, gacc, gb,
    bsum, box1, half, box2, box3, box4, fin, box1b, halfb, box2b, finb,
    ga0, box1c, halfc, box2c, finc,
    bias_mine, vec1, vec2, xs, firsts,
    p_send, p_recv, send, recv, local_sem, sa, ma, sb, mb, sc, mc, vs, vs2, load,
):
    nv, nw, hpd, hd = plan.nv, plan.nw, plan.hpd, plan.hd
    sub, sr, st, pairs = plan.sub, plan.sr, plan.st, plan.pairs
    slots, groups, pw, width = plan.slots, plan.groups, plan.pw, plan.width
    b, v, core, parity, slot, group = plan.here()
    mine = parity == core
    owner = b - core + parity
    base = plan.base(group)
    odds = [plan.odd(h, group) for h in range(hpd)]
    core_mate = (b + 1 - 2 * core, v)
    x_copy = pltpu.make_async_copy(xw, xs, load.at[0])
    first_copy = pltpu.make_async_copy(d_first, firsts, load.at[1])
    pair_copies = [
        [
            pltpu.make_async_copy(
                src.at[2 * pair : min(2 * pair + 2, hpd)],
                dst.at[2 * pair : min(2 * pair + 2, hpd)],
                load.at[2 + 3 * pair + n],
            )
            for n, (src, dst) in enumerate(((qa_in, qa), (ka_in, ka), (va_in, va)))
        ]
        for pair in range(pairs)
    ]
    for copies in pair_copies:
        for copy in copies:
            copy.start()
    x_copy.start()
    first_copy.start()
    enter(plan, b, v, core, across=True)
    tokens = Sums(
        plan, lambda p: ga.at[p], sums, box1, half, box2, box3, box4, fin, sa, ma
    )
    last = pairs - 1
    tail = ShortSums(plan, gb, last_sums, box1b, halfb, box2b, finb, sb, mb)
    opening = (
        ShortSums(plan, ga0, first_sums, box1c, halfc, box2c, finc, sc, mc) if last > 0 else tail
    )

    tile = lane_of((st, LANES))

    def prepare(i, pair):
        rows = rows16(i * st, st)
        for h in range(2 * pair, min(2 * pair + 2, hpd)):
            at = (h // 2) * LANES
            data = in_half(tile, odds[h], hd)
            column = extra_lane(tile, odds[h], hd)
            grad = d_att[i, :, :, at : at + LANES].reshape(st, LANES).astype(F32)
            prod = grad * att[i, :, :, at : at + LANES].reshape(st, LANES).astype(F32)
            delta = jnp.sum(jnp.where(data, prod, 0.0), axis=1, keepdims=True)
            high, mid, tail = (term.astype(F32) for term in three_parts(-delta))
            extra = jnp.where(column == 0, high, jnp.where(column == 1, mid, tail))
            da[h, rows, :] = jnp.where(
                data, grad, jnp.where((column >= 0) & (column < 3), extra, 0.0)
            ).astype(LOW)

    def open_pair(pair):
        for copy in pair_copies[pair]:
            copy.wait()
        for h in range(2 * pair, min(2 * pair + 2, hpd)):
            turned = jnp.transpose(ka[h])
            if hpd == 1:
                kt[h] = jnp.where(odds[h] == 1, turned[hd:], turned[:hd])
            else:
                kt[h] = turned[odds[h] * hd : (odds[h] + 1) * hd]
        loop(0, sub, lambda i: prepare(i, pair))

    tokens.step0(0)
    for kind, ref in enumerate((wq, wk, wv)):
        wcat[:, kind * pw : (kind + 1) * pw] = ref[:, pl.ds(base, pw)]
    dk[...] = jnp.zeros_like(dk)
    dv[...] = jnp.zeros_like(dv)
    dqt[...] = jnp.zeros_like(dqt)
    gacc[...] = jnp.zeros_like(gacc)

    def attend(pair, qi, ki):
        rows, keys = pl.ds(pl.multiple_of(qi * st, st), st), pl.ds(pl.multiple_of(ki * st, st), st)
        key_parts, value_parts = [], []
        for h in range(2 * pair, min(2 * pair + 2, hpd)):
            q = qa[h, rows, :]
            d = da[h, rows, :]
            prob = jnp.exp(mm_nt(ka[h, keys, :], q))
            d_score = (prob * mm_nt(va[h, keys, :], d)).astype(LOW)
            value_parts.append(mm(prob.astype(LOW), d))
            key_parts.append(mm(d_score, q))
            dqt[pl.ds(pair * LANES + odds[h] * hd, hd), rows] += mm(kt[h, :, keys], d_score)
        if hpd == 1:
            key_parts.append(jnp.zeros_like(key_parts[0]))
            value_parts.append(jnp.zeros_like(value_parts[0]))
        first = in_half(tile, odds[2 * pair], hd)
        dv[pair, keys, :] += jnp.where(first, value_parts[0], value_parts[1])
        dk[pair, keys, :] += jnp.where(first, key_parts[0], key_parts[1])

    def gather_pair(pair, i):
        rows = rows16(i * st, st)
        at = pair * LANES
        dqt_block = dqt[at : at + LANES, pl.ds(pl.multiple_of(i * st, st), st)]
        dq = jnp.transpose(dqt_block)
        terms = (dq * (hd**-0.5), dk[pair, rows, :], dv[pair, rows, :])
        for kind, term in enumerate(terms):
            dall[rows, kind * pw + at : kind * pw + at + LANES] = term.astype(LOW)
        block = xs[rows, :]
        turned = (dqt_block * (hd**-0.5), jnp.transpose(terms[1]), jnp.transpose(terms[2]))
        for kind, term in enumerate(turned):
            gacc[kind * LANES : (kind + 1) * LANES, :] += mm(term.astype(LOW), block)
        for kind, row in ((0, 0), (2, 1)):
            bsum[row * 8 : row * 8 + 8, :] += fold_rows(terms[kind].astype(LOW).astype(F32))

    lanes = gb.shape[-1]

    def put_pair(pair, ref):
        if plan.piece > 3 * width or lanes > LANES:
            ref[...] = jnp.zeros_like(ref)
        at = base if hpd == 1 else pl.multiple_of(group * LANES, LANES)
        for kind in range(3):
            ref[0, kind * width : (kind + 1) * width, pl.ds(at, LANES)] = jnp.transpose(
                gacc[kind * LANES : (kind + 1) * LANES, :]
            ).astype(LOW)

    def put_vectors(ref, low):
        ups = small_up.shape[1] // width
        rows = [jnp.sum(small[at], axis=0, keepdims=True) for at in range(6)]
        rows += [
            jnp.sum(small_up[:, at * width : (at + 1) * width], axis=0, keepdims=True)
            for at in range(ups)
        ]
        rows += [jnp.zeros((16 - len(rows), width), F32)]
        block = jnp.concatenate(rows, axis=0).astype(LOW)
        for part in range(width // lanes):
            ref[0, low + 16 * part : low + 16 * part + 16, :] = block[
                :, part * lanes : (part + 1) * lanes
            ]

    x_copy.wait()

    bsum[...] = jnp.zeros_like(bsum)

    def put_bias(pair):
        at = base if hpd == 1 else pl.multiple_of(group * LANES, LANES)
        for row in range(2):
            bias_mine[2 * pair + row : 2 * pair + row + 1, pl.ds(at, LANES)] = jnp.sum(
                bsum[row * 8 : row * 8 + 8, :], axis=0, keepdims=True
            )
        bsum[...] = jnp.zeros_like(bsum)

    bias_mine[...] = jnp.zeros_like(bias_mine)
    for pair in range(pairs - 1):
        open_pair(pair)

        def square(t):
            tokens.at(pair * sub * sub + t + 1, count)
            attend(pair, t // sub, lax.rem(t, sub))

        loop(0, sub * sub, square)
        loop(0, sub, lambda i: gather_pair(pair, i))
        put_bias(pair)
        if pair == 0:
            put_pair(pair, ga0)
            put_vectors(ga0, 3 * width)
            opening.step0(0)
        gacc[...] = jnp.zeros_like(gacc)

    open_pair(last)
    before = last * sub * sub
    share = nv // groups
    mine_rows = share * sr

    def device_of(g):
        return b - core + g % 2, v - lax.rem(v, plan.cpw) + g // 2

    def part_copy(i, g):
        return remote(
            part.at[i, g * mine_rows : (g + 1) * mine_rows, :], mate.at[i, group],
            p_send.at[i, g], p_recv.at[i, group], device_of(g),
        )

    def send_parts(i):
        rows = rows16(i * st, st)
        total = mm_nt(dall[rows, :], wcat[...])
        part[i] = total.astype(LOW)
        own[i % 2] = total
        for g in range(groups):

            @pl.when(g != group)
            def _():
                part_copy(i, g).start()

    def final_copy(i, n):
        d = group * share + n
        return remote(
            final.at[i, n], dx.at[slot, i], send.at[i, n], recv.at[slot, i], (owner, d)
        )

    def is_own(n):
        return mine & (group * share + n == v)

    def own_copy(i, n):
        return pltpu.make_async_copy(final.at[i, n], dx.at[slot, i], local_sem.at[i])

    def send_final(i):
        total = own[i % 2, rows16(group * mine_rows, mine_rows), :]
        for g in range(groups):

            @pl.when(g != group)
            def _():
                arrived(mate.at[i, g], p_recv.at[i, g])

            @pl.when(g == group)
            def _():
                mate[i, g] = jnp.zeros((mine_rows, width), LOW)

        for g in range(groups):
            total = total + mate[i, g].astype(F32)
        final[i] = total.astype(LOW).reshape(share, sr, width)
        for n in range(share):

            @pl.when(is_own(n))
            def _():
                own_copy(i, n).start()

            @pl.when(jnp.logical_not(is_own(n)))
            def _():
                final_copy(i, n).start()

    def shrink(i):
        start = i * (2 * sub - i)

        def angle(t):
            done = start + t
            tokens.at(before + done + 1, count)
            if last > 0:
                for due, step in ((1, opening.step1), (13, opening.step2), (24, opening.step3)):

                    @pl.when(done == due)
                    def _():
                        step(0)

            n = sub - i
            attend(
                last, jnp.where(t < n, i, i + 1 + t - n), jnp.where(t < n, i + t, i)
            )

        loop(0, 2 * (sub - i) - 1, angle)
        gather_pair(last, i)

        @pl.when(i == sub - 1)
        def _():
            put_pair(last, gb)
            if last == 0:
                put_vectors(gb, 3 * width)
            tail.step0(0)

        send_parts(i)

        @pl.when(i > 0)
        def _():
            send_final(i - 1)

    loop(0, sub, shrink)
    tiles = before + sub * sub
    loop(tiles + 1, max(tiles + 1, tokens.end(count)), lambda t: tokens.at(t, count))

    put_bias(last)
    core_vec = remote(bias_mine, vec1, vs.at[0], vs.at[1], core_mate)
    core_vec.start()
    send_final(sub - 1)
    tail.step1(0)
    arrived(vec1, vs.at[1])
    core_vec.wait_send()
    bias_mine[...] = bias_mine[...] + vec1[...]

    def vec_spread(o):
        return remote(
            bias_mine, vec2.at[tail.me], vs2.at[0, o], vs2.at[1, tail.me],
            tail.device(tail.peer(o)),
        )

    loop(1, 2 * nv, lambda o: vec_spread(o).start())
    vec2[tail.me] = bias_mine[...]
    first_copy.wait()

    def finish(i):
        for n in range(share):

            @pl.when(is_own(n))
            def _():
                own_copy(i, n).wait()

        for w in range(nw):
            self_sent = mine & (slot == w) & (v // share == group)

            @pl.when(jnp.logical_not(self_sent))
            def _():
                arrived(dx.at[w, i], recv.at[w, i])

        gi[:, i] = (firsts[:, i] + dx[:, i].astype(F32)).astype(LOW)

    loop(0, sub - 1, finish)
    if last > 0:
        opening.step4(0)
    tail.step2(0)

    def vec_take(o):
        j = tail.peer(o)
        arrived(vec2.at[j], vs2.at[1, j])

    loop(1, 2 * nv, vec_take)
    total = vec2[0]
    for j in range(1, 2 * nv):
        total = total + vec2[j]
    vectors[...] = total
    loop(sub - 1, sub, finish)
    tail.step3(0)

    def close(i):
        for n in range(share):

            @pl.when(jnp.logical_not(is_own(n)))
            def _():
                final_copy(i, n).wait_send()

        for g in range(groups):

            @pl.when(g != group)
            def _():
                part_copy(i, g).wait_send()

    loop(0, sub, close)
    loop(1, 2 * nv, lambda o: vec_spread(o).wait_send())
    tail.step4(0)


def output_kernel(
    plan, ff, sums, first_sums, last_sums, vectors,
    gq, gk, gv, go, gu, gd, bq, bv, bo, g1, s1, bu, bd, g2, s2,
    block_in, first_in, last_in, block_out, wide_out, load, store,
):
    width = plan.width
    blocks = ff // width
    lanes = last_in.shape[-1]
    total = 2 * blocks + 1

    def block_loads(n):
        at = (n % 3) * width
        return [
            pltpu.make_async_copy(
                sums.at[2 * (n // 3) + side, at : at + width, :],
                block_in.at[n, :, side * (width // 2) : (side + 1) * (width // 2)],
                load.at[2 * n + side],
            )
            for side in range(2)
        ]

    def block_store(n):
        if n == 2 * blocks:
            dst = go
        elif n % 2:
            dst = gd.at[n // 2 * width : (n // 2 + 1) * width, :]
        else:
            dst = gu.at[:, n // 2 * width : (n // 2 + 1) * width]
        return pltpu.make_async_copy(block_out.at[n], dst, store.at[n])

    parts = [(first_sums, first_in), (last_sums, last_in)][2 - min(plan.pairs, 2) :]
    part_loads = [
        pltpu.make_async_copy(src, dst, load.at[2 * total + n]) for n, (src, dst) in enumerate(parts)
    ]
    wide_stores = [
        pltpu.make_async_copy(wide_out.at[n], dst, store.at[total + n])
        for n, dst in enumerate((gq, gk, gv))
    ]
    for n in range(total):
        for copy in block_loads(n):
            copy.start()
    for copy in part_loads:
        copy.start()
    for n in range(total):
        for copy in block_loads(n):
            copy.wait()
        block_out[n] = block_in[n].astype(F32)
        block_store(n).start()
    for copy in part_loads:
        copy.wait()
    groups = lanes // LANES
    for kind in range(3):
        for pair, (_, ref) in enumerate(parts):
            for group in range(groups):
                at = (group * plan.pairs + pair) * LANES
                wide_out[kind, :, at : at + LANES] = ref[
                    0, kind * width : (kind + 1) * width, group * LANES : (group + 1) * LANES
                ].astype(F32)
        wide_stores[kind].start()
    low = 3 * width
    ref = parts[0][1]
    rows = jnp.concatenate(
        [ref[0, low + 16 * n : low + 16 * n + 16, :] for n in range(width // lanes)], axis=1
    ).astype(F32)
    for n, ref in enumerate((g2, s2, bd, g1, s1, bo)):
        ref[...] = rows[n]
    for f in range(blocks):
        bu[f * width : (f + 1) * width] = rows[6 + f]
    for row, ref in enumerate((bq, bv)):
        for pair in range(plan.pairs):
            for group in range(groups):
                at = (group * plan.pairs + pair) * LANES
                ref[at : at + LANES] = vectors[2 * pair + row, group * LANES : (group + 1) * LANES]
    for n in range(total):
        block_store(n).wait()
    for copy in wide_stores:
        copy.wait()


def params(number):
    return pltpu.CompilerParams(
        vmem_limit_bytes=VMEM_BYTES, collective_id=number, has_side_effects=True
    )


def sum_scratch(plan, number, lanes):
    piece = plan.piece
    nh = plan.nv // 2
    return [
        pltpu.VMEM((number, piece // 2, lanes), LOW),
        pltpu.VMEM((number, piece // 2, lanes), LOW),
        pltpu.VMEM((number, piece // 4, lanes), LOW),
        pltpu.VMEM((number, piece // 8, lanes), LOW),
        pltpu.VMEM((number, nh, piece // 8 // nh, lanes), LOW),
        pltpu.VMEM((number, piece // 8 // nh, lanes), LOW),
    ]


def short_scratch(plan, rows, lanes):
    peers = 2 * plan.nv
    return [
        pltpu.VMEM((1, rows // 2, lanes), LOW),
        pltpu.VMEM((1, rows // 2, lanes), LOW),
        pltpu.VMEM((1, peers, rows // 2 // peers, lanes), LOW),
        pltpu.VMEM((1, rows // 2 // peers, lanes), LOW),
    ]


def sum_sems(number, steps, peers):
    return [DMA((2, steps, number)), DMA((2, 2, number, peers))]


def body(
    plan,
    inputs, w_query, w_key, w_value, w_out, b_query, b_value, b_out, gain_one, shift_one,
    w_up, b_up, w_down, b_down, gain_two, shift_two, cotangent, valid_mask,
):
    nv, nw, width = plan.nv, plan.nw, plan.width
    slots, hpd, hd, pw, groups = plan.slots, plan.hpd, plan.hd, plan.pw, plan.groups
    sub, sr, st, pairs = plan.sub, plan.sr, plan.st, plan.pairs
    ff = w_up.shape[1]
    rows, cr = plan.rows, nw * sr
    piece = plan.piece
    shape = jax.ShapeDtypeStruct
    ANY = pl.BlockSpec(memory_space=pl.ANY)
    count = (2 * ff // width + 1) // 3 * 2

    heads = shape((hpd, slots, LANES), LOW)
    blocked = (nw, sub, sr, width)
    mask = valid_mask.reshape(nv, sub, sr).transpose(1, 0, 2).reshape(slots // LANES, LANES)
    qa, ka, va, xw, att, out, d_first, d_att, ga, small, small_up = pl.pallas_call(
        functools.partial(forward_kernel, plan, ff),
        out_shape=(
            heads,
            heads,
            heads,
            shape((sub, nv, sr, width), LOW),
            shape((sub, nv, sr, pw), LOW),
            shape(blocked, LOW),
            shape(blocked, F32),
            shape((sub, nv, sr, pw), LOW),
            shape((count, piece, width // 2), LOW),
            shape((6, 8, width), F32),
            shape((8, ff), F32),
        ),
        in_specs=[VM] * 7 + [ANY, ANY] + [VM] * 3 + [ANY, VM, ANY] + [VM] * 3,
        out_specs=(ANY,) * 7 + (VM, ANY, VM, VM),
        scratch_shapes=[
            pltpu.VMEM((hpd, slots, LANES), LOW),
            pltpu.VMEM((hpd, slots, LANES), LOW),
            pltpu.VMEM((hpd, slots, LANES), LOW),
            pltpu.VMEM((sub, nv, sr, width), LOW),
            pltpu.VMEM((sub, nv, sr, pw), LOW),
            pltpu.VMEM(blocked, LOW),
            pltpu.VMEM(blocked, F32),
            pltpu.VMEM(blocked, LOW),
            pltpu.VMEM((width, width), LOW),
            pltpu.VMEM((width, ff), LOW),
            pltpu.VMEM((ff, width), LOW),
            pltpu.VMEM((width, 3 * hpd * LANES), LOW),
            pltpu.VMEM((slots, LANES), LOW),
            pltpu.VMEM((8, width), F32),
            pltpu.VMEM((hpd, (sub + 1) // 2 * st, LANES), F32),
            pltpu.VMEM((nw, groups, sub, sr, pw), LOW),
            pltpu.VMEM((rows, width), LOW),
            pltpu.VMEM((rows, width), LOW),
            pltpu.VMEM((rows, ff), LOW),
            pltpu.VMEM((cr, ff), F32),
            pltpu.VMEM((rows, ff), LOW),
            pltpu.VMEM((rows, width), LOW),
            pltpu.VMEM((rows, width), LOW),
            pltpu.VMEM((sub, nw, groups, sr, pw), LOW),
            pltpu.VMEM((2, width, width), LOW),
            DMA((sub, nv)),
            DMA((sub, nv)),
            DMA((sub, nv)),
            DMA((sub, nv)),
            DMA((nw, groups, sub)),
            DMA((sub,)),
            DMA((sub, nw, groups)),
            DMA((sub, nv)),
            DMA((sub,)),
            DMA,
            DMA((2, 2)),
            DMA((4,)),
            DMA((7,)),
        ],
        compiler_params=params(1),
        name="forward_and_tokens",
    )(
        inputs.reshape(blocked), w_query, w_key, w_value, b_query, b_value, mask,
        cotangent.reshape(blocked), w_out, b_out, gain_one, shift_one,
        w_up, b_up, w_down, b_down, gain_two, shift_two,
    )

    share = nv // groups
    lanes = width // pairs
    unit = 16 * 4 * nv
    more = -(-(3 * width + 16 * width // lanes) // unit) * unit
    first_rows = more if pairs > 1 else unit
    last_rows = piece if pairs > 1 else more
    gi, sums, first_sums, last_sums, vectors = pl.pallas_call(
        functools.partial(backward_kernel, plan, count),
        out_shape=(
            shape(blocked, LOW),
            shape((count, piece, width // 2), LOW),
            shape((1, first_rows, lanes), LOW),
            shape((1, last_rows, lanes), LOW),
            shape((8, lanes), F32),
        ),
        in_specs=[ANY] * 3 + [VM] * 2 + [ANY] + [VM] * 3 + [ANY, ANY, VM, VM],
        out_specs=(VM, ANY, ANY, ANY, VM),
        scratch_shapes=[
            pltpu.VMEM((hpd, slots, LANES), LOW),
            pltpu.VMEM((hpd, slots, LANES), LOW),
            pltpu.VMEM((hpd, slots, LANES), LOW),
            pltpu.VMEM((hpd, slots, LANES), LOW),
            pltpu.VMEM((hpd, hd, slots), LOW),
            pltpu.VMEM((pw, slots), F32),
            pltpu.VMEM((pairs, slots, LANES), F32),
            pltpu.VMEM((pairs, slots, LANES), F32),
            pltpu.VMEM((slots, 3 * pw), LOW),
            pltpu.VMEM((width, 3 * pw), LOW),
            pltpu.VMEM((sub, st, width), LOW),
            pltpu.VMEM((sub, groups, share * sr, width), LOW),
            pltpu.VMEM((2, st, width), F32),
            pltpu.VMEM((sub, share, sr, width), LOW),
            pltpu.VMEM((nw, sub, sr, width), LOW),
            pltpu.VMEM((3 * LANES, width), F32),
            pltpu.VMEM((1, last_rows, lanes), LOW),
            pltpu.VMEM((16, LANES), F32),
        ]
        + sum_scratch(plan, count, width // 2)
        + short_scratch(plan, last_rows, lanes)
        + [pltpu.VMEM((1, first_rows, lanes), LOW)]
        + short_scratch(plan, first_rows, lanes)
        + [
            pltpu.VMEM((8, lanes), F32),
            pltpu.VMEM((8, lanes), F32),
            pltpu.VMEM((2 * nv, 8, lanes), F32),
            pltpu.VMEM((slots, width), LOW),
            pltpu.VMEM(blocked, F32),
            DMA((sub, groups)),
            DMA((sub, groups)),
            DMA((sub, share)),
            DMA((nw, sub)),
            DMA((sub,)),
        ]
        + sum_sems(count, 8, nv // 2)
        + sum_sems(1, 3, 2 * nv)
        + sum_sems(1, 3, 2 * nv)
        + [DMA((2,)), DMA((2, 2 * nv)), DMA((2 + 3 * pairs,))],
        compiler_params=params(2),
        name="attention_backward",
    )(
        qa, ka, va, att, d_att, xw.reshape(slots, width), w_query, w_key, w_value, d_first,
        ga, small, small_up,
    )

    square = shape((width, width), F32)
    one = shape((width,), F32)
    total = 2 * ff // width + 1
    gq, gk, gv, go, gu, gd, bq, bv, bo, g1, s1, bu, bd, g2, s2 = pl.pallas_call(
        functools.partial(output_kernel, plan, ff),
        out_shape=(square,) * 4
        + (shape((width, ff), F32), shape((ff, width), F32))
        + (one,) * 5
        + (shape((ff,), F32),)
        + (one,) * 3,
        in_specs=[ANY] * 3 + [VM],
        out_specs=(ANY,) * 6 + (VM,) * 9,
        scratch_shapes=[
            pltpu.VMEM((total, width, width), LOW),
            pltpu.VMEM((1, first_rows, lanes), LOW),
            pltpu.VMEM((1, last_rows, lanes), LOW),
            pltpu.VMEM((total, width, width), F32),
            pltpu.VMEM((3, width, width), F32),
            DMA((2 * total + 2,)),
            DMA((total + 3,)),
        ],
        compiler_params=pltpu.CompilerParams(vmem_limit_bytes=VMEM_BYTES),
        name="outputs",
    )(sums, first_sums, last_sums, vectors)
    return (
        out.reshape(inputs.shape), gi.reshape(inputs.shape),
        gq, gk, gv, go, bq, bv, bo, g1, s1, gu, bu, gd, bd, g2, s2,
    )


def solution(mesh):
    data = P("batch", "var", None)

    def run(*args):
        plan = Plan(mesh, args[0].shape)
        return jax.shard_map(
            functools.partial(body, plan),
            mesh=mesh,
            in_specs=(data,) + (P(),) * 15 + (data, P()),
            out_specs=(data, data) + (P(),) * 15,
            check_vma=False,
        )(*args)

    return run
```

```python
import functools

import jax
import jax.numpy as jnp
from jax import lax
from jax.experimental import pallas as pl
from jax.experimental.pallas import tpu as pltpu
from jax.sharding import PartitionSpec as P

HEADS = 8
LANES = 128
LOW = jnp.bfloat16
F32 = jnp.float32
MESH = pl.DeviceIdType.MESH
DMA = pltpu.SemaphoreType.DMA
VM = pl.BlockSpec(memory_space=pltpu.VMEM)
VMEM_BYTES = 62 << 20


def mm(left, right):
    return jnp.dot(left, right, preferred_element_type=F32)


def mm_nt(left, right):
    return lax.dot_general(left, right, (((1,), (1,)), ((), ())), preferred_element_type=F32)


def mm_tn(left, right):
    return lax.dot_general(left, right, (((0,), (0,)), ((), ())), preferred_element_type=F32)


def lane_of(shape):
    return lax.broadcasted_iota(jnp.int32, shape, len(shape) - 1)


def in_half(lane, odd, hd):
    return (lane >= hd) == (odd == 1)


def extra_lane(lane, odd, hd):
    return jnp.where(in_half(lane, odd, hd), -1, lane - hd * (1 - odd))


def vec(ref):
    return ref[...].reshape(1, -1).astype(F32)


def three_parts(value):
    high = value.astype(LOW)
    rest = value - high.astype(F32)
    mid = rest.astype(LOW)
    tail = (rest - mid.astype(F32)).astype(LOW)
    return high, mid, tail


class Plan:
    def __init__(self, mesh, inputs_shape):
        windows, slots, width = inputs_shape
        self.nv = mesh.shape["var"]
        self.nb = mesh.shape["batch"]
        self.nw = windows // self.nb
        self.local = slots // self.nv
        self.slots = slots
        self.width = width
        self.hd = width // HEADS
        self.cpw = self.nv // (2 * self.nw)
        self.groups = 2 * self.cpw
        self.hpd = HEADS // self.groups
        self.pairs = max(self.hpd // 2, 1)
        self.pw = self.pairs * LANES
        self.rows = self.nw * self.local
        self.sub = next(
            n for n in (5, 4, 2, 1)
            if self.local % (16 * n) == 0 and slots % (LANES * n) == 0
        )
        self.sr = self.local // self.sub
        self.st = self.nv * self.sr
        unit = 16 * self.nv * self.nb
        self.piece = -(-3 * width // unit) * unit

    def here(self):
        b = lax.axis_index("batch")
        v = lax.axis_index("var")
        core = lax.rem(b, 2)
        window = v // self.cpw
        parity = window // self.nw
        slot = lax.rem(window, self.nw)
        group = lax.rem(v, self.cpw) * 2 + core
        return b, v, core, parity, slot, group

    def odd(self, h, group):
        return lax.rem(group, 2) if self.hpd == 1 else h % 2

    def base(self, group):
        if self.hpd == 1:
            return pl.multiple_of((group // 2) * LANES, LANES)
        return pl.multiple_of(group * self.pw, LANES)


def loop(low, high, step):
    def run(index, carry):
        step(index)
        return carry

    lax.fori_loop(low, high, run, 0)


def greet(plan, b, v, core, across=False):
    barrier = pltpu.get_barrier_semaphore()
    partner = b + 1 - 2 * core

    def greet_same(o):
        pl.semaphore_signal(
            barrier, inc=1, device_id=(b, lax.rem(v + o, plan.nv)), device_id_type=MESH
        )

    def greet_other(o):
        pl.semaphore_signal(
            barrier, inc=1, device_id=(partner, lax.rem(v + o, plan.nv)), device_id_type=MESH
        )

    loop(1, plan.nv, greet_same)
    loop(0, plan.nv, greet_other)
    def greet_across(o):
        pl.semaphore_signal(
            barrier, inc=1, device_id=(b + 2 - 4 * (b // 2), lax.rem(v + o, plan.nv)),
            device_id_type=MESH,
        )

    if across:
        loop(0, plan.nv, greet_across)


def all_here(plan, across=False):
    count = (3 if across else 2) * plan.nv - 1
    pl.semaphore_wait(pltpu.get_barrier_semaphore(), count)


def arrived(ref, sem):
    pltpu.make_async_copy(ref, ref, sem).wait()


def gelu_and_slope(pre):
    size = jnp.abs(pre)
    bell = jnp.exp(pre * pre * -0.5)
    t = 1.0 / (1.0 + 0.2316418882663604 * size)
    poly = t * (
        0.127414796
        + t * (-0.142248368 + t * (0.7107068705 + t * (-0.7265760135 + t * 0.5307027145)))
    )
    below = poly * bell
    phi = jnp.where(pre < 0, below, 1.0 - below)
    return pre * phi, phi + pre * bell * 0.3989422804014327


def fold_rows(value):
    rows, width = value.shape
    return jnp.sum(value.reshape(rows // 8, 8, width), axis=0)


def sum_rows(value):
    return jnp.sum(fold_rows(value), axis=0, keepdims=True)


def norm_parts(rows):
    center = rows - jnp.mean(rows, axis=-1, keepdims=True)
    spread = jnp.mean(center * center, axis=-1, keepdims=True)
    inverse = lax.rsqrt(spread + 1e-05)
    return center * inverse, inverse


def norm_back(unit, inverse, grad):
    return inverse * (
        grad
        - jnp.mean(grad, axis=-1, keepdims=True)
        - unit * jnp.mean(grad * unit, axis=-1, keepdims=True)
    )


def remote(src, dst, send_sem, recv_sem, device):
    return pltpu.make_async_remote_copy(
        src_ref=src, dst_ref=dst, send_sem=send_sem, recv_sem=recv_sem,
        device_id=device, device_id_type=MESH,
    )


def rows16(start, size):
    return pl.ds(pl.multiple_of(start, 16), size)


TOP = 8


def forward_kernel(
    plan, ff, x, wq, wk, wv, bq, bv, mask, cot, wo, bo, g1, s1, wu, bu, wd, bd, g2, s2,
    qa_out, ka_out, va_out, xw_out, att_out, out_out, first_out, d_att, pieces, small,
    qa, ka, va, xw, att, d_first, cot_s, wo_s, wu_s, wd_s,
    waug, kaug, bias, acc, got, att_s, mid_s, act_s, pre_s, branch_s, dout_s,
    send, recv, pass_on, a_send, a_recv, a_local, d_send, d_recv, d_local, local_sem, stage_sem,
    load, store,
):
    nv, nw, hpd, hd, pw = plan.nv, plan.nw, plan.hpd, plan.hd, plan.pw
    sub, sr, st, width, groups = plan.sub, plan.sr, plan.st, plan.width, plan.groups
    b, v, core, parity, slot, group = plan.here()
    mine = parity == core
    partner = b + 1 - 2 * core
    owner = b - core + parity
    odds = [plan.odd(h, group) for h in range(hpd)]
    loads = [
        pltpu.make_async_copy(src, dst, load.at[n])
        for n, (src, dst) in enumerate(((wo, wo_s), (wu, wu_s), (wd, wd_s), (cot, cot_s)))
    ]
    stores = [
        pltpu.make_async_copy(src, dst, store.at[n])
        for n, (src, dst) in enumerate((
            (xw, xw_out), (ka, ka_out), (va, va_out), (qa, qa_out), (att, att_out),
            (d_first, first_out), (cot_s, out_out),
        ))
    ]
    greet(plan, b, v, core)

    def out_copy(i, o):
        d = lax.rem(v + o, nv)
        return remote(
            x.at[lax.rem(d // plan.cpw, nw), i], xw.at[i, v], send.at[i, o], recv.at[i, v], (b, d)
        )

    def wanted(o):
        return (lax.rem(v + o, nv) // plan.cpw) // nw == core

    def start_out(n):
        @pl.when(wanted(lax.rem(n, nv)) & (lax.rem(n, nv) > 0))
        def _():
            out_copy(n // nv, lax.rem(n, nv)).start()

    def end_out(n):
        @pl.when(wanted(lax.rem(n, nv)) & (lax.rem(n, nv) > 0))
        def _():
            out_copy(n // nv, lax.rem(n, nv)).wait_send()

    def own_x():
        return pltpu.make_async_copy(x.at[slot], xw.at[:, v], local_sem)

    def forward_copy(i, s):
        at = xw.at[i, s]
        return remote(at, at, pass_on.at[i, s], recv.at[i, s], (partner, v))

    lane = lane_of((width, LANES))
    base = plan.base(group)
    for kind, ref in enumerate((wq, wk, wv)):
        for h in range(hpd):
            both = ref[:, pl.ds(base + (h // 2) * LANES, LANES)].astype(F32)
            at = (kind * hpd + h) * LANES
            waug[:, at : at + LANES] = jnp.where(in_half(lane, odds[h], hd), both, 0.0).astype(LOW)
    bias[0:1, :] = vec(bq)
    bias[1:2, :] = vec(bv)

    all_here(plan)
    loop(0, min(2, sub) * nv, start_out)
    for copy in loads:
        copy.start()

    @pl.when(mine)
    def _():
        own_x().start()

    square = lane_of((LANES, LANES))
    diag = square == lax.broadcasted_iota(jnp.int32, (LANES, LANES), 0)
    place = lax.rem(square, hd)
    ones = jnp.where((place > 0) & (place < 4), 1.0, 0.0)
    for at in range(plan.slots // LANES):
        row = jnp.where(mask[at : at + 1, :] > 0, 0.0, -1e30)
        column = jnp.sum(jnp.where(diag, row, 0.0), axis=1, keepdims=True)
        kaug[at * LANES : (at + 1) * LANES, :] = jnp.where(place == 0, column, ones).astype(LOW)

    tile = lane_of((st, LANES))
    data = [in_half(tile, odd, hd) for odd in odds]
    column = [extra_lane(tile, odd, hd) for odd in odds]

    def extra_column(value, h, at):
        if hpd == 1:
            return jnp.where(
                odds[h] == 1, value[:, at : at + 1], value[:, hd + at : hd + at + 1]
            )
        at += hd * (1 - odds[h])
        return value[:, at : at + 1]

    small[...] = jnp.zeros_like(small)

    def bias_of(kind, h):
        return bias[kind : kind + 1, pl.ds(base + (h // 2) * LANES, LANES)]

    def project(i):
        rows = rows16(i * st, st)
        extra = kaug[rows, :].astype(F32)
        both = mm(xw[i].reshape(st, width), waug[:, 0 : 3 * hpd * LANES])
        for h in range(hpd):
            q = both[:, h * LANES : (h + 1) * LANES] + bias_of(0, h)
            q = q.astype(LOW).astype(F32) * (hd**-0.5)
            qa[h, rows, :] = jnp.where(data[h], q, jnp.where(column[h] == 0, 1.0, 0.0)).astype(LOW)
            k = both[:, (hpd + h) * LANES : (hpd + h + 1) * LANES]
            ka[h, rows, :] = jnp.where(data[h], k, extra).astype(LOW)
            val = both[:, (2 * hpd + h) * LANES : (2 * hpd + h + 1) * LANES] + bias_of(1, h)
            va[h, rows, :] = jnp.where(
                data[h], val, jnp.where((column[h] >= 0) & (column[h] < 3), 1.0, 0.0)
            ).astype(LOW)

    hr = st // 2
    half_data = [value[:hr] for value in data]
    half_column = [value[:hr] for value in column]

    def attend(i, side, low, high, merge):
        rows = rows16(i * st + side * hr, hr)
        keys = slice(low * st, high * st)
        score = mm_nt(qa[0, rows, :], ka[0, keys, :])
        states = []
        for h in range(hpd):
            if h + 1 < hpd:
                ahead = mm_nt(qa[h + 1, rows, :], ka[h + 1, keys, :])
            top = jnp.max(score, axis=1, keepdims=True)
            if merge:
                state = acc[h, rows, :]
                old = extra_column(state, h, TOP)
                top = jnp.maximum(old, top)
            expo = jnp.exp(score - top)
            mixed = mm(expo.astype(LOW), va[h, keys, :])
            if merge:
                mixed = state * jnp.exp(old - top) + mixed
            states.append((top, mixed))
            score = ahead if h + 1 < hpd else None
        return states

    def hold(i, low, high):
        def part(side):
            rows = rows16(i * st + side * hr, hr)
            for h, (top, mixed) in enumerate(attend(i, side, low, high, False)):
                acc[h, rows, :] = jnp.where(half_column[h] == TOP, top, mixed)

        loop(0, 2, part)

    def att_copy(i, o):
        d = lax.rem(v + o, nv)
        return remote(
            att.at[i, d], got.at[slot, group, i], a_send.at[i, o], a_recv.at[slot, group, i],
            (owner, d),
        )

    def att_own(i):
        return pltpu.make_async_copy(att.at[i, v], got.at[slot, group, i], a_local.at[i])

    def settle(i, low, high, merge):
        def part(side):
            rows = rows16(i * st + side * hr, hr)
            done = []
            for h, (top, mixed) in enumerate(attend(i, side, low, high, merge)):
                total = extra_column(mixed, h, 0)
                done.append(mixed / total)
                high_part, mid, tail = three_parts(-(top + jnp.log(total)))
                at = half_column[h]
                qa[h, rows, :] = jnp.where(
                    at == 1,
                    high_part,
                    jnp.where(at == 2, mid, jnp.where(at == 3, tail, qa[h, rows, :])),
                )
            owners = pl.ds(side * (nv // 2), nv // 2)
            for pair in range(plan.pairs):
                other = 0.0 if hpd == 1 else done[2 * pair + 1]
                att[i, owners, :, pair * LANES : (pair + 1) * LANES] = (
                    jnp.where(half_data[2 * pair], done[2 * pair], other)
                    .astype(LOW)
                    .reshape(nv // 2, sr, LANES)
                )

        loop(0, 2, part)
        loop(1, nv, lambda o: att_copy(i, o).start())

        @pl.when(mine)
        def _():
            att_own(i).start()

        @pl.when(jnp.logical_not(mine))
        def _():
            att_copy(i, 0).start()

    def arrive(i):
        def take(o):
            s = lax.rem(v + o, nv)
            arrived(xw.at[i, s], recv.at[i, s])

            @pl.when(mine)
            def _():
                forward_copy(i, s).start()

        loop(1, nv, take)

        @pl.when(jnp.logical_not(mine))
        def _():
            arrived(xw.at[i, v], recv.at[i, v])

        @pl.when(i + 2 < sub)
        def _():
            loop((i + 2) * nv, (i + 3) * nv, start_out)

        project(i)

    @pl.when(mine)
    def _():
        own_x().wait()
        loop(0, sub, lambda n: forward_copy(n, v).start())

    early = min(2, sub)
    loop(0, early, arrive)
    if early < sub:
        loop(0, early, lambda i: hold(i, 0, early))
    for i in range(early, sub):
        arrive(i)
        if i < sub - 1:
            hold(i, 0, i + 1)
    for copy in stores[:3]:
        copy.start()
    if early < sub:
        settle(sub - 1, 0, sub, False)
        loop(0, early, lambda i: settle(i, early, sub, True))
        for i in range(early, sub - 1):
            settle(i, i + 1, sub, True)
    else:
        loop(0, sub, lambda i: settle(i, 0, sub, False))

    for copy in stores[3:5]:
        copy.start()
    for copy in loads:
        copy.wait()

    step = 512
    cr = nw * sr

    def target(w, g):
        return b - core + g % 2, (core * nw + w) * plan.cpw + g // 2

    def is_self(w, g):
        tb, tv = target(w, g)
        return (tb == b) & (tv == v)

    def grad_copy(i, w, g):
        return remote(
            got.at[w, g, i], d_att.at[i, v], d_send.at[i, w, g], d_recv.at[i, v], target(w, g)
        )

    def grad_own(i, w, g):
        return pltpu.make_async_copy(got.at[w, g, i], d_att.at[i, v], d_local.at[i])

    def slope_at(n):
        return n % hpd, slice(n // hpd * cr, (n // hpd + 1) * cr)

    def keep_slope(f, slope):
        for n in range(step // LANES):
            h, at = slope_at(f // LANES + n)
            acc[h, at, :] = slope[:, n * LANES : (n + 1) * LANES]

    def kept_slope(f):
        places = [slope_at(f // LANES + n) for n in range(step // LANES)]
        return jnp.concatenate([acc[h, at, :] for h, at in places], axis=1)

    def tokens(n):
        i = lax.rem(n + sub - 1, sub)
        for w in range(nw):
            for g in range(groups):
                own = mine & (slot == w) & (group == g)

                @pl.when(own)
                def _():
                    att_own(i).wait()

                @pl.when(jnp.logical_not(own))
                def _():
                    arrived(got.at[w, g, i], a_recv.at[w, g, i])

        rows = rows16(i * cr, cr)
        if hpd == 1:
            parts = [got[:, g, i] + got[:, g + 1, i] for g in range(0, groups, 2)]
        else:
            parts = [got[:, g, i] for g in range(groups)]
        attended = jnp.concatenate([part.reshape(cr, pw) for part in parts], axis=1)
        att_s[rows, :] = attended
        first = x[:, i].reshape(cr, width).astype(F32) + mm(attended, wo_s[...]) + vec(bo)
        unit1, inv1 = norm_parts(first)
        middle = unit1 * vec(g1) + vec(s1)
        mid_low = middle.astype(LOW)
        mid_s[rows, :] = mid_low
        total = middle + vec(bd)

        def before(f):
            return mm(mid_low, wu_s[:, f : f + step]) + bu[f : f + step].reshape(1, -1).astype(F32)

        pre = before(0)
        for f in range(0, ff, step):
            ahead = before(f + step) if f + step < ff else None
            act, slope = gelu_and_slope(pre)
            act_low = act.astype(LOW)
            act_s[rows, f : f + step] = act_low
            keep_slope(f, slope)
            total = total + mm(act_low, wd_s[f : f + step, :])
            pre = ahead
        unit2, inv2 = norm_parts(total)
        result = (unit2 * vec(g2) + vec(s2)).astype(LOW).reshape(nw, sr, width)
        grad = cot_s[:, i].reshape(cr, width).astype(F32)
        cot_s[:, i] = result
        small[0:1, :] += sum_rows(grad * unit2)
        small[1:2, :] += sum_rows(grad)
        d_second = norm_back(unit2, inv2, grad * vec(g2))
        branch = d_second.astype(LOW)
        branch_s[rows, :] = branch
        small[2:3, :] += sum_rows(branch.astype(F32))
        d_middle = d_second

        def back(f):
            return mm_nt(branch, wd_s[f : f + step, :])

        d_act = back(0)
        for f in range(0, ff, step):
            ahead = back(f + step) if f + step < ff else None
            d_pre = (d_act * kept_slope(f)).astype(LOW)
            pre_s[rows, f : f + step] = d_pre
            at = 6 + f // step
            small[at : at + 1, :] += sum_rows(d_pre.astype(F32))
            d_middle = d_middle + mm_nt(d_pre, wu_s[:, f : f + step])
            d_act = ahead
        small[3:4, :] += sum_rows(d_middle * unit1)
        small[4:5, :] += sum_rows(d_middle)
        d_one = norm_back(unit1, inv1, d_middle * vec(g1))
        d_first[:, i] = d_one.reshape(nw, sr, width)
        d_out = d_one.astype(LOW)
        dout_s[rows, :] = d_out
        small[5:6, :] += sum_rows(d_out.astype(F32))
        d_attended = mm_nt(d_out, wo_s[...]).astype(LOW).reshape(nw, sr, width)
        for w in range(nw):
            for g in range(groups):
                at = (g // 2) * LANES if hpd == 1 else g * pw
                got[w, g, i] = d_attended[w, :, at : at + pw]

                @pl.when(is_self(w, g))
                def _():
                    grad_own(i, w, g).start()

                @pl.when(jnp.logical_not(is_self(w, g)))
                def _():
                    grad_copy(i, w, g).start()

    loop(0, sub, tokens)
    for copy in stores[5:]:
        copy.start()

    blocks = 2 * ff // step + 1
    spare = plan.piece - 3 * width

    half = width // 2

    def stage_copies(n):
        at = (n % 3) * width
        return [
            pltpu.make_async_copy(
                waug.at[:, (n % 2) * width + side * half : (n % 2) * width + (side + 1) * half],
                pieces.at[2 * (n // 3) + side, at : at + width, :],
                stage_sem.at[n % 2, side],
            )
            for side in range(2)
        ]

    def put(n, value):
        if n >= 2:
            for copy in stage_copies(n - 2):
                copy.wait()
        waug[:, (n % 2) * width : (n % 2 + 1) * width] = value.astype(LOW)
        for copy in stage_copies(n):
            copy.start()

    for f in range(ff // step):
        put(2 * f, mm_tn(mid_s[...], pre_s[:, f * step : (f + 1) * step]))
        put(2 * f + 1, mm_tn(act_s[:, f * step : (f + 1) * step], branch_s[...]))
    put(blocks - 1, mm_tn(att_s[...], dout_s[...]))
    for n in (blocks - 2, blocks - 1):
        for copy in stage_copies(n):
            copy.wait()
    if spare > 0:
        waug[:, 0:width] = jnp.zeros((width, width), LOW)
        for n in range(pieces.shape[0]):
            for at in range(0, spare, width):
                size = min(width, spare - at)
                pad = pltpu.make_async_copy(
                    waug.at[0:size, 0:half],
                    pieces.at[n, 3 * width + at : 3 * width + at + size, :],
                    stage_sem.at[0, 0],
                )
                pad.start()
                pad.wait()

    def take(n):
        i, s = n // nv, lax.rem(n, nv)

        @pl.when(jnp.logical_not((s == v) & mine))
        def _():
            arrived(d_att.at[i, s], d_recv.at[i, s])

    loop(0, sub * nv, take)

    def finish(i):
        for w in range(nw):
            for g in range(groups):

                @pl.when(is_self(w, g))
                def _():
                    grad_own(i, w, g).wait()

                @pl.when(jnp.logical_not(is_self(w, g)))
                def _():
                    grad_copy(i, w, g).wait_send()

        @pl.when(jnp.logical_not(mine))
        def _():
            att_copy(i, 0).wait_send()

        loop(1, nv, lambda o: att_copy(i, o).wait_send())

        @pl.when(mine)
        def _():
            loop(0, nv, lambda s: forward_copy(i, s).wait_send())

    loop(0, sub, finish)
    loop(0, sub * nv, end_out)
    for copy in stores:
        copy.wait()


class Sums:
    def __init__(
        self, plan, rows, source, sums, box1, half, box2, box3, box4, fin, pair_sems, many_sems
    ):
        self.plan, self.source, self.sums = plan, source, sums
        self.box1, self.half, self.box2, self.box3 = box1, half, box2, box3
        self.box4, self.fin = box4, fin
        self.s, self.m = pair_sems, many_sems
        b, v = lax.axis_index("batch"), lax.axis_index("var")
        self.b, self.v = b, v
        self.core, self.xs, self.lo, self.hi = lax.rem(b, 2), b // 2, lax.rem(v, 2), v // 2
        self.nh = plan.nv // 2
        self.half_rows = rows // 2
        self.quarter, self.eighth = rows // 4, rows // 8
        self.chunk = self.eighth // self.nh

    def mate(self, p, first):
        over_x = (p % 2 == 0) if first else (p % 2 == 1)
        db, dv = self.b + 2 - 4 * self.xs, self.v + 1 - 2 * self.lo
        return jnp.where(over_x, db, self.b), jnp.where(over_x, self.v, dv)

    def coords(self, p):
        even = p % 2 == 0
        return jnp.where(even, self.xs, self.lo), jnp.where(even, self.lo, self.xs)

    def pair(self, p, at, src, dst, device):
        return remote(src, dst, self.s.at[0, at, p], self.s.at[1, at, p], device)

    def core_copy(self, p):
        rows = rows16((1 - self.core) * self.half_rows, self.half_rows)
        device = (self.b + 1 - 2 * self.core, self.v)
        return self.pair(p, 0, self.source(p).at[rows, :], self.box1.at[p], device)

    def own_copy(self, p):
        rows = rows16(self.core * self.half_rows, self.half_rows)
        return pltpu.make_async_copy(
            self.source(p).at[rows, :], self.half.at[p], self.s.at[0, 6, p]
        )

    def first_copy(self, p):
        c1, _ = self.coords(p)
        rows = rows16((1 - c1) * self.quarter, self.quarter)
        return self.pair(p, 1, self.half.at[p, rows, :], self.box2.at[p], self.mate(p, True))

    def second_copy(self, p):
        c1, c2 = self.coords(p)
        rows = rows16(c1 * self.quarter + (1 - c2) * self.eighth, self.eighth)
        return self.pair(p, 2, self.half.at[p, rows, :], self.box3.at[p], self.mate(p, False))

    def peer(self, o):
        return lax.rem(self.hi + o, self.nh)

    def many_copy(self, p, o):
        d = self.peer(o)
        c1, c2 = self.coords(p)
        rows = rows16(c1 * self.quarter + c2 * self.eighth + d * self.chunk, self.chunk)
        return remote(
            self.half.at[p, rows, :], self.box4.at[p, self.hi],
            self.m.at[0, 0, p, o], self.m.at[1, 0, p, self.hi], (self.b, d * 2 + self.lo),
        )

    def region(self, p, start, size):
        return self.sums.at[p, rows16(self.core * self.half_rows + start, size), :]

    def chunk_at(self, p, who):
        c1, c2 = self.coords(p)
        start = c1 * self.quarter + c2 * self.eighth + who * self.chunk
        return self.region(p, start, self.chunk)

    def spread_copy(self, p, o):
        return remote(
            self.fin.at[p], self.chunk_at(p, self.hi),
            self.m.at[0, 1, p, o], self.m.at[1, 1, p, self.hi],
            (self.b, self.peer(o) * 2 + self.lo),
        )

    def keep_copy(self, p):
        return pltpu.make_async_copy(
            self.fin.at[p], self.chunk_at(p, self.hi), self.s.at[0, 7, p]
        )

    def back_second(self, p):
        c1, c2 = self.coords(p)
        at = self.region(p, c1 * self.quarter + c2 * self.eighth, self.eighth)
        return self.pair(p, 3, at, at, self.mate(p, False))

    def back_first(self, p):
        c1, _ = self.coords(p)
        at = self.region(p, c1 * self.quarter, self.quarter)
        return self.pair(p, 4, at, at, self.mate(p, True))

    def back_core(self, p):
        at = self.region(p, 0, self.half_rows)
        return self.pair(p, 5, at, at, (self.b + 1 - 2 * self.core, self.v))

    def came(self, p, at, ref):
        arrived(ref, self.s.at[1, at, p])

    def step0(self, p):
        self.core_copy(p).start()
        self.own_copy(p).start()

    def step1(self, p):
        self.own_copy(p).wait()
        self.came(p, 0, self.box1.at[p])
        self.half[p] = (self.half[p].astype(F32) + self.box1[p].astype(F32)).astype(LOW)
        self.first_copy(p).start()

    def add(self, p, start, size, other):
        rows = rows16(start, size)
        total = self.half[p, rows, :].astype(F32) + other.astype(F32)
        self.half[p, rows, :] = total.astype(LOW)

    def step2(self, p):
        c1, _ = self.coords(p)
        self.came(p, 1, self.box2.at[p])
        self.first_copy(p).wait_send()
        self.add(p, c1 * self.quarter, self.quarter, self.box2[p])
        self.second_copy(p).start()

    def step3(self, p):
        c1, c2 = self.coords(p)
        self.came(p, 2, self.box3.at[p])
        self.second_copy(p).wait_send()
        self.add(p, c1 * self.quarter + c2 * self.eighth, self.eighth, self.box3[p])
        loop(1, self.nh, lambda o: self.many_copy(p, o).start())

    def step4(self, p):
        def take(o):
            s = self.peer(o)
            arrived(self.box4.at[p, s], self.m.at[1, 0, p, s])

        loop(1, self.nh, take)
        c1, c2 = self.coords(p)
        rows = rows16(c1 * self.quarter + c2 * self.eighth + self.hi * self.chunk, self.chunk)
        total = self.half[p, rows, :].astype(F32)
        for o in range(1, self.nh):
            total = total + self.box4[p, self.peer(o)].astype(F32)
        self.fin[p] = total.astype(LOW)
        self.keep_copy(p).start()
        loop(1, self.nh, lambda o: self.spread_copy(p, o).start())

    def step5(self, p):
        def take(o):
            s = self.peer(o)
            arrived(self.chunk_at(p, s), self.m.at[1, 1, p, s])

        loop(1, self.nh, take)
        self.keep_copy(p).wait()
        self.back_second(p).start()

    def step6(self, p):
        c1, c2 = self.coords(p)
        self.came(p, 3, self.region(p, c1 * self.quarter + (1 - c2) * self.eighth, self.eighth))
        self.back_first(p).start()

    def step7(self, p):
        c1, _ = self.coords(p)
        self.came(p, 4, self.region(p, (1 - c1) * self.quarter, self.quarter))
        self.back_core(p).start()

    def step8(self, p):
        rows = rows16((1 - self.core) * self.half_rows, self.half_rows)
        self.came(p, 5, self.sums.at[p, rows, :])
        self.core_copy(p).wait_send()
        loop(1, self.nh, lambda o: self.many_copy(p, o).wait_send())
        loop(1, self.nh, lambda o: self.spread_copy(p, o).wait_send())
        self.back_second(p).wait_send()
        self.back_first(p).wait_send()
        self.back_core(p).wait_send()

    DUE = (0, 2, 8, 14, 20, 26, 30, 36, 38)
    LAG = 2

    def at(self, tile, count):
        steps = (
            self.step0, self.step1, self.step2, self.step3, self.step4,
            self.step5, self.step6, self.step7, self.step8,
        )
        @pl.when((tile & 1) == 0)
        def _():
            for due, step in reversed(tuple(zip(self.DUE, steps))):
                piece = (tile - due) >> 1

                @pl.when((piece >= 0) & (piece < count))
                def _():
                    step(piece)

    def end(self, count):
        return self.DUE[-1] + self.LAG * (count - 1) + 1


class ShortSums:
    def __init__(self, plan, source, sums, box1, half, box2, fin, pair_sems, many_sems):
        self.plan, self.source, self.sums = plan, source, sums
        self.box1, self.half, self.box2, self.fin = box1, half, box2, fin
        self.s, self.m = pair_sems, many_sems
        b, v = lax.axis_index("batch"), lax.axis_index("var")
        self.b, self.v, self.core = b, v, lax.rem(b, 2)
        self.peers = 2 * plan.nv
        self.me = (b // 2) * plan.nv + v
        self.half_rows = source.shape[1] // 2
        self.chunk = self.half_rows // self.peers

    def peer(self, o):
        return lax.rem(self.me + o, self.peers)

    def device(self, j):
        return (j // self.plan.nv) * 2 + self.core, lax.rem(j, self.plan.nv)

    def core_copy(self, p):
        rows = rows16((1 - self.core) * self.half_rows, self.half_rows)
        return remote(
            self.source.at[p, rows, :], self.box1.at[p], self.s.at[0, 0, p], self.s.at[1, 0, p],
            (self.b + 1 - 2 * self.core, self.v),
        )

    def many_copy(self, p, o):
        j = self.peer(o)
        return remote(
            self.half.at[p, rows16(j * self.chunk, self.chunk), :], self.box2.at[p, self.me],
            self.m.at[0, 0, p, o], self.m.at[1, 0, p, self.me], self.device(j),
        )

    def chunk_at(self, p, j):
        rows = rows16(self.core * self.half_rows + j * self.chunk, self.chunk)
        return self.sums.at[p, rows, :]

    def spread_copy(self, p, o):
        return remote(
            self.fin.at[p], self.chunk_at(p, self.me),
            self.m.at[0, 1, p, o], self.m.at[1, 1, p, self.me], self.device(self.peer(o)),
        )

    def keep_copy(self, p):
        return pltpu.make_async_copy(
            self.fin.at[p], self.chunk_at(p, self.me), self.s.at[0, 2, p]
        )

    def back_core(self, p):
        at = self.sums.at[p, rows16(self.core * self.half_rows, self.half_rows), :]
        return remote(
            at, at, self.s.at[0, 1, p], self.s.at[1, 1, p],
            (self.b + 1 - 2 * self.core, self.v),
        )

    def step0(self, p):
        self.core_copy(p).start()

    def step1(self, p):
        arrived(self.box1.at[p], self.s.at[1, 0, p])
        rows = rows16(self.core * self.half_rows, self.half_rows)
        total = self.source[p, rows, :].astype(F32) + self.box1[p].astype(F32)
        self.half[p] = total.astype(LOW)
        loop(1, self.peers, lambda o: self.many_copy(p, o).start())

    def step2(self, p):
        def take(o):
            j = self.peer(o)
            arrived(self.box2.at[p, j], self.m.at[1, 0, p, j])

        loop(1, self.peers, take)
        total = self.half[p, rows16(self.me * self.chunk, self.chunk), :].astype(F32)
        for o in range(1, self.peers):
            total = total + self.box2[p, self.peer(o)].astype(F32)
        self.fin[p] = total.astype(LOW)
        self.keep_copy(p).start()
        loop(1, self.peers, lambda o: self.spread_copy(p, o).start())

    def step3(self, p):
        def take(o):
            j = self.peer(o)
            arrived(self.chunk_at(p, j), self.m.at[1, 1, p, j])

        loop(1, self.peers, take)
        self.keep_copy(p).wait()
        self.back_core(p).start()

    def step4(self, p):
        rows = rows16((1 - self.core) * self.half_rows, self.half_rows)
        arrived(self.sums.at[p, rows, :], self.s.at[1, 1, p])
        self.core_copy(p).wait_send()
        loop(1, self.peers, lambda o: self.many_copy(p, o).wait_send())
        loop(1, self.peers, lambda o: self.spread_copy(p, o).wait_send())
        self.back_core(p).wait_send()


def backward_kernel(
    plan, count, qa_in, ka_in, va_in, att, d_att, xw, wq, wk, wv, d_first, ga, small,
    gi, sums, first_sums, last_sums, vectors,
    qa, ka, va,
    da, kt, dqt, dk, dv, dall, wcat, part, mate, own, final, dx, gacc, gb,
    bsum, box1, half, box2, box3, box4, fin, box1b, halfb, box2b, finb,
    ga0, box1c, halfc, box2c, box3c, box4c, finc,
    bias_mine, vec1, vec2, xs, firsts,
    p_send, p_recv, send, recv, local_sem, sa, ma, sb, mb, sc, mc, vs, vs2, load,
):
    nv, nw, hpd, hd = plan.nv, plan.nw, plan.hpd, plan.hd
    sub, sr, st, pairs = plan.sub, plan.sr, plan.st, plan.pairs
    slots, groups, pw, width = plan.slots, plan.groups, plan.pw, plan.width
    b, v, core, parity, slot, group = plan.here()
    mine = parity == core
    owner = b - core + parity
    base = plan.base(group)
    odds = [plan.odd(h, group) for h in range(hpd)]
    core_mate = (b + 1 - 2 * core, v)
    x_copy = pltpu.make_async_copy(xw, xs, load.at[0])
    first_copy = pltpu.make_async_copy(d_first, firsts, load.at[1])
    pair_copies = [
        [
            pltpu.make_async_copy(
                src.at[2 * pair : min(2 * pair + 2, hpd)],
                dst.at[2 * pair : min(2 * pair + 2, hpd)],
                load.at[2 + 3 * pair + n],
            )
            for n, (src, dst) in enumerate(((qa_in, qa), (ka_in, ka), (va_in, va)))
        ]
        for pair in range(pairs)
    ]
    for copies in pair_copies:
        for copy in copies:
            copy.start()
    x_copy.start()
    first_copy.start()
    greet(plan, b, v, core, across=True)
    tokens = Sums(
        plan, plan.piece, lambda p: ga.at[p], sums, box1, half, box2, box3, box4, fin, sa, ma
    )
    last = pairs - 1
    tail = ShortSums(plan, gb, last_sums, box1b, halfb, box2b, finb, sb, mb)
    opening = Sums(
        plan, ga0.shape[1], lambda p: ga0.at[p], first_sums,
        box1c, halfc, box2c, box3c, box4c, finc, sc, mc,
    )

    tile = lane_of((st, LANES))

    def prepare(i, pair):
        rows = rows16(i * st, st)
        for h in range(2 * pair, min(2 * pair + 2, hpd)):
            at = (h // 2) * LANES
            data = in_half(tile, odds[h], hd)
            column = extra_lane(tile, odds[h], hd)
            grad = d_att[i, :, :, at : at + LANES].reshape(st, LANES).astype(F32)
            prod = grad * att[i, :, :, at : at + LANES].reshape(st, LANES).astype(F32)
            delta = jnp.sum(jnp.where(data, prod, 0.0), axis=1, keepdims=True)
            high, mid, tail = (term.astype(F32) for term in three_parts(-delta))
            extra = jnp.where(column == 0, high, jnp.where(column == 1, mid, tail))
            da[h, rows, :] = jnp.where(
                data, grad, jnp.where((column >= 0) & (column < 3), extra, 0.0)
            ).astype(LOW)

    def open_pair(pair):
        for copy in pair_copies[pair]:
            copy.wait()
        for h in range(2 * pair, min(2 * pair + 2, hpd)):
            turned = jnp.transpose(ka[h])
            if hpd == 1:
                kt[h] = jnp.where(odds[h] == 1, turned[hd:], turned[:hd])
            else:
                kt[h] = turned[odds[h] * hd : (odds[h] + 1) * hd]
        loop(0, sub, lambda i: prepare(i, pair))

    for kind, ref in enumerate((wq, wk, wv)):
        wcat[:, kind * pw : (kind + 1) * pw] = ref[:, pl.ds(base, pw)]
    dk[...] = jnp.zeros_like(dk)
    dv[...] = jnp.zeros_like(dv)
    dqt[...] = jnp.zeros_like(dqt)
    gacc[...] = jnp.zeros_like(gacc)
    all_here(plan, across=True)
    tokens.step0(0)

    def attend(pair, qi, ki):
        rows, keys = pl.ds(pl.multiple_of(qi * st, st), st), pl.ds(pl.multiple_of(ki * st, st), st)
        key_parts, value_parts = [], []
        for h in range(2 * pair, min(2 * pair + 2, hpd)):
            q = qa[h, rows, :]
            d = da[h, rows, :]
            prob = jnp.exp(mm_nt(ka[h, keys, :], q))
            d_score = (prob * mm_nt(va[h, keys, :], d)).astype(LOW)
            value_parts.append(mm(prob.astype(LOW), d))
            key_parts.append(mm(d_score, q))
            dqt[pl.ds(pair * LANES + odds[h] * hd, hd), rows] += mm(kt[h, :, keys], d_score)
        if hpd == 1:
            key_parts.append(jnp.zeros_like(key_parts[0]))
            value_parts.append(jnp.zeros_like(value_parts[0]))
        first = in_half(tile, odds[2 * pair], hd)
        dv[pair, keys, :] += jnp.where(first, value_parts[0], value_parts[1])
        dk[pair, keys, :] += jnp.where(first, key_parts[0], key_parts[1])

    def gather_pair(pair, i):
        rows = rows16(i * st, st)
        at = pair * LANES
        dqt_block = dqt[at : at + LANES, pl.ds(pl.multiple_of(i * st, st), st)]
        dq = jnp.transpose(dqt_block)
        terms = (dq * (hd**-0.5), dk[pair, rows, :], dv[pair, rows, :])
        for kind, term in enumerate(terms):
            dall[rows, kind * pw + at : kind * pw + at + LANES] = term.astype(LOW)
        block = xs[rows, :]
        turned = (dqt_block * (hd**-0.5), jnp.transpose(terms[1]), jnp.transpose(terms[2]))
        for kind, term in enumerate(turned):
            gacc[kind * LANES : (kind + 1) * LANES, :] += mm(term.astype(LOW), block)
        for kind, row in ((0, 0), (2, 1)):
            bsum[row * 8 : row * 8 + 8, :] += fold_rows(terms[kind].astype(LOW).astype(F32))

    lanes = gb.shape[-1]

    def put_pair(pair, ref):
        if plan.piece > 3 * width or lanes > LANES:
            ref[...] = jnp.zeros_like(ref)
        at = base if hpd == 1 else pl.multiple_of(group * LANES, LANES)
        for kind in range(3):
            ref[0, kind * width : (kind + 1) * width, pl.ds(at, LANES)] = jnp.transpose(
                gacc[kind * LANES : (kind + 1) * LANES, :]
            ).astype(LOW)

    def put_vectors(ref, low):
        block = small[...].astype(LOW)
        for part in range(width // lanes):
            ref[0, low + 16 * part : low + 16 * part + 16, :] = block[
                :, part * lanes : (part + 1) * lanes
            ]

    x_copy.wait()

    bsum[...] = jnp.zeros_like(bsum)

    def put_bias(pair):
        at = base if hpd == 1 else pl.multiple_of(group * LANES, LANES)
        for row in range(2):
            bias_mine[2 * pair + row : 2 * pair + row + 1, pl.ds(at, LANES)] = jnp.sum(
                bsum[row * 8 : row * 8 + 8, :], axis=0, keepdims=True
            )
        bsum[...] = jnp.zeros_like(bsum)

    bias_mine[...] = jnp.zeros_like(bias_mine)
    for pair in range(pairs - 1):
        open_pair(pair)

        def square(t):
            tokens.at(pair * sub * sub + t + 1, count)
            attend(pair, t // sub, lax.rem(t, sub))

        loop(0, sub * sub, square)
        loop(0, sub, lambda i: gather_pair(pair, i))
        put_bias(pair)
        if pair == 0:
            put_pair(pair, ga0)
            put_vectors(ga0, 3 * width)
            opening.step0(0)
        gacc[...] = jnp.zeros_like(gacc)

    open_pair(last)
    before = last * sub * sub
    share = nv // groups
    mine_rows = share * sr

    def device_of(g):
        return b - core + g % 2, v - lax.rem(v, plan.cpw) + g // 2

    def part_copy(i, g):
        return remote(
            part.at[i, g * mine_rows : (g + 1) * mine_rows, :], mate.at[i, group],
            p_send.at[i, g], p_recv.at[i, group], device_of(g),
        )

    def send_parts(i):
        rows = rows16(i * st, st)
        total = mm_nt(dall[rows, :], wcat[...])
        part[i] = total.astype(LOW)
        own[i % 2] = total
        for g in range(groups):

            @pl.when(g != group)
            def _():
                part_copy(i, g).start()

    def final_copy(i, n):
        d = group * share + n
        return remote(
            final.at[i, n], dx.at[slot, i], send.at[i, n], recv.at[slot, i], (owner, d)
        )

    def is_own(n):
        return mine & (group * share + n == v)

    def own_copy(i, n):
        return pltpu.make_async_copy(final.at[i, n], dx.at[slot, i], local_sem.at[i])

    def send_final(i):
        total = own[i % 2, rows16(group * mine_rows, mine_rows), :]
        for g in range(groups):

            @pl.when(g != group)
            def _():
                arrived(mate.at[i, g], p_recv.at[i, g])

            @pl.when(g == group)
            def _():
                mate[i, g] = jnp.zeros((mine_rows, width), LOW)

        for g in range(groups):
            total = total + mate[i, g].astype(F32)
        final[i] = total.astype(LOW).reshape(share, sr, width)
        for n in range(share):

            @pl.when(is_own(n))
            def _():
                own_copy(i, n).start()

            @pl.when(jnp.logical_not(is_own(n)))
            def _():
                final_copy(i, n).start()

    def shrink(i):
        start = i * (2 * sub - i)

        def angle(t):
            done = start + t
            tokens.at(before + done + 1, count)
            if last > 0:
                for due, step in (
                    (1, opening.step1), (7, opening.step2), (11, opening.step3),
                    (16, opening.step4), (21, opening.step5),
                ):

                    @pl.when(done == due)
                    def _():
                        step(0)

            n = sub - i
            attend(
                last, jnp.where(t < n, i, i + 1 + t - n), jnp.where(t < n, i + t, i)
            )

        loop(0, 2 * (sub - i) - 1, angle)
        gather_pair(last, i)

        @pl.when(i == sub - 1)
        def _():
            put_pair(last, gb)
            if last == 0:
                put_vectors(gb, 3 * width)
            tail.step0(0)

        send_parts(i)

        @pl.when(i == sub - 1)
        def _():
            tail.step1(0)

        @pl.when(i > 0)
        def _():
            send_final(i - 1)

    loop(0, sub, shrink)
    tiles = before + sub * sub
    loop(tiles + 1, max(tiles + 1, tokens.end(count)), lambda t: tokens.at(t, count))

    put_bias(last)
    core_vec = remote(bias_mine, vec1, vs.at[0], vs.at[1], core_mate)
    core_vec.start()
    send_final(sub - 1)
    arrived(vec1, vs.at[1])
    core_vec.wait_send()
    bias_mine[...] = bias_mine[...] + vec1[...]

    def vec_spread(o):
        return remote(
            bias_mine, vec2.at[tail.me], vs2.at[0, o], vs2.at[1, tail.me],
            tail.device(tail.peer(o)),
        )

    loop(1, 2 * nv, lambda o: vec_spread(o).start())
    vec2[tail.me] = bias_mine[...]
    first_copy.wait()

    def finish(i):
        for n in range(share):

            @pl.when(is_own(n))
            def _():
                own_copy(i, n).wait()

        for w in range(nw):
            self_sent = mine & (slot == w) & (v // share == group)

            @pl.when(jnp.logical_not(self_sent))
            def _():
                arrived(dx.at[w, i], recv.at[w, i])

        gi[:, i] = (firsts[:, i] + dx[:, i].astype(F32)).astype(LOW)

    if last > 0:
        opening.step6(0)
    loop(0, sub - 1, finish)
    tail.step2(0)
    if last > 0:
        opening.step7(0)

    def vec_take(o):
        j = tail.peer(o)
        arrived(vec2.at[j], vs2.at[1, j])

    loop(1, 2 * nv, vec_take)
    total = vec2[0]
    for j in range(1, 2 * nv):
        total = total + vec2[j]
    vectors[...] = total
    loop(sub - 1, sub, finish)
    tail.step3(0)
    if last > 0:
        opening.step8(0)

    def close(i):
        for n in range(share):

            @pl.when(jnp.logical_not(is_own(n)))
            def _():
                final_copy(i, n).wait_send()

        for g in range(groups):

            @pl.when(g != group)
            def _():
                part_copy(i, g).wait_send()

    loop(0, sub, close)
    loop(1, 2 * nv, lambda o: vec_spread(o).wait_send())
    tail.step4(0)


def output_kernel(
    plan, ff, sums, first_sums, last_sums, vectors,
    gq, gk, gv, go, gu, gd, bq, bv, bo, g1, s1, bu, bd, g2, s2,
    block_in, first_in, last_in, block_out, wide_out, load, store,
):
    width = plan.width
    blocks = ff // width
    lanes = last_in.shape[-1]
    total = 2 * blocks + 1

    def block_loads(n):
        at = (n % 3) * width
        return [
            pltpu.make_async_copy(
                sums.at[2 * (n // 3) + side, at : at + width, :],
                block_in.at[n, :, side * (width // 2) : (side + 1) * (width // 2)],
                load.at[2 * n + side],
            )
            for side in range(2)
        ]

    def block_store(n):
        if n == 2 * blocks:
            dst = go
        elif n % 2:
            dst = gd.at[n // 2 * width : (n // 2 + 1) * width, :]
        else:
            dst = gu.at[:, n // 2 * width : (n // 2 + 1) * width]
        return pltpu.make_async_copy(block_out.at[n], dst, store.at[n])

    parts = [(first_sums, first_in), (last_sums, last_in)][2 - min(plan.pairs, 2) :]
    part_loads = [
        pltpu.make_async_copy(src, dst, load.at[2 * total + n]) for n, (src, dst) in enumerate(parts)
    ]
    wide_stores = [
        pltpu.make_async_copy(wide_out.at[n], dst, store.at[total + n])
        for n, dst in enumerate((gq, gk, gv))
    ]
    for n in range(total):
        for copy in block_loads(n):
            copy.start()
    for copy in part_loads:
        copy.start()
    for n in range(total):
        for copy in block_loads(n):
            copy.wait()
        block_out[n] = block_in[n].astype(F32)
        block_store(n).start()
    for copy in part_loads:
        copy.wait()
    groups = lanes // LANES
    for kind in range(3):
        for pair, (_, ref) in enumerate(parts):
            for group in range(groups):
                at = (group * plan.pairs + pair) * LANES
                wide_out[kind, :, at : at + LANES] = ref[
                    0, kind * width : (kind + 1) * width, group * LANES : (group + 1) * LANES
                ].astype(F32)
        wide_stores[kind].start()
    low = 3 * width
    ref = parts[0][1]
    rows = jnp.concatenate(
        [ref[0, low + 16 * n : low + 16 * n + 16, :] for n in range(width // lanes)], axis=1
    ).astype(F32)
    for n, ref in enumerate((g2, s2, bd, g1, s1, bo)):
        ref[...] = rows[n]
    for f in range(blocks):
        bu[f * width : (f + 1) * width] = rows[6 + f]
    for row, ref in enumerate((bq, bv)):
        for pair in range(plan.pairs):
            for group in range(groups):
                at = (group * plan.pairs + pair) * LANES
                ref[at : at + LANES] = vectors[2 * pair + row, group * LANES : (group + 1) * LANES]
    for n in range(total):
        block_store(n).wait()
    for copy in wide_stores:
        copy.wait()


def params(number):
    return pltpu.CompilerParams(
        vmem_limit_bytes=VMEM_BYTES, collective_id=number, has_side_effects=True
    )


def sum_scratch(plan, number, lanes, piece):
    nh = plan.nv // 2
    return [
        pltpu.VMEM((number, piece // 2, lanes), LOW),
        pltpu.VMEM((number, piece // 2, lanes), LOW),
        pltpu.VMEM((number, piece // 4, lanes), LOW),
        pltpu.VMEM((number, piece // 8, lanes), LOW),
        pltpu.VMEM((number, nh, piece // 8 // nh, lanes), LOW),
        pltpu.VMEM((number, piece // 8 // nh, lanes), LOW),
    ]


def short_scratch(plan, rows, lanes):
    peers = 2 * plan.nv
    return [
        pltpu.VMEM((1, rows // 2, lanes), LOW),
        pltpu.VMEM((1, rows // 2, lanes), LOW),
        pltpu.VMEM((1, peers, rows // 2 // peers, lanes), LOW),
        pltpu.VMEM((1, rows // 2 // peers, lanes), LOW),
    ]


def sum_sems(number, steps, peers):
    return [DMA((2, steps, number)), DMA((2, 2, number, peers))]


def body(
    plan,
    inputs, w_query, w_key, w_value, w_out, b_query, b_value, b_out, gain_one, shift_one,
    w_up, b_up, w_down, b_down, gain_two, shift_two, cotangent, valid_mask,
):
    nv, nw, width = plan.nv, plan.nw, plan.width
    slots, hpd, hd, pw, groups = plan.slots, plan.hpd, plan.hd, plan.pw, plan.groups
    sub, sr, st, pairs = plan.sub, plan.sr, plan.st, plan.pairs
    ff = w_up.shape[1]
    rows, cr = plan.rows, nw * sr
    piece = plan.piece
    shape = jax.ShapeDtypeStruct
    ANY = pl.BlockSpec(memory_space=pl.ANY)
    count = (2 * ff // width + 1) // 3 * 2

    heads = shape((hpd, slots, LANES), LOW)
    blocked = (nw, sub, sr, width)
    mask = valid_mask.reshape(nv, sub, sr).transpose(1, 0, 2).reshape(slots // LANES, LANES)
    qa, ka, va, xw, att, out, d_first, d_att, ga, small = pl.pallas_call(
        functools.partial(forward_kernel, plan, ff),
        out_shape=(
            heads,
            heads,
            heads,
            shape((sub, nv, sr, width), LOW),
            shape((sub, nv, sr, pw), LOW),
            shape(blocked, LOW),
            shape(blocked, F32),
            shape((sub, nv, sr, pw), LOW),
            shape((count, piece, width // 2), LOW),
            shape((16, width), F32),
        ),
        in_specs=[VM] * 7 + [ANY, ANY] + [VM] * 3 + [ANY, VM, ANY] + [VM] * 3,
        out_specs=(ANY,) * 7 + (VM, ANY, VM),
        scratch_shapes=[
            pltpu.VMEM((hpd, slots, LANES), LOW),
            pltpu.VMEM((hpd, slots, LANES), LOW),
            pltpu.VMEM((hpd, slots, LANES), LOW),
            pltpu.VMEM((sub, nv, sr, width), LOW),
            pltpu.VMEM((sub, nv, sr, pw), LOW),
            pltpu.VMEM(blocked, F32),
            pltpu.VMEM(blocked, LOW),
            pltpu.VMEM((width, width), LOW),
            pltpu.VMEM((width, ff), LOW),
            pltpu.VMEM((ff, width), LOW),
            pltpu.VMEM((width, max(3 * hpd * LANES, 2 * width)), LOW),
            pltpu.VMEM((slots, LANES), LOW),
            pltpu.VMEM((8, width), F32),
            pltpu.VMEM((hpd, max((sub - 1) * st, ff // LANES // hpd * cr), LANES), F32),
            pltpu.VMEM((nw, groups, sub, sr, pw), LOW),
            pltpu.VMEM((rows, width), LOW),
            pltpu.VMEM((rows, width), LOW),
            pltpu.VMEM((rows, ff), LOW),
            pltpu.VMEM((rows, ff), LOW),
            pltpu.VMEM((rows, width), LOW),
            pltpu.VMEM((rows, width), LOW),
            DMA((sub, nv)),
            DMA((sub, nv)),
            DMA((sub, nv)),
            DMA((sub, nv)),
            DMA((nw, groups, sub)),
            DMA((sub,)),
            DMA((sub, nw, groups)),
            DMA((sub, nv)),
            DMA((sub,)),
            DMA,
            DMA((2, 2)),
            DMA((4,)),
            DMA((7,)),
        ],
        compiler_params=params(1),
        name="forward_and_tokens",
    )(
        inputs.reshape(blocked), w_query, w_key, w_value, b_query, b_value, mask,
        cotangent.reshape(blocked), w_out, b_out, gain_one, shift_one,
        w_up, b_up, w_down, b_down, gain_two, shift_two,
    )

    share = nv // groups
    lanes = width // pairs
    unit = 16 * 4 * nv
    more = -(-(3 * width + 16 * width // lanes) // unit) * unit
    first_rows = more if pairs > 1 else unit
    last_rows = piece if pairs > 1 else more
    gi, sums, first_sums, last_sums, vectors = pl.pallas_call(
        functools.partial(backward_kernel, plan, count),
        out_shape=(
            shape(blocked, LOW),
            shape((count, piece, width // 2), LOW),
            shape((1, first_rows, lanes), LOW),
            shape((1, last_rows, lanes), LOW),
            shape((8, lanes), F32),
        ),
        in_specs=[ANY] * 3 + [VM] * 2 + [ANY] + [VM] * 3 + [ANY, ANY, VM],
        out_specs=(VM, ANY, ANY, ANY, VM),
        scratch_shapes=[
            pltpu.VMEM((hpd, slots, LANES), LOW),
            pltpu.VMEM((hpd, slots, LANES), LOW),
            pltpu.VMEM((hpd, slots, LANES), LOW),
            pltpu.VMEM((hpd, slots, LANES), LOW),
            pltpu.VMEM((hpd, hd, slots), LOW),
            pltpu.VMEM((pw, slots), F32),
            pltpu.VMEM((pairs, slots, LANES), F32),
            pltpu.VMEM((pairs, slots, LANES), F32),
            pltpu.VMEM((slots, 3 * pw), LOW),
            pltpu.VMEM((width, 3 * pw), LOW),
            pltpu.VMEM((sub, st, width), LOW),
            pltpu.VMEM((sub, groups, share * sr, width), LOW),
            pltpu.VMEM((2, st, width), F32),
            pltpu.VMEM((sub, share, sr, width), LOW),
            pltpu.VMEM((nw, sub, sr, width), LOW),
            pltpu.VMEM((3 * LANES, width), F32),
            pltpu.VMEM((1, last_rows, lanes), LOW),
            pltpu.VMEM((16, LANES), F32),
        ]
        + sum_scratch(plan, count, width // 2, piece)
        + short_scratch(plan, last_rows, lanes)
        + [pltpu.VMEM((1, first_rows, lanes), LOW)]
        + sum_scratch(plan, 1, lanes, first_rows)
        + [
            pltpu.VMEM((8, lanes), F32),
            pltpu.VMEM((8, lanes), F32),
            pltpu.VMEM((2 * nv, 8, lanes), F32),
            pltpu.VMEM((slots, width), LOW),
            pltpu.VMEM(blocked, F32),
            DMA((sub, groups)),
            DMA((sub, groups)),
            DMA((sub, share)),
            DMA((nw, sub)),
            DMA((sub,)),
        ]
        + sum_sems(count, 8, nv // 2)
        + sum_sems(1, 3, 2 * nv)
        + sum_sems(1, 8, nv // 2)
        + [DMA((2,)), DMA((2, 2 * nv)), DMA((2 + 3 * pairs,))],
        compiler_params=params(2),
        name="attention_backward",
    )(
        qa, ka, va, att, d_att, xw.reshape(slots, width), w_query, w_key, w_value, d_first,
        ga, small,
    )

    square = shape((width, width), F32)
    one = shape((width,), F32)
    total = 2 * ff // width + 1
    gq, gk, gv, go, gu, gd, bq, bv, bo, g1, s1, bu, bd, g2, s2 = pl.pallas_call(
        functools.partial(output_kernel, plan, ff),
        out_shape=(square,) * 4
        + (shape((width, ff), F32), shape((ff, width), F32))
        + (one,) * 5
        + (shape((ff,), F32),)
        + (one,) * 3,
        in_specs=[ANY] * 3 + [VM],
        out_specs=(ANY,) * 6 + (VM,) * 9,
        scratch_shapes=[
            pltpu.VMEM((total, width, width), LOW),
            pltpu.VMEM((1, first_rows, lanes), LOW),
            pltpu.VMEM((1, last_rows, lanes), LOW),
            pltpu.VMEM((total, width, width), F32),
            pltpu.VMEM((3, width, width), F32),
            DMA((2 * total + 2,)),
            DMA((total + 3,)),
        ],
        compiler_params=pltpu.CompilerParams(vmem_limit_bytes=VMEM_BYTES),
        name="outputs",
    )(sums, first_sums, last_sums, vectors)
    return (
        out.reshape(inputs.shape), gi.reshape(inputs.shape),
        gq, gk, gv, go, bq, bv, bo, g1, s1, gu, bu, gd, bd, g2, s2,
    )


def solution(mesh):
    data = P("batch", "var", None)

    def run(*args):
        plan = Plan(mesh, args[0].shape)
        return jax.shard_map(
            functools.partial(body, plan),
            mesh=mesh,
            in_specs=(data,) + (P(),) * 15 + (data, P()),
            out_specs=(data, data) + (P(),) * 15,
            check_vma=False,
        )(*args)

    return run
```

```python
import functools

import jax
import jax.numpy as jnp
from jax import lax
from jax.experimental import pallas as pl
from jax.experimental.pallas import tpu as pltpu
from jax.sharding import PartitionSpec as P

HEADS = 8
LANES = 128
LOW = jnp.bfloat16
F32 = jnp.float32
MESH = pl.DeviceIdType.MESH
DMA = pltpu.SemaphoreType.DMA
VM = pl.BlockSpec(memory_space=pltpu.VMEM)
VMEM_BYTES = 62 << 20


def mm(left, right):
    return jnp.dot(left, right, preferred_element_type=F32)


def mm_nt(left, right):
    return lax.dot_general(left, right, (((1,), (1,)), ((), ())), preferred_element_type=F32)


def mm_tn(left, right):
    return lax.dot_general(left, right, (((0,), (0,)), ((), ())), preferred_element_type=F32)


def lane_of(shape):
    return lax.broadcasted_iota(jnp.int32, shape, len(shape) - 1)


def in_half(lane, odd, hd):
    return (lane >= hd) == (odd == 1)


def extra_lane(lane, odd, hd):
    return jnp.where(in_half(lane, odd, hd), -1, lane - hd * (1 - odd))


def vec(ref):
    return ref[...].reshape(1, -1).astype(F32)


def three_parts(value):
    high = value.astype(LOW)
    rest = value - high.astype(F32)
    mid = rest.astype(LOW)
    tail = (rest - mid.astype(F32)).astype(LOW)
    return high, mid, tail


class Plan:
    def __init__(self, mesh, inputs_shape):
        windows, slots, width = inputs_shape
        self.nv = mesh.shape["var"]
        self.nb = mesh.shape["batch"]
        self.nw = windows // self.nb
        self.local = slots // self.nv
        self.slots = slots
        self.width = width
        self.hd = width // HEADS
        self.cpw = self.nv // (2 * self.nw)
        self.groups = 2 * self.cpw
        self.hpd = HEADS // self.groups
        self.pairs = max(self.hpd // 2, 1)
        self.pw = self.pairs * LANES
        self.rows = self.nw * self.local
        self.sub = next(
            n for n in (5, 4, 2, 1)
            if self.local % (16 * n) == 0 and slots % (LANES * n) == 0
        )
        self.sr = self.local // self.sub
        self.st = self.nv * self.sr
        unit = 16 * self.nv * self.nb
        self.piece = -(-3 * width // unit) * unit

    def here(self):
        b = lax.axis_index("batch")
        v = lax.axis_index("var")
        core = lax.rem(b, 2)
        window = v // self.cpw
        parity = window // self.nw
        slot = lax.rem(window, self.nw)
        group = lax.rem(v, self.cpw) * 2 + core
        return b, v, core, parity, slot, group

    def odd(self, h, group):
        return lax.rem(group, 2) if self.hpd == 1 else h % 2

    def base(self, group):
        if self.hpd == 1:
            return pl.multiple_of((group // 2) * LANES, LANES)
        return pl.multiple_of(group * self.pw, LANES)


def loop(low, high, step):
    def run(index, carry):
        step(index)
        return carry

    lax.fori_loop(low, high, run, 0)


def greet(plan, b, v, core, across=False):
    barrier = pltpu.get_barrier_semaphore()
    partner = b + 1 - 2 * core

    def greet_same(o):
        pl.semaphore_signal(
            barrier, inc=1, device_id=(b, lax.rem(v + o, plan.nv)), device_id_type=MESH
        )

    def greet_other(o):
        pl.semaphore_signal(
            barrier, inc=1, device_id=(partner, lax.rem(v + o, plan.nv)), device_id_type=MESH
        )

    loop(1, plan.nv, greet_same)
    loop(0, plan.nv, greet_other)
    def greet_across(o):
        pl.semaphore_signal(
            barrier, inc=1, device_id=(b + 2 - 4 * (b // 2), lax.rem(v + o, plan.nv)),
            device_id_type=MESH,
        )

    if across:
        loop(0, plan.nv, greet_across)


def all_here(plan, across=False):
    count = (3 if across else 2) * plan.nv - 1
    pl.semaphore_wait(pltpu.get_barrier_semaphore(), count)


def arrived(ref, sem):
    pltpu.make_async_copy(ref, ref, sem).wait()


def gelu_and_slope(pre):
    size = jnp.abs(pre)
    bell = jnp.exp(pre * pre * -0.5)
    t = 1.0 / (1.0 + 0.2316418882663604 * size)
    poly = t * (
        0.127414796
        + t * (-0.142248368 + t * (0.7107068705 + t * (-0.7265760135 + t * 0.5307027145)))
    )
    below = poly * bell
    phi = jnp.where(pre < 0, below, 1.0 - below)
    return pre * phi, phi + pre * bell * 0.3989422804014327


def fold_rows(value):
    rows, width = value.shape
    return jnp.sum(value.reshape(rows // 8, 8, width), axis=0)


def sum_rows(value):
    return jnp.sum(fold_rows(value), axis=0, keepdims=True)


def norm_parts(rows):
    center = rows - jnp.mean(rows, axis=-1, keepdims=True)
    spread = jnp.mean(center * center, axis=-1, keepdims=True)
    inverse = lax.rsqrt(spread + 1e-05)
    return center * inverse, inverse


def norm_back(unit, inverse, grad):
    return inverse * (
        grad
        - jnp.mean(grad, axis=-1, keepdims=True)
        - unit * jnp.mean(grad * unit, axis=-1, keepdims=True)
    )


def remote(src, dst, send_sem, recv_sem, device):
    return pltpu.make_async_remote_copy(
        src_ref=src, dst_ref=dst, send_sem=send_sem, recv_sem=recv_sem,
        device_id=device, device_id_type=MESH,
    )


def rows16(start, size):
    return pl.ds(pl.multiple_of(start, 16), size)


TOP = 8


def forward_kernel(
    plan, ff, x, wq, wk, wv, bq, bv, mask, cot, wo, bo, g1, s1, wu, bu, wd, bd, g2, s2,
    qa_out, ka_out, va_out, xw_out, att_out, out_out, first_out, d_att, pieces, small,
    qa, ka, va, xw, att, d_first, cot_s, wo_s, wu_s, wd_s,
    waug, kaug, bias, acc, got, att_s, mid_s, act_s, pre_s, branch_s, dout_s,
    send, recv, pass_on, a_send, a_recv, a_local, d_send, d_recv, d_local, local_sem, stage_sem,
    load, store,
):
    nv, nw, hpd, hd, pw = plan.nv, plan.nw, plan.hpd, plan.hd, plan.pw
    sub, sr, st, width, groups = plan.sub, plan.sr, plan.st, plan.width, plan.groups
    b, v, core, parity, slot, group = plan.here()
    mine = parity == core
    partner = b + 1 - 2 * core
    owner = b - core + parity
    odds = [plan.odd(h, group) for h in range(hpd)]
    loads = [
        pltpu.make_async_copy(src, dst, load.at[n])
        for n, (src, dst) in enumerate(((wo, wo_s), (wu, wu_s), (wd, wd_s), (cot, cot_s)))
    ]
    stores = [
        pltpu.make_async_copy(src, dst, store.at[n])
        for n, (src, dst) in enumerate((
            (xw, xw_out), (ka, ka_out), (va, va_out), (qa, qa_out), (att, att_out),
            (d_first, first_out), (cot_s, out_out),
        ))
    ]
    greet(plan, b, v, core)

    def out_copy(i, o):
        d = lax.rem(v + o, nv)
        return remote(
            x.at[lax.rem(d // plan.cpw, nw), i], xw.at[i, v], send.at[i, o], recv.at[i, v], (b, d)
        )

    def wanted(o):
        return (lax.rem(v + o, nv) // plan.cpw) // nw == core

    def start_out(n):
        @pl.when(wanted(lax.rem(n, nv)) & (lax.rem(n, nv) > 0))
        def _():
            out_copy(n // nv, lax.rem(n, nv)).start()

    def end_out(n):
        @pl.when(wanted(lax.rem(n, nv)) & (lax.rem(n, nv) > 0))
        def _():
            out_copy(n // nv, lax.rem(n, nv)).wait_send()

    def own_x():
        return pltpu.make_async_copy(x.at[slot], xw.at[:, v], local_sem)

    def forward_copy(i, s):
        at = xw.at[i, s]
        return remote(at, at, pass_on.at[i, s], recv.at[i, s], (partner, v))

    lane = lane_of((width, LANES))
    base = plan.base(group)
    for kind, ref in enumerate((wq, wk, wv)):
        for h in range(hpd):
            both = ref[:, pl.ds(base + (h // 2) * LANES, LANES)].astype(F32)
            at = (kind * hpd + h) * LANES
            waug[:, at : at + LANES] = jnp.where(in_half(lane, odds[h], hd), both, 0.0).astype(LOW)
    bias[0:1, :] = vec(bq)
    bias[1:2, :] = vec(bv)

    all_here(plan)
    loop(0, min(2, sub) * nv, start_out)
    for copy in loads:
        copy.start()

    @pl.when(mine)
    def _():
        own_x().start()

    square = lane_of((LANES, LANES))
    diag = square == lax.broadcasted_iota(jnp.int32, (LANES, LANES), 0)
    place = lax.rem(square, hd)
    ones = jnp.where((place > 0) & (place < 4), 1.0, 0.0)
    for at in range(plan.slots // LANES):
        row = jnp.where(mask[at : at + 1, :] > 0, 0.0, -1e30)
        column = jnp.sum(jnp.where(diag, row, 0.0), axis=1, keepdims=True)
        kaug[at * LANES : (at + 1) * LANES, :] = jnp.where(place == 0, column, ones).astype(LOW)

    tile = lane_of((st, LANES))
    data = [in_half(tile, odd, hd) for odd in odds]
    column = [extra_lane(tile, odd, hd) for odd in odds]

    def extra_column(value, h, at):
        if hpd == 1:
            return jnp.where(
                odds[h] == 1, value[:, at : at + 1], value[:, hd + at : hd + at + 1]
            )
        at += hd * (1 - odds[h])
        return value[:, at : at + 1]

    small[...] = jnp.zeros_like(small)

    def bias_of(kind, h):
        return bias[kind : kind + 1, pl.ds(base + (h // 2) * LANES, LANES)]

    def project(i):
        rows = rows16(i * st, st)
        extra = kaug[rows, :].astype(F32)
        both = mm(xw[i].reshape(st, width), waug[:, 0 : 3 * hpd * LANES])
        for h in range(hpd):
            q = both[:, h * LANES : (h + 1) * LANES] + bias_of(0, h)
            q = q.astype(LOW).astype(F32) * (hd**-0.5)
            qa[h, rows, :] = jnp.where(data[h], q, jnp.where(column[h] == 0, 1.0, 0.0)).astype(LOW)
            k = both[:, (hpd + h) * LANES : (hpd + h + 1) * LANES]
            ka[h, rows, :] = jnp.where(data[h], k, extra).astype(LOW)
            val = both[:, (2 * hpd + h) * LANES : (2 * hpd + h + 1) * LANES] + bias_of(1, h)
            va[h, rows, :] = jnp.where(
                data[h], val, jnp.where((column[h] >= 0) & (column[h] < 3), 1.0, 0.0)
            ).astype(LOW)


    def attend(i, side, hr, low, high, merge):
        rows = rows16(i * st + side * hr, hr)
        keys = slice(low * st, high * st)
        score = mm_nt(qa[0, rows, :], ka[0, keys, :])
        states = []
        for h in range(hpd):
            if h + 1 < hpd:
                ahead = mm_nt(qa[h + 1, rows, :], ka[h + 1, keys, :])
            top = jnp.max(score, axis=1, keepdims=True)
            if merge:
                state = acc[h, rows, :]
                old = extra_column(state, h, TOP)
                top = jnp.maximum(old, top)
            expo = jnp.exp(score - top)
            mixed = mm(expo.astype(LOW), va[h, keys, :])
            if merge:
                mixed = state * jnp.exp(old - top) + mixed
            states.append((top, mixed))
            score = ahead if h + 1 < hpd else None
        return states

    def height(low, high):
        return st if high - low <= 3 else st // 2

    def hold(i, low, high):
        hr = height(low, high)
        def part(side):
            rows = rows16(i * st + side * hr, hr)
            for h, (top, mixed) in enumerate(attend(i, side, hr, low, high, False)):
                acc[h, rows, :] = jnp.where(column[h][:hr] == TOP, top, mixed)

        loop(0, st // hr, part)

    def att_copy(i, o):
        d = lax.rem(v + o, nv)
        return remote(
            att.at[i, d], got.at[slot, group, i], a_send.at[i, o], a_recv.at[slot, group, i],
            (owner, d),
        )

    def att_own(i):
        return pltpu.make_async_copy(att.at[i, v], got.at[slot, group, i], a_local.at[i])

    def settle(i, low, high, merge):
        hr = height(low, high)
        nh = nv * hr // st

        def part(side):
            rows = rows16(i * st + side * hr, hr)
            done = []
            for h, (top, mixed) in enumerate(attend(i, side, hr, low, high, merge)):
                total = extra_column(mixed, h, 0)
                done.append(mixed / total)
                high_part, mid, tail = three_parts(-(top + jnp.log(total)))
                at = column[h][:hr]
                qa[h, rows, :] = jnp.where(
                    at == 1,
                    high_part,
                    jnp.where(at == 2, mid, jnp.where(at == 3, tail, qa[h, rows, :])),
                )
            owners = pl.ds(side * nh, nh)
            for pair in range(plan.pairs):
                other = 0.0 if hpd == 1 else done[2 * pair + 1]
                att[i, owners, :, pair * LANES : (pair + 1) * LANES] = (
                    jnp.where(data[2 * pair][:hr], done[2 * pair], other)
                    .astype(LOW)
                    .reshape(nh, sr, LANES)
                )

        loop(0, st // hr, part)
        loop(1, nv, lambda o: att_copy(i, o).start())

        @pl.when(mine)
        def _():
            att_own(i).start()

        @pl.when(jnp.logical_not(mine))
        def _():
            att_copy(i, 0).start()

    def arrive(i):
        def take(o):
            s = lax.rem(v + o, nv)
            arrived(xw.at[i, s], recv.at[i, s])

            @pl.when(mine)
            def _():
                forward_copy(i, s).start()

        loop(1, nv, take)

        @pl.when(jnp.logical_not(mine))
        def _():
            arrived(xw.at[i, v], recv.at[i, v])

        @pl.when(i + 2 < sub)
        def _():
            loop((i + 2) * nv, (i + 3) * nv, start_out)

        project(i)

    @pl.when(mine)
    def _():
        own_x().wait()
        loop(0, sub, lambda n: forward_copy(n, v).start())

    early = min(2, sub)
    loop(0, early, arrive)
    if early < sub:
        loop(0, early, lambda i: hold(i, 0, early))
    for i in range(early, sub):
        arrive(i)
        if i < sub - 1:
            hold(i, 0, i + 1)
    for copy in stores[:3]:
        copy.start()
    if early < sub:
        settle(sub - 1, 0, sub, False)
        loop(0, early, lambda i: settle(i, early, sub, True))
        for i in range(early, sub - 1):
            settle(i, i + 1, sub, True)
    else:
        loop(0, sub, lambda i: settle(i, 0, sub, False))

    for copy in stores[3:5]:
        copy.start()
    for copy in loads:
        copy.wait()

    step = 512
    cr = nw * sr

    def target(w, g):
        return b - core + g % 2, (core * nw + w) * plan.cpw + g // 2

    def is_self(w, g):
        tb, tv = target(w, g)
        return (tb == b) & (tv == v)

    def grad_copy(i, w, g):
        return remote(
            got.at[w, g, i], d_att.at[i, v], d_send.at[i, w, g], d_recv.at[i, v], target(w, g)
        )

    def grad_own(i, w, g):
        return pltpu.make_async_copy(got.at[w, g, i], d_att.at[i, v], d_local.at[i])

    def slope_at(n):
        return n % hpd, slice(n // hpd * cr, (n // hpd + 1) * cr)

    def keep_slope(f, slope):
        for n in range(step // LANES):
            h, at = slope_at(f // LANES + n)
            acc[h, at, :] = slope[:, n * LANES : (n + 1) * LANES]

    def kept_slope(f):
        places = [slope_at(f // LANES + n) for n in range(step // LANES)]
        return jnp.concatenate([acc[h, at, :] for h, at in places], axis=1)

    def tokens(n):
        i = lax.rem(n + sub - 1, sub)
        for w in range(nw):
            for g in range(groups):
                own = mine & (slot == w) & (group == g)

                @pl.when(own)
                def _():
                    att_own(i).wait()

                @pl.when(jnp.logical_not(own))
                def _():
                    arrived(got.at[w, g, i], a_recv.at[w, g, i])

        rows = rows16(i * cr, cr)
        if hpd == 1:
            parts = [got[:, g, i] + got[:, g + 1, i] for g in range(0, groups, 2)]
        else:
            parts = [got[:, g, i] for g in range(groups)]
        attended = jnp.concatenate([part.reshape(cr, pw) for part in parts], axis=1)
        att_s[rows, :] = attended
        first = x[:, i].reshape(cr, width).astype(F32) + mm(attended, wo_s[...]) + vec(bo)
        unit1, inv1 = norm_parts(first)
        middle = unit1 * vec(g1) + vec(s1)
        mid_low = middle.astype(LOW)
        mid_s[rows, :] = mid_low
        total = middle + vec(bd)

        def before(f):
            return mm(mid_low, wu_s[:, f : f + step]) + bu[f : f + step].reshape(1, -1).astype(F32)

        pre = before(0)
        for f in range(0, ff, step):
            ahead = before(f + step) if f + step < ff else None
            act, slope = gelu_and_slope(pre)
            act_low = act.astype(LOW)
            act_s[rows, f : f + step] = act_low
            keep_slope(f, slope)
            total = total + mm(act_low, wd_s[f : f + step, :])
            pre = ahead
        unit2, inv2 = norm_parts(total)
        result = (unit2 * vec(g2) + vec(s2)).astype(LOW).reshape(nw, sr, width)
        grad = cot_s[:, i].reshape(cr, width).astype(F32)
        cot_s[:, i] = result
        small[0:1, :] += sum_rows(grad * unit2)
        small[1:2, :] += sum_rows(grad)
        d_second = norm_back(unit2, inv2, grad * vec(g2))
        branch = d_second.astype(LOW)
        branch_s[rows, :] = branch
        small[2:3, :] += sum_rows(branch.astype(F32))
        d_middle = d_second

        def back(f):
            return mm_nt(branch, wd_s[f : f + step, :])

        d_act = back(0)
        for f in range(0, ff, step):
            ahead = back(f + step) if f + step < ff else None
            d_pre = (d_act * kept_slope(f)).astype(LOW)
            pre_s[rows, f : f + step] = d_pre
            at = 6 + f // step
            small[at : at + 1, :] += sum_rows(d_pre.astype(F32))
            d_middle = d_middle + mm_nt(d_pre, wu_s[:, f : f + step])
            d_act = ahead
        small[3:4, :] += sum_rows(d_middle * unit1)
        small[4:5, :] += sum_rows(d_middle)
        d_one = norm_back(unit1, inv1, d_middle * vec(g1))
        d_first[:, i] = d_one.reshape(nw, sr, width)
        d_out = d_one.astype(LOW)
        dout_s[rows, :] = d_out
        small[5:6, :] += sum_rows(d_out.astype(F32))
        d_attended = mm_nt(d_out, wo_s[...]).astype(LOW).reshape(nw, sr, width)
        for w in range(nw):
            for g in range(groups):
                at = (g // 2) * LANES if hpd == 1 else g * pw
                got[w, g, i] = d_attended[w, :, at : at + pw]

                @pl.when(is_self(w, g))
                def _():
                    grad_own(i, w, g).start()

                @pl.when(jnp.logical_not(is_self(w, g)))
                def _():
                    grad_copy(i, w, g).start()

    loop(0, sub, tokens)
    for copy in stores[5:]:
        copy.start()

    blocks = 2 * ff // step + 1
    spare = plan.piece - 3 * width

    half = width // 2

    def stage_copies(n):
        at = (n % 3) * width
        return [
            pltpu.make_async_copy(
                waug.at[:, (n % 2) * width + side * half : (n % 2) * width + (side + 1) * half],
                pieces.at[2 * (n // 3) + side, at : at + width, :],
                stage_sem.at[n % 2, side],
            )
            for side in range(2)
        ]

    def put(n, value):
        if n >= 2:
            for copy in stage_copies(n - 2):
                copy.wait()
        waug[:, (n % 2) * width : (n % 2 + 1) * width] = value.astype(LOW)
        for copy in stage_copies(n):
            copy.start()

    for f in range(ff // step):
        put(2 * f, mm_tn(mid_s[...], pre_s[:, f * step : (f + 1) * step]))
        put(2 * f + 1, mm_tn(act_s[:, f * step : (f + 1) * step], branch_s[...]))
    put(blocks - 1, mm_tn(att_s[...], dout_s[...]))
    for n in (blocks - 2, blocks - 1):
        for copy in stage_copies(n):
            copy.wait()
    if spare > 0:
        waug[:, 0:width] = jnp.zeros((width, width), LOW)
        for n in range(pieces.shape[0]):
            for at in range(0, spare, width):
                size = min(width, spare - at)
                pad = pltpu.make_async_copy(
                    waug.at[0:size, 0:half],
                    pieces.at[n, 3 * width + at : 3 * width + at + size, :],
                    stage_sem.at[0, 0],
                )
                pad.start()
                pad.wait()

    def take(n):
        i, s = n // nv, lax.rem(n, nv)

        @pl.when(jnp.logical_not((s == v) & mine))
        def _():
            arrived(d_att.at[i, s], d_recv.at[i, s])

    loop(0, sub * nv, take)

    def finish(i):
        for w in range(nw):
            for g in range(groups):

                @pl.when(is_self(w, g))
                def _():
                    grad_own(i, w, g).wait()

                @pl.when(jnp.logical_not(is_self(w, g)))
                def _():
                    grad_copy(i, w, g).wait_send()

        @pl.when(jnp.logical_not(mine))
        def _():
            att_copy(i, 0).wait_send()

        loop(1, nv, lambda o: att_copy(i, o).wait_send())

        @pl.when(mine)
        def _():
            loop(0, nv, lambda s: forward_copy(i, s).wait_send())

    loop(0, sub, finish)
    loop(0, sub * nv, end_out)
    for copy in stores:
        copy.wait()


class Sums:
    def __init__(
        self, plan, rows, source, sums, box1, half, box2, box3, box4, fin, pair_sems, many_sems
    ):
        self.plan, self.source, self.sums = plan, source, sums
        self.box1, self.half, self.box2, self.box3 = box1, half, box2, box3
        self.box4, self.fin = box4, fin
        self.s, self.m = pair_sems, many_sems
        b, v = lax.axis_index("batch"), lax.axis_index("var")
        self.b, self.v = b, v
        self.core, self.xs, self.lo, self.hi = lax.rem(b, 2), b // 2, lax.rem(v, 2), v // 2
        self.nh = plan.nv // 2
        self.half_rows = rows // 2
        self.quarter, self.eighth = rows // 4, rows // 8
        self.chunk = self.eighth // self.nh

    def mate(self, p, first):
        over_x = (p % 2 == 0) if first else (p % 2 == 1)
        db, dv = self.b + 2 - 4 * self.xs, self.v + 1 - 2 * self.lo
        return jnp.where(over_x, db, self.b), jnp.where(over_x, self.v, dv)

    def coords(self, p):
        even = p % 2 == 0
        return jnp.where(even, self.xs, self.lo), jnp.where(even, self.lo, self.xs)

    def pair(self, p, at, src, dst, device):
        return remote(src, dst, self.s.at[0, at, p], self.s.at[1, at, p], device)

    def core_copy(self, p):
        rows = rows16((1 - self.core) * self.half_rows, self.half_rows)
        device = (self.b + 1 - 2 * self.core, self.v)
        return self.pair(p, 0, self.source(p).at[rows, :], self.box1.at[p], device)

    def own_copy(self, p):
        rows = rows16(self.core * self.half_rows, self.half_rows)
        return pltpu.make_async_copy(
            self.source(p).at[rows, :], self.half.at[p], self.s.at[0, 6, p]
        )

    def first_copy(self, p):
        c1, _ = self.coords(p)
        rows = rows16((1 - c1) * self.quarter, self.quarter)
        return self.pair(p, 1, self.half.at[p, rows, :], self.box2.at[p], self.mate(p, True))

    def second_copy(self, p):
        c1, c2 = self.coords(p)
        rows = rows16(c1 * self.quarter + (1 - c2) * self.eighth, self.eighth)
        return self.pair(p, 2, self.half.at[p, rows, :], self.box3.at[p], self.mate(p, False))

    def peer(self, o):
        return lax.rem(self.hi + o, self.nh)

    def many_copy(self, p, o):
        d = self.peer(o)
        c1, c2 = self.coords(p)
        rows = rows16(c1 * self.quarter + c2 * self.eighth + d * self.chunk, self.chunk)
        return remote(
            self.half.at[p, rows, :], self.box4.at[p, self.hi],
            self.m.at[0, 0, p, o], self.m.at[1, 0, p, self.hi], (self.b, d * 2 + self.lo),
        )

    def region(self, p, start, size):
        return self.sums.at[p, rows16(self.core * self.half_rows + start, size), :]

    def chunk_at(self, p, who):
        c1, c2 = self.coords(p)
        start = c1 * self.quarter + c2 * self.eighth + who * self.chunk
        return self.region(p, start, self.chunk)

    def spread_copy(self, p, o):
        return remote(
            self.fin.at[p], self.chunk_at(p, self.hi),
            self.m.at[0, 1, p, o], self.m.at[1, 1, p, self.hi],
            (self.b, self.peer(o) * 2 + self.lo),
        )

    def keep_copy(self, p):
        return pltpu.make_async_copy(
            self.fin.at[p], self.chunk_at(p, self.hi), self.s.at[0, 7, p]
        )

    def back_second(self, p):
        c1, c2 = self.coords(p)
        at = self.region(p, c1 * self.quarter + c2 * self.eighth, self.eighth)
        return self.pair(p, 3, at, at, self.mate(p, False))

    def back_first(self, p):
        c1, _ = self.coords(p)
        at = self.region(p, c1 * self.quarter, self.quarter)
        return self.pair(p, 4, at, at, self.mate(p, True))

    def back_core(self, p):
        at = self.region(p, 0, self.half_rows)
        return self.pair(p, 5, at, at, (self.b + 1 - 2 * self.core, self.v))

    def came(self, p, at, ref):
        arrived(ref, self.s.at[1, at, p])

    def step0(self, p):
        self.core_copy(p).start()
        self.own_copy(p).start()

    def step1(self, p):
        self.own_copy(p).wait()
        self.came(p, 0, self.box1.at[p])
        self.half[p] = (self.half[p].astype(F32) + self.box1[p].astype(F32)).astype(LOW)
        self.first_copy(p).start()

    def add(self, p, start, size, other):
        rows = rows16(start, size)
        total = self.half[p, rows, :].astype(F32) + other.astype(F32)
        self.half[p, rows, :] = total.astype(LOW)

    def step2(self, p):
        c1, _ = self.coords(p)
        self.came(p, 1, self.box2.at[p])
        self.first_copy(p).wait_send()
        self.add(p, c1 * self.quarter, self.quarter, self.box2[p])
        self.second_copy(p).start()

    def step3(self, p):
        c1, c2 = self.coords(p)
        self.came(p, 2, self.box3.at[p])
        self.second_copy(p).wait_send()
        self.add(p, c1 * self.quarter + c2 * self.eighth, self.eighth, self.box3[p])
        loop(1, self.nh, lambda o: self.many_copy(p, o).start())

    def step4(self, p):
        def take(o):
            s = self.peer(o)
            arrived(self.box4.at[p, s], self.m.at[1, 0, p, s])

        loop(1, self.nh, take)
        c1, c2 = self.coords(p)
        rows = rows16(c1 * self.quarter + c2 * self.eighth + self.hi * self.chunk, self.chunk)
        total = self.half[p, rows, :].astype(F32)
        for o in range(1, self.nh):
            total = total + self.box4[p, self.peer(o)].astype(F32)
        self.fin[p] = total.astype(LOW)
        self.keep_copy(p).start()
        loop(1, self.nh, lambda o: self.spread_copy(p, o).start())

    def step5(self, p):
        def take(o):
            s = self.peer(o)
            arrived(self.chunk_at(p, s), self.m.at[1, 1, p, s])

        loop(1, self.nh, take)
        self.keep_copy(p).wait()
        self.back_second(p).start()

    def step6(self, p):
        c1, c2 = self.coords(p)
        self.came(p, 3, self.region(p, c1 * self.quarter + (1 - c2) * self.eighth, self.eighth))
        self.back_first(p).start()

    def step7(self, p):
        c1, _ = self.coords(p)
        self.came(p, 4, self.region(p, (1 - c1) * self.quarter, self.quarter))
        self.back_core(p).start()

    def step8(self, p):
        rows = rows16((1 - self.core) * self.half_rows, self.half_rows)
        self.came(p, 5, self.sums.at[p, rows, :])
        self.core_copy(p).wait_send()
        loop(1, self.nh, lambda o: self.many_copy(p, o).wait_send())
        loop(1, self.nh, lambda o: self.spread_copy(p, o).wait_send())
        self.back_second(p).wait_send()
        self.back_first(p).wait_send()
        self.back_core(p).wait_send()

    DUE = (0, 4, 10, 16, 22, 30, 34, 40, 44)
    LAG = 2

    def at(self, tile, count):
        steps = (
            self.step0, self.step1, self.step2, self.step3, self.step4,
            self.step5, self.step6, self.step7, self.step8,
        )
        @pl.when((tile & 1) == 0)
        def _():
            for due, step in reversed(tuple(zip(self.DUE, steps))):
                piece = (tile - due) >> 1

                @pl.when((piece >= 0) & (piece < count))
                def _():
                    step(piece)

    def end(self, count):
        return self.DUE[-1] + self.LAG * (count - 1) + 1


class ShortSums:
    def __init__(self, plan, source, sums, box1, half, box2, fin, pair_sems, many_sems):
        self.plan, self.source, self.sums = plan, source, sums
        self.box1, self.half, self.box2, self.fin = box1, half, box2, fin
        self.s, self.m = pair_sems, many_sems
        b, v = lax.axis_index("batch"), lax.axis_index("var")
        self.b, self.v, self.core = b, v, lax.rem(b, 2)
        self.peers = 2 * plan.nv
        self.me = (b // 2) * plan.nv + v
        self.half_rows = source.shape[1] // 2
        self.chunk = self.half_rows // self.peers

    def peer(self, o):
        return lax.rem(self.me + o, self.peers)

    def device(self, j):
        return (j // self.plan.nv) * 2 + self.core, lax.rem(j, self.plan.nv)

    def core_copy(self, p):
        rows = rows16((1 - self.core) * self.half_rows, self.half_rows)
        return remote(
            self.source.at[p, rows, :], self.box1.at[p], self.s.at[0, 0, p], self.s.at[1, 0, p],
            (self.b + 1 - 2 * self.core, self.v),
        )

    def many_copy(self, p, o):
        j = self.peer(o)
        return remote(
            self.half.at[p, rows16(j * self.chunk, self.chunk), :], self.box2.at[p, self.me],
            self.m.at[0, 0, p, o], self.m.at[1, 0, p, self.me], self.device(j),
        )

    def chunk_at(self, p, j):
        rows = rows16(self.core * self.half_rows + j * self.chunk, self.chunk)
        return self.sums.at[p, rows, :]

    def spread_copy(self, p, o):
        return remote(
            self.fin.at[p], self.chunk_at(p, self.me),
            self.m.at[0, 1, p, o], self.m.at[1, 1, p, self.me], self.device(self.peer(o)),
        )

    def keep_copy(self, p):
        return pltpu.make_async_copy(
            self.fin.at[p], self.chunk_at(p, self.me), self.s.at[0, 2, p]
        )

    def back_core(self, p):
        at = self.sums.at[p, rows16(self.core * self.half_rows, self.half_rows), :]
        return remote(
            at, at, self.s.at[0, 1, p], self.s.at[1, 1, p],
            (self.b + 1 - 2 * self.core, self.v),
        )

    def step0(self, p):
        self.core_copy(p).start()

    def step1(self, p):
        arrived(self.box1.at[p], self.s.at[1, 0, p])
        rows = rows16(self.core * self.half_rows, self.half_rows)
        total = self.source[p, rows, :].astype(F32) + self.box1[p].astype(F32)
        self.half[p] = total.astype(LOW)
        loop(1, self.peers, lambda o: self.many_copy(p, o).start())

    def step2(self, p):
        def take(o):
            j = self.peer(o)
            arrived(self.box2.at[p, j], self.m.at[1, 0, p, j])

        loop(1, self.peers, take)
        total = self.half[p, rows16(self.me * self.chunk, self.chunk), :].astype(F32)
        for o in range(1, self.peers):
            total = total + self.box2[p, self.peer(o)].astype(F32)
        self.fin[p] = total.astype(LOW)
        self.keep_copy(p).start()
        loop(1, self.peers, lambda o: self.spread_copy(p, o).start())

    def step3(self, p):
        def take(o):
            j = self.peer(o)
            arrived(self.chunk_at(p, j), self.m.at[1, 1, p, j])

        loop(1, self.peers, take)
        self.keep_copy(p).wait()
        self.back_core(p).start()

    def step4(self, p):
        rows = rows16((1 - self.core) * self.half_rows, self.half_rows)
        arrived(self.sums.at[p, rows, :], self.s.at[1, 1, p])
        self.core_copy(p).wait_send()
        loop(1, self.peers, lambda o: self.many_copy(p, o).wait_send())
        loop(1, self.peers, lambda o: self.spread_copy(p, o).wait_send())
        self.back_core(p).wait_send()


def backward_kernel(
    plan, count, qa_in, ka_in, va_in, att, d_att, xw, wq, wk, wv, d_first, ga, small,
    gi, sums, first_sums, last_sums, vectors,
    qa, ka, va,
    da, kt, dqt, dk, dv, dall, wcat, part, mate, own, final, dx, gacc, gb,
    bsum, box1, half, box2, box3, box4, fin, box1b, halfb, box2b, finb,
    ga0, box1c, halfc, box2c, box3c, box4c, finc,
    bias_mine, vec1, vec2, xs, firsts,
    p_send, p_recv, send, recv, local_sem, sa, ma, sb, mb, sc, mc, vs, vs2, load,
):
    nv, nw, hpd, hd = plan.nv, plan.nw, plan.hpd, plan.hd
    sub, sr, st, pairs = plan.sub, plan.sr, plan.st, plan.pairs
    slots, groups, pw, width = plan.slots, plan.groups, plan.pw, plan.width
    b, v, core, parity, slot, group = plan.here()
    mine = parity == core
    owner = b - core + parity
    base = plan.base(group)
    odds = [plan.odd(h, group) for h in range(hpd)]
    core_mate = (b + 1 - 2 * core, v)
    x_copy = pltpu.make_async_copy(xw, xs, load.at[0])
    first_copy = pltpu.make_async_copy(d_first, firsts, load.at[1])
    pair_copies = [
        [
            pltpu.make_async_copy(
                src.at[2 * pair : min(2 * pair + 2, hpd)],
                dst.at[2 * pair : min(2 * pair + 2, hpd)],
                load.at[2 + 3 * pair + n],
            )
            for n, (src, dst) in enumerate(((qa_in, qa), (ka_in, ka), (va_in, va)))
        ]
        for pair in range(pairs)
    ]
    for copies in pair_copies:
        for copy in copies:
            copy.start()
    x_copy.start()
    first_copy.start()
    greet(plan, b, v, core, across=True)
    tokens = Sums(
        plan, plan.piece, lambda p: ga.at[p], sums, box1, half, box2, box3, box4, fin, sa, ma
    )
    last = pairs - 1
    tail = ShortSums(plan, gb, last_sums, box1b, halfb, box2b, finb, sb, mb)
    opening = Sums(
        plan, ga0.shape[1], lambda p: ga0.at[p], first_sums,
        box1c, halfc, box2c, box3c, box4c, finc, sc, mc,
    )

    tile = lane_of((st, LANES))

    def prepare(i, pair):
        rows = rows16(i * st, st)
        for h in range(2 * pair, min(2 * pair + 2, hpd)):
            at = (h // 2) * LANES
            data = in_half(tile, odds[h], hd)
            column = extra_lane(tile, odds[h], hd)
            grad = d_att[i, :, :, at : at + LANES].reshape(st, LANES).astype(F32)
            prod = grad * att[i, :, :, at : at + LANES].reshape(st, LANES).astype(F32)
            delta = jnp.sum(jnp.where(data, prod, 0.0), axis=1, keepdims=True)
            high, mid, tail = (term.astype(F32) for term in three_parts(-delta))
            extra = jnp.where(column == 0, high, jnp.where(column == 1, mid, tail))
            da[h, rows, :] = jnp.where(
                data, grad, jnp.where((column >= 0) & (column < 3), extra, 0.0)
            ).astype(LOW)

    def open_pair(pair):
        for copy in pair_copies[pair]:
            copy.wait()
        for h in range(2 * pair, min(2 * pair + 2, hpd)):
            turned = jnp.transpose(ka[h])
            if hpd == 1:
                kt[h] = jnp.where(odds[h] == 1, turned[hd:], turned[:hd])
            else:
                kt[h] = turned[odds[h] * hd : (odds[h] + 1) * hd]
        loop(0, sub, lambda i: prepare(i, pair))

    for kind, ref in enumerate((wq, wk, wv)):
        wcat[:, kind * pw : (kind + 1) * pw] = ref[:, pl.ds(base, pw)]
    dk[...] = jnp.zeros_like(dk)
    dv[...] = jnp.zeros_like(dv)
    dqt[...] = jnp.zeros_like(dqt)
    gacc[...] = jnp.zeros_like(gacc)
    all_here(plan, across=True)
    tokens.step0(0)

    def attend(pair, qi, ki):
        rows, keys = pl.ds(pl.multiple_of(qi * st, st), st), pl.ds(pl.multiple_of(ki * st, st), st)
        key_parts, value_parts = [], []
        for h in range(2 * pair, min(2 * pair + 2, hpd)):
            q = qa[h, rows, :]
            d = da[h, rows, :]
            prob = jnp.exp(mm_nt(ka[h, keys, :], q))
            d_score = (prob * mm_nt(va[h, keys, :], d)).astype(LOW)
            value_parts.append(mm(prob.astype(LOW), d))
            key_parts.append(mm(d_score, q))
            dqt[pl.ds(pair * LANES + odds[h] * hd, hd), rows] += mm(kt[h, :, keys], d_score)
        if hpd == 1:
            key_parts.append(jnp.zeros_like(key_parts[0]))
            value_parts.append(jnp.zeros_like(value_parts[0]))
        first = in_half(tile, odds[2 * pair], hd)
        dv[pair, keys, :] += jnp.where(first, value_parts[0], value_parts[1])
        dk[pair, keys, :] += jnp.where(first, key_parts[0], key_parts[1])

    def gather_pair(pair, i):
        rows = rows16(i * st, st)
        at = pair * LANES
        dqt_block = dqt[at : at + LANES, pl.ds(pl.multiple_of(i * st, st), st)]
        dq = jnp.transpose(dqt_block)
        terms = (dq * (hd**-0.5), dk[pair, rows, :], dv[pair, rows, :])
        for kind, term in enumerate(terms):
            dall[rows, kind * pw + at : kind * pw + at + LANES] = term.astype(LOW)
        block = xs[rows, :]
        turned = (dqt_block * (hd**-0.5), jnp.transpose(terms[1]), jnp.transpose(terms[2]))
        for kind, term in enumerate(turned):
            gacc[kind * LANES : (kind + 1) * LANES, :] += mm(term.astype(LOW), block)
        for kind, row in ((0, 0), (2, 1)):
            bsum[row * 8 : row * 8 + 8, :] += fold_rows(terms[kind].astype(LOW).astype(F32))

    lanes = gb.shape[-1]

    def put_pair(pair, ref):
        if plan.piece > 3 * width or lanes > LANES:
            ref[...] = jnp.zeros_like(ref)
        at = base if hpd == 1 else pl.multiple_of(group * LANES, LANES)
        for kind in range(3):
            ref[0, kind * width : (kind + 1) * width, pl.ds(at, LANES)] = jnp.transpose(
                gacc[kind * LANES : (kind + 1) * LANES, :]
            ).astype(LOW)

    def put_vectors(ref, low):
        block = small[...].astype(LOW)
        for part in range(width // lanes):
            ref[0, low + 16 * part : low + 16 * part + 16, :] = block[
                :, part * lanes : (part + 1) * lanes
            ]

    x_copy.wait()

    bsum[...] = jnp.zeros_like(bsum)

    def put_bias(pair):
        at = base if hpd == 1 else pl.multiple_of(group * LANES, LANES)
        for row in range(2):
            bias_mine[2 * pair + row : 2 * pair + row + 1, pl.ds(at, LANES)] = jnp.sum(
                bsum[row * 8 : row * 8 + 8, :], axis=0, keepdims=True
            )
        bsum[...] = jnp.zeros_like(bsum)

    bias_mine[...] = jnp.zeros_like(bias_mine)
    for pair in range(pairs - 1):
        open_pair(pair)

        def square(t):
            tokens.at(pair * sub * sub + t + 1, count)
            attend(pair, t // sub, lax.rem(t, sub))

        loop(0, sub * sub, square)
        loop(0, sub, lambda i: gather_pair(pair, i))
        put_bias(pair)
        if pair == 0:
            put_pair(pair, ga0)
            put_vectors(ga0, 3 * width)
            opening.step0(0)
        gacc[...] = jnp.zeros_like(gacc)

    open_pair(last)
    before = last * sub * sub
    share = nv // groups
    mine_rows = share * sr

    def device_of(g):
        return b - core + g % 2, v - lax.rem(v, plan.cpw) + g // 2

    def part_copy(i, g):
        return remote(
            part.at[i, g * mine_rows : (g + 1) * mine_rows, :], mate.at[i, group],
            p_send.at[i, g], p_recv.at[i, group], device_of(g),
        )

    def send_parts(i):
        rows = rows16(i * st, st)
        total = mm_nt(dall[rows, :], wcat[...])
        part[i] = total.astype(LOW)
        own[i % 2] = total
        for g in range(groups):

            @pl.when(g != group)
            def _():
                part_copy(i, g).start()

    def final_copy(i, n):
        d = group * share + n
        return remote(
            final.at[i, n], dx.at[slot, i], send.at[i, n], recv.at[slot, i], (owner, d)
        )

    def is_own(n):
        return mine & (group * share + n == v)

    def own_copy(i, n):
        return pltpu.make_async_copy(final.at[i, n], dx.at[slot, i], local_sem.at[i])

    def send_final(i):
        total = own[i % 2, rows16(group * mine_rows, mine_rows), :]
        for g in range(groups):

            @pl.when(g != group)
            def _():
                arrived(mate.at[i, g], p_recv.at[i, g])

            @pl.when(g == group)
            def _():
                mate[i, g] = jnp.zeros((mine_rows, width), LOW)

        for g in range(groups):
            total = total + mate[i, g].astype(F32)
        final[i] = total.astype(LOW).reshape(share, sr, width)
        for n in range(share):

            @pl.when(is_own(n))
            def _():
                own_copy(i, n).start()

            @pl.when(jnp.logical_not(is_own(n)))
            def _():
                final_copy(i, n).start()

    def shrink(i):
        start = i * (2 * sub - i)

        def angle(t):
            done = start + t
            tokens.at(before + done + 1, count)
            if last > 0:
                for due, step in (
                    (1, opening.step1), (7, opening.step2), (11, opening.step3),
                    (16, opening.step4), (21, opening.step5),
                ):

                    @pl.when(done == due)
                    def _():
                        step(0)

            @pl.when((t == 1) & (i > 0))
            def _():
                send_final(i - 1)

            n = sub - i
            attend(
                last, jnp.where(t < n, i, i + 1 + t - n), jnp.where(t < n, i + t, i)
            )

        loop(0, 2 * (sub - i) - 1, angle)
        gather_pair(last, i)

        @pl.when(i == sub - 1)
        def _():
            put_pair(last, gb)
            if last == 0:
                put_vectors(gb, 3 * width)
            tail.step0(0)

        send_parts(i)

        @pl.when(i == sub - 1)
        def _():
            tail.step1(0)
            if sub > 1:
                send_final(sub - 2)

    loop(0, sub, shrink)
    tiles = before + sub * sub
    loop(tiles + 1, max(tiles + 1, tokens.end(count)), lambda t: tokens.at(t, count))

    put_bias(last)
    core_vec = remote(bias_mine, vec1, vs.at[0], vs.at[1], core_mate)
    core_vec.start()
    send_final(sub - 1)
    arrived(vec1, vs.at[1])
    core_vec.wait_send()
    bias_mine[...] = bias_mine[...] + vec1[...]

    def vec_spread(o):
        return remote(
            bias_mine, vec2.at[tail.me], vs2.at[0, o], vs2.at[1, tail.me],
            tail.device(tail.peer(o)),
        )

    loop(1, 2 * nv, lambda o: vec_spread(o).start())
    vec2[tail.me] = bias_mine[...]
    first_copy.wait()

    def finish(i):
        for n in range(share):

            @pl.when(is_own(n))
            def _():
                own_copy(i, n).wait()

        for w in range(nw):
            self_sent = mine & (slot == w) & (v // share == group)

            @pl.when(jnp.logical_not(self_sent))
            def _():
                arrived(dx.at[w, i], recv.at[w, i])

        gi[:, i] = (firsts[:, i] + dx[:, i].astype(F32)).astype(LOW)

    if last > 0:
        opening.step6(0)
    tail.step2(0)
    if last > 0:
        opening.step7(0)
    loop(0, sub - 1, finish)

    def vec_take(o):
        j = tail.peer(o)
        arrived(vec2.at[j], vs2.at[1, j])

    loop(1, 2 * nv, vec_take)
    total = vec2[0]
    for j in range(1, 2 * nv):
        total = total + vec2[j]
    vectors[...] = total
    loop(sub - 1, sub, finish)
    tail.step3(0)
    if last > 0:
        opening.step8(0)

    def close(i):
        for n in range(share):

            @pl.when(jnp.logical_not(is_own(n)))
            def _():
                final_copy(i, n).wait_send()

        for g in range(groups):

            @pl.when(g != group)
            def _():
                part_copy(i, g).wait_send()

    loop(0, sub, close)
    loop(1, 2 * nv, lambda o: vec_spread(o).wait_send())
    tail.step4(0)


def output_kernel(
    plan, ff, sums, first_sums, last_sums, vectors,
    gq, gk, gv, go, gu, gd, bq, bv, bo, g1, s1, bu, bd, g2, s2,
    block_in, first_in, last_in, block_out, wide_out, load, store,
):
    width = plan.width
    blocks = ff // width
    lanes = last_in.shape[-1]
    total = 2 * blocks + 1

    def block_loads(n):
        at = (n % 3) * width
        return [
            pltpu.make_async_copy(
                sums.at[2 * (n // 3) + side, at : at + width, :],
                block_in.at[n, :, side * (width // 2) : (side + 1) * (width // 2)],
                load.at[2 * n + side],
            )
            for side in range(2)
        ]

    def block_store(n):
        if n == 2 * blocks:
            dst = go
        elif n % 2:
            dst = gd.at[n // 2 * width : (n // 2 + 1) * width, :]
        else:
            dst = gu.at[:, n // 2 * width : (n // 2 + 1) * width]
        return pltpu.make_async_copy(block_out.at[n], dst, store.at[n])

    parts = [(first_sums, first_in), (last_sums, last_in)][2 - min(plan.pairs, 2) :]
    part_loads = [
        pltpu.make_async_copy(src, dst, load.at[2 * total + n]) for n, (src, dst) in enumerate(parts)
    ]
    wide_stores = [
        pltpu.make_async_copy(wide_out.at[n], dst, store.at[total + n])
        for n, dst in enumerate((gq, gk, gv))
    ]
    for n in range(total):
        for copy in block_loads(n):
            copy.start()
    for copy in part_loads:
        copy.start()
    for n in range(total):
        for copy in block_loads(n):
            copy.wait()
        block_out[n] = block_in[n].astype(F32)
        block_store(n).start()
    for copy in part_loads:
        copy.wait()
    groups = lanes // LANES
    for kind in range(3):
        for pair, (_, ref) in enumerate(parts):
            for group in range(groups):
                at = (group * plan.pairs + pair) * LANES
                wide_out[kind, :, at : at + LANES] = ref[
                    0, kind * width : (kind + 1) * width, group * LANES : (group + 1) * LANES
                ].astype(F32)
        wide_stores[kind].start()
    low = 3 * width
    ref = parts[0][1]
    rows = jnp.concatenate(
        [ref[0, low + 16 * n : low + 16 * n + 16, :] for n in range(width // lanes)], axis=1
    ).astype(F32)
    for n, ref in enumerate((g2, s2, bd, g1, s1, bo)):
        ref[...] = rows[n]
    for f in range(blocks):
        bu[f * width : (f + 1) * width] = rows[6 + f]
    for row, ref in enumerate((bq, bv)):
        for pair in range(plan.pairs):
            for group in range(groups):
                at = (group * plan.pairs + pair) * LANES
                ref[at : at + LANES] = vectors[2 * pair + row, group * LANES : (group + 1) * LANES]
    for n in range(total):
        block_store(n).wait()
    for copy in wide_stores:
        copy.wait()


def params(number):
    return pltpu.CompilerParams(
        vmem_limit_bytes=VMEM_BYTES, collective_id=number, has_side_effects=True
    )


def sum_scratch(plan, number, lanes, piece):
    nh = plan.nv // 2
    return [
        pltpu.VMEM((number, piece // 2, lanes), LOW),
        pltpu.VMEM((number, piece // 2, lanes), LOW),
        pltpu.VMEM((number, piece // 4, lanes), LOW),
        pltpu.VMEM((number, piece // 8, lanes), LOW),
        pltpu.VMEM((number, nh, piece // 8 // nh, lanes), LOW),
        pltpu.VMEM((number, piece // 8 // nh, lanes), LOW),
    ]


def short_scratch(plan, rows, lanes):
    peers = 2 * plan.nv
    return [
        pltpu.VMEM((1, rows // 2, lanes), LOW),
        pltpu.VMEM((1, rows // 2, lanes), LOW),
        pltpu.VMEM((1, peers, rows // 2 // peers, lanes), LOW),
        pltpu.VMEM((1, rows // 2 // peers, lanes), LOW),
    ]


def sum_sems(number, steps, peers):
    return [DMA((2, steps, number)), DMA((2, 2, number, peers))]


def body(
    plan,
    inputs, w_query, w_key, w_value, w_out, b_query, b_value, b_out, gain_one, shift_one,
    w_up, b_up, w_down, b_down, gain_two, shift_two, cotangent, valid_mask,
):
    nv, nw, width = plan.nv, plan.nw, plan.width
    slots, hpd, hd, pw, groups = plan.slots, plan.hpd, plan.hd, plan.pw, plan.groups
    sub, sr, st, pairs = plan.sub, plan.sr, plan.st, plan.pairs
    ff = w_up.shape[1]
    rows, cr = plan.rows, nw * sr
    piece = plan.piece
    shape = jax.ShapeDtypeStruct
    ANY = pl.BlockSpec(memory_space=pl.ANY)
    count = (2 * ff // width + 1) // 3 * 2

    heads = shape((hpd, slots, LANES), LOW)
    blocked = (nw, sub, sr, width)
    mask = valid_mask.reshape(nv, sub, sr).transpose(1, 0, 2).reshape(slots // LANES, LANES)
    qa, ka, va, xw, att, out, d_first, d_att, ga, small = pl.pallas_call(
        functools.partial(forward_kernel, plan, ff),
        out_shape=(
            heads,
            heads,
            heads,
            shape((sub, nv, sr, width), LOW),
            shape((sub, nv, sr, pw), LOW),
            shape(blocked, LOW),
            shape(blocked, F32),
            shape((sub, nv, sr, pw), LOW),
            shape((count, piece, width // 2), LOW),
            shape((16, width), F32),
        ),
        in_specs=[VM] * 7 + [ANY, ANY] + [VM] * 3 + [ANY, VM, ANY] + [VM] * 3,
        out_specs=(ANY,) * 7 + (VM, ANY, VM),
        scratch_shapes=[
            pltpu.VMEM((hpd, slots, LANES), LOW),
            pltpu.VMEM((hpd, slots, LANES), LOW),
            pltpu.VMEM((hpd, slots, LANES), LOW),
            pltpu.VMEM((sub, nv, sr, width), LOW),
            pltpu.VMEM((sub, nv, sr, pw), LOW),
            pltpu.VMEM(blocked, F32),
            pltpu.VMEM(blocked, LOW),
            pltpu.VMEM((width, width), LOW),
            pltpu.VMEM((width, ff), LOW),
            pltpu.VMEM((ff, width), LOW),
            pltpu.VMEM((width, max(3 * hpd * LANES, 2 * width)), LOW),
            pltpu.VMEM((slots, LANES), LOW),
            pltpu.VMEM((8, width), F32),
            pltpu.VMEM((hpd, max((sub - 1) * st, ff // LANES // hpd * cr), LANES), F32),
            pltpu.VMEM((nw, groups, sub, sr, pw), LOW),
            pltpu.VMEM((rows, width), LOW),
            pltpu.VMEM((rows, width), LOW),
            pltpu.VMEM((rows, ff), LOW),
            pltpu.VMEM((rows, ff), LOW),
            pltpu.VMEM((rows, width), LOW),
            pltpu.VMEM((rows, width), LOW),
            DMA((sub, nv)),
            DMA((sub, nv)),
            DMA((sub, nv)),
            DMA((sub, nv)),
            DMA((nw, groups, sub)),
            DMA((sub,)),
            DMA((sub, nw, groups)),
            DMA((sub, nv)),
            DMA((sub,)),
            DMA,
            DMA((2, 2)),
            DMA((4,)),
            DMA((7,)),
        ],
        compiler_params=params(1),
        name="forward_and_tokens",
    )(
        inputs.reshape(blocked), w_query, w_key, w_value, b_query, b_value, mask,
        cotangent.reshape(blocked), w_out, b_out, gain_one, shift_one,
        w_up, b_up, w_down, b_down, gain_two, shift_two,
    )

    share = nv // groups
    lanes = width // pairs
    unit = 16 * 4 * nv
    more = -(-(3 * width + 16 * width // lanes) // unit) * unit
    first_rows = more if pairs > 1 else unit
    last_rows = piece if pairs > 1 else more
    gi, sums, first_sums, last_sums, vectors = pl.pallas_call(
        functools.partial(backward_kernel, plan, count),
        out_shape=(
            shape(blocked, LOW),
            shape((count, piece, width // 2), LOW),
            shape((1, first_rows, lanes), LOW),
            shape((1, last_rows, lanes), LOW),
            shape((8, lanes), F32),
        ),
        in_specs=[ANY] * 3 + [VM] * 2 + [ANY] + [VM] * 3 + [ANY, ANY, VM],
        out_specs=(VM, ANY, ANY, ANY, VM),
        scratch_shapes=[
            pltpu.VMEM((hpd, slots, LANES), LOW),
            pltpu.VMEM((hpd, slots, LANES), LOW),
            pltpu.VMEM((hpd, slots, LANES), LOW),
            pltpu.VMEM((hpd, slots, LANES), LOW),
            pltpu.VMEM((hpd, hd, slots), LOW),
            pltpu.VMEM((pw, slots), F32),
            pltpu.VMEM((pairs, slots, LANES), F32),
            pltpu.VMEM((pairs, slots, LANES), F32),
            pltpu.VMEM((slots, 3 * pw), LOW),
            pltpu.VMEM((width, 3 * pw), LOW),
            pltpu.VMEM((sub, st, width), LOW),
            pltpu.VMEM((sub, groups, share * sr, width), LOW),
            pltpu.VMEM((2, st, width), F32),
            pltpu.VMEM((sub, share, sr, width), LOW),
            pltpu.VMEM((nw, sub, sr, width), LOW),
            pltpu.VMEM((3 * LANES, width), F32),
            pltpu.VMEM((1, last_rows, lanes), LOW),
            pltpu.VMEM((16, LANES), F32),
        ]
        + sum_scratch(plan, count, width // 2, piece)
        + short_scratch(plan, last_rows, lanes)
        + [pltpu.VMEM((1, first_rows, lanes), LOW)]
        + sum_scratch(plan, 1, lanes, first_rows)
        + [
            pltpu.VMEM((8, lanes), F32),
            pltpu.VMEM((8, lanes), F32),
            pltpu.VMEM((2 * nv, 8, lanes), F32),
            pltpu.VMEM((slots, width), LOW),
            pltpu.VMEM(blocked, F32),
            DMA((sub, groups)),
            DMA((sub, groups)),
            DMA((sub, share)),
            DMA((nw, sub)),
            DMA((sub,)),
        ]
        + sum_sems(count, 8, nv // 2)
        + sum_sems(1, 3, 2 * nv)
        + sum_sems(1, 8, nv // 2)
        + [DMA((2,)), DMA((2, 2 * nv)), DMA((2 + 3 * pairs,))],
        compiler_params=params(2),
        name="attention_backward",
    )(
        qa, ka, va, att, d_att, xw.reshape(slots, width), w_query, w_key, w_value, d_first,
        ga, small,
    )

    square = shape((width, width), F32)
    one = shape((width,), F32)
    total = 2 * ff // width + 1
    gq, gk, gv, go, gu, gd, bq, bv, bo, g1, s1, bu, bd, g2, s2 = pl.pallas_call(
        functools.partial(output_kernel, plan, ff),
        out_shape=(square,) * 4
        + (shape((width, ff), F32), shape((ff, width), F32))
        + (one,) * 5
        + (shape((ff,), F32),)
        + (one,) * 3,
        in_specs=[ANY] * 3 + [VM],
        out_specs=(ANY,) * 6 + (VM,) * 9,
        scratch_shapes=[
            pltpu.VMEM((total, width, width), LOW),
            pltpu.VMEM((1, first_rows, lanes), LOW),
            pltpu.VMEM((1, last_rows, lanes), LOW),
            pltpu.VMEM((total, width, width), F32),
            pltpu.VMEM((3, width, width), F32),
            DMA((2 * total + 2,)),
            DMA((total + 3,)),
        ],
        compiler_params=pltpu.CompilerParams(vmem_limit_bytes=VMEM_BYTES),
        name="outputs",
    )(sums, first_sums, last_sums, vectors)
    return (
        out.reshape(inputs.shape), gi.reshape(inputs.shape),
        gq, gk, gv, go, bq, bv, bo, g1, s1, gu, bu, gd, bd, g2, s2,
    )


def solution(mesh):
    data = P("batch", "var", None)

    def run(*args):
        plan = Plan(mesh, args[0].shape)
        return jax.shard_map(
            functools.partial(body, plan),
            mesh=mesh,
            in_specs=(data,) + (P(),) * 15 + (data, P()),
            out_specs=(data, data) + (P(),) * 15,
            check_vma=False,
        )(*args)

    return run
```

```python
import functools

import jax
import jax.numpy as jnp
from jax import lax
from jax.experimental import pallas as pl
from jax.experimental.pallas import tpu as pltpu
from jax.sharding import PartitionSpec as P

HEADS = 8
LANES = 128
LOW = jnp.bfloat16
F32 = jnp.float32
MESH = pl.DeviceIdType.MESH
DMA = pltpu.SemaphoreType.DMA
VM = pl.BlockSpec(memory_space=pltpu.VMEM)
VMEM_BYTES = 62 << 20


def mm(left, right):
    return jnp.dot(left, right, preferred_element_type=F32)


def mm_nt(left, right):
    return lax.dot_general(left, right, (((1,), (1,)), ((), ())), preferred_element_type=F32)


def mm_tn(left, right):
    return lax.dot_general(left, right, (((0,), (0,)), ((), ())), preferred_element_type=F32)


def lane_of(shape):
    return lax.broadcasted_iota(jnp.int32, shape, len(shape) - 1)


def in_half(lane, odd, hd):
    return (lane >= hd) == (odd == 1)


def extra_lane(lane, odd, hd):
    return jnp.where(in_half(lane, odd, hd), -1, lane - hd * (1 - odd))


def vec(ref):
    return ref[...].reshape(1, -1).astype(F32)


def three_parts(value):
    high = value.astype(LOW)
    rest = value - high.astype(F32)
    mid = rest.astype(LOW)
    tail = (rest - mid.astype(F32)).astype(LOW)
    return high, mid, tail


class Plan:
    def __init__(self, mesh, inputs_shape):
        windows, slots, width = inputs_shape
        self.nv = mesh.shape["var"]
        self.nb = mesh.shape["batch"]
        self.nw = windows // self.nb
        self.local = slots // self.nv
        self.slots = slots
        self.width = width
        self.hd = width // HEADS
        self.cpw = self.nv // (2 * self.nw)
        self.groups = 2 * self.cpw
        self.hpd = HEADS // self.groups
        self.pairs = max(self.hpd // 2, 1)
        self.pw = self.pairs * LANES
        self.rows = self.nw * self.local
        self.sub = next(
            n for n in (5, 4, 2, 1)
            if self.local % (16 * n) == 0 and slots % (LANES * n) == 0
        )
        self.sr = self.local // self.sub
        self.st = self.nv * self.sr
        unit = 16 * self.nv * self.nb
        self.piece = -(-3 * width // unit) * unit

    def here(self):
        b = lax.axis_index("batch")
        v = lax.axis_index("var")
        core = lax.rem(b, 2)
        window = v // self.cpw
        parity = window // self.nw
        slot = lax.rem(window, self.nw)
        group = lax.rem(v, self.cpw) * 2 + core
        return b, v, core, parity, slot, group

    def odd(self, h, group):
        return lax.rem(group, 2) if self.hpd == 1 else h % 2

    def base(self, group):
        if self.hpd == 1:
            return pl.multiple_of((group // 2) * LANES, LANES)
        return pl.multiple_of(group * self.pw, LANES)


def loop(low, high, step):
    def run(index, carry):
        step(index)
        return carry

    lax.fori_loop(low, high, run, 0)


def greet(plan, b, v, core, across=False):
    barrier = pltpu.get_barrier_semaphore()
    partner = b + 1 - 2 * core

    def greet_same(o):
        pl.semaphore_signal(
            barrier, inc=1, device_id=(b, lax.rem(v + o, plan.nv)), device_id_type=MESH
        )

    def greet_other(o):
        pl.semaphore_signal(
            barrier, inc=1, device_id=(partner, lax.rem(v + o, plan.nv)), device_id_type=MESH
        )

    loop(1, plan.nv, greet_same)
    loop(0, plan.nv, greet_other)
    def greet_across(o):
        pl.semaphore_signal(
            barrier, inc=1, device_id=(b + 2 - 4 * (b // 2), lax.rem(v + o, plan.nv)),
            device_id_type=MESH,
        )

    if across:
        loop(0, plan.nv, greet_across)


def all_here(plan, across=False):
    count = (3 if across else 2) * plan.nv - 1
    pl.semaphore_wait(pltpu.get_barrier_semaphore(), count)


def arrived(ref, sem):
    pltpu.make_async_copy(ref, ref, sem).wait()


def gelu_and_slope(pre):
    size = jnp.abs(pre)
    bell = jnp.exp(pre * pre * -0.5)
    t = 1.0 / (1.0 + 0.2316418882663604 * size)
    poly = t * (
        0.127414796
        + t * (-0.142248368 + t * (0.7107068705 + t * (-0.7265760135 + t * 0.5307027145)))
    )
    below = poly * bell
    phi = jnp.where(pre < 0, below, 1.0 - below)
    return pre * phi, phi + pre * bell * 0.3989422804014327


def fold_rows(value):
    rows, width = value.shape
    return jnp.sum(value.reshape(rows // 8, 8, width), axis=0)


def sum_rows(value):
    return jnp.sum(fold_rows(value), axis=0, keepdims=True)


def norm_parts(rows):
    center = rows - jnp.mean(rows, axis=-1, keepdims=True)
    spread = jnp.mean(center * center, axis=-1, keepdims=True)
    inverse = lax.rsqrt(spread + 1e-05)
    return center * inverse, inverse


def norm_back(unit, inverse, grad):
    return inverse * (
        grad
        - jnp.mean(grad, axis=-1, keepdims=True)
        - unit * jnp.mean(grad * unit, axis=-1, keepdims=True)
    )


def remote(src, dst, send_sem, recv_sem, device):
    return pltpu.make_async_remote_copy(
        src_ref=src, dst_ref=dst, send_sem=send_sem, recv_sem=recv_sem,
        device_id=device, device_id_type=MESH,
    )


def rows16(start, size):
    return pl.ds(pl.multiple_of(start, 16), size)


TOP = 8


def forward_kernel(
    plan, ff, x, wq, wk, wv, bq, bv, mask, cot, wo, bo, g1, s1, wu, bu, wd, bd, g2, s2,
    qa_out, ka_out, va_out, xw_out, att_out, out_out, first_out, d_att, pieces, small,
    qa, ka, va, xw, att, d_first, cot_s, wo_s, wu_s, wd_s,
    waug, kaug, bias, acc, got, att_s, mid_s, act_s, pre_s, branch_s, dout_s,
    send, recv, pass_on, a_send, a_recv, a_local, d_send, d_recv, d_local, local_sem, stage_sem,
    load, store,
):
    nv, nw, hpd, hd, pw = plan.nv, plan.nw, plan.hpd, plan.hd, plan.pw
    sub, sr, st, width, groups = plan.sub, plan.sr, plan.st, plan.width, plan.groups
    b, v, core, parity, slot, group = plan.here()
    mine = parity == core
    partner = b + 1 - 2 * core
    owner = b - core + parity
    odds = [plan.odd(h, group) for h in range(hpd)]
    loads = [
        pltpu.make_async_copy(src, dst, load.at[n])
        for n, (src, dst) in enumerate(((wo, wo_s), (wu, wu_s), (wd, wd_s), (cot, cot_s)))
    ]
    stores = [
        pltpu.make_async_copy(src, dst, store.at[n])
        for n, (src, dst) in enumerate((
            (xw, xw_out), (ka, ka_out), (va, va_out), (qa, qa_out), (att, att_out),
            (d_first, first_out), (cot_s, out_out),
        ))
    ]
    greet(plan, b, v, core)

    def out_copy(i, o):
        d = lax.rem(v + o, nv)
        return remote(
            x.at[lax.rem(d // plan.cpw, nw), i], xw.at[i, v], send.at[i, o], recv.at[i, v], (b, d)
        )

    def wanted(o):
        return (lax.rem(v + o, nv) // plan.cpw) // nw == core

    def start_out(n):
        @pl.when(wanted(lax.rem(n, nv)) & (lax.rem(n, nv) > 0))
        def _():
            out_copy(n // nv, lax.rem(n, nv)).start()

    def end_out(n):
        @pl.when(wanted(lax.rem(n, nv)) & (lax.rem(n, nv) > 0))
        def _():
            out_copy(n // nv, lax.rem(n, nv)).wait_send()

    def own_x():
        return pltpu.make_async_copy(x.at[slot], xw.at[:, v], local_sem)

    def forward_copy(i, s):
        at = xw.at[i, s]
        return remote(at, at, pass_on.at[i, s], recv.at[i, s], (partner, v))

    lane = lane_of((width, LANES))
    base = plan.base(group)
    for kind, ref in enumerate((wq, wk, wv)):
        for h in range(hpd):
            both = ref[:, pl.ds(base + (h // 2) * LANES, LANES)].astype(F32)
            at = (kind * hpd + h) * LANES
            waug[:, at : at + LANES] = jnp.where(in_half(lane, odds[h], hd), both, 0.0).astype(LOW)
    bias[0:1, :] = vec(bq)
    bias[1:2, :] = vec(bv)

    all_here(plan)
    loop(0, min(2, sub) * nv, start_out)
    for copy in loads:
        copy.start()

    @pl.when(mine)
    def _():
        own_x().start()

    square = lane_of((LANES, LANES))
    diag = square == lax.broadcasted_iota(jnp.int32, (LANES, LANES), 0)
    place = lax.rem(square, hd)
    ones = jnp.where((place > 0) & (place < 4), 1.0, 0.0)
    for at in range(plan.slots // LANES):
        row = jnp.where(mask[at : at + 1, :] > 0, 0.0, -1e30)
        column = jnp.sum(jnp.where(diag, row, 0.0), axis=1, keepdims=True)
        kaug[at * LANES : (at + 1) * LANES, :] = jnp.where(place == 0, column, ones).astype(LOW)

    tile = lane_of((st, LANES))
    data = [in_half(tile, odd, hd) for odd in odds]
    column = [extra_lane(tile, odd, hd) for odd in odds]

    def extra_column(value, h, at):
        if hpd == 1:
            return jnp.where(
                odds[h] == 1, value[:, at : at + 1], value[:, hd + at : hd + at + 1]
            )
        at += hd * (1 - odds[h])
        return value[:, at : at + 1]

    small[...] = jnp.zeros_like(small)

    def bias_of(kind, h):
        return bias[kind : kind + 1, pl.ds(base + (h // 2) * LANES, LANES)]

    def project(i):
        rows = rows16(i * st, st)
        extra = kaug[rows, :].astype(F32)
        both = mm(xw[i].reshape(st, width), waug[:, 0 : 3 * hpd * LANES])
        for h in range(hpd):
            q = both[:, h * LANES : (h + 1) * LANES] + bias_of(0, h)
            q = q.astype(LOW).astype(F32) * (hd**-0.5)
            qa[h, rows, :] = jnp.where(data[h], q, jnp.where(column[h] == 0, 1.0, 0.0)).astype(LOW)
            k = both[:, (hpd + h) * LANES : (hpd + h + 1) * LANES]
            ka[h, rows, :] = jnp.where(data[h], k, extra).astype(LOW)
            val = both[:, (2 * hpd + h) * LANES : (2 * hpd + h + 1) * LANES] + bias_of(1, h)
            va[h, rows, :] = jnp.where(
                data[h], val, jnp.where((column[h] >= 0) & (column[h] < 3), 1.0, 0.0)
            ).astype(LOW)


    def attend(i, side, hr, low, high, merge):
        rows = rows16(i * st + side * hr, hr)
        keys = slice(low * st, high * st)
        score = mm_nt(qa[0, rows, :], ka[0, keys, :])
        states = []
        for h in range(hpd):
            if h + 1 < hpd:
                ahead = mm_nt(qa[h + 1, rows, :], ka[h + 1, keys, :])
            top = jnp.max(score, axis=1, keepdims=True)
            if merge:
                state = acc[h, rows, :]
                old = extra_column(state, h, TOP)
                top = jnp.maximum(old, top)
            expo = jnp.exp(score - top)
            mixed = mm(expo.astype(LOW), va[h, keys, :])
            if merge:
                mixed = state * jnp.exp(old - top) + mixed
            states.append((top, mixed))
            score = ahead if h + 1 < hpd else None
        return states

    def height(low, high):
        return st if high - low <= 3 else st // 2

    def hold(i, low, high):
        hr = height(low, high)
        def part(side):
            rows = rows16(i * st + side * hr, hr)
            for h, (top, mixed) in enumerate(attend(i, side, hr, low, high, False)):
                acc[h, rows, :] = jnp.where(column[h][:hr] == TOP, top, mixed)

        loop(0, st // hr, part)

    def att_copy(i, o):
        d = lax.rem(v + o, nv)
        return remote(
            att.at[i, d], got.at[slot, group, i], a_send.at[i, o], a_recv.at[slot, group, i],
            (owner, d),
        )

    def att_own(i):
        return pltpu.make_async_copy(att.at[i, v], got.at[slot, group, i], a_local.at[i])

    def settle(i, low, high, merge):
        hr = height(low, high)
        nh = nv * hr // st

        def part(side):
            rows = rows16(i * st + side * hr, hr)
            done = []
            for h, (top, mixed) in enumerate(attend(i, side, hr, low, high, merge)):
                total = extra_column(mixed, h, 0)
                done.append(mixed / total)
                high_part, mid, tail = three_parts(-(top + jnp.log(total)))
                at = column[h][:hr]
                qa[h, rows, :] = jnp.where(
                    at == 1,
                    high_part,
                    jnp.where(at == 2, mid, jnp.where(at == 3, tail, qa[h, rows, :])),
                )
            owners = pl.ds(side * nh, nh)
            for pair in range(plan.pairs):
                other = 0.0 if hpd == 1 else done[2 * pair + 1]
                att[i, owners, :, pair * LANES : (pair + 1) * LANES] = (
                    jnp.where(data[2 * pair][:hr], done[2 * pair], other)
                    .astype(LOW)
                    .reshape(nh, sr, LANES)
                )

        loop(0, st // hr, part)
        loop(1, nv, lambda o: att_copy(i, o).start())

        @pl.when(mine)
        def _():
            att_own(i).start()

        @pl.when(jnp.logical_not(mine))
        def _():
            att_copy(i, 0).start()

    def arrive(i):
        def take(o):
            s = lax.rem(v + o, nv)
            arrived(xw.at[i, s], recv.at[i, s])

            @pl.when(mine)
            def _():
                forward_copy(i, s).start()

        loop(1, nv, take)

        @pl.when(jnp.logical_not(mine))
        def _():
            arrived(xw.at[i, v], recv.at[i, v])

        @pl.when(i + 2 < sub)
        def _():
            loop((i + 2) * nv, (i + 3) * nv, start_out)

        project(i)

    @pl.when(mine)
    def _():
        own_x().wait()
        loop(0, sub, lambda n: forward_copy(n, v).start())

    early = min(2, sub)
    loop(0, early, arrive)
    if early < sub:
        loop(0, early, lambda i: hold(i, 0, early))
    for i in range(early, sub):
        arrive(i)
        if i < sub - 1:
            hold(i, 0, i + 1)
    for copy in stores[:3]:
        copy.start()
    if early < sub:
        settle(sub - 1, 0, sub, False)
        loop(0, early, lambda i: settle(i, early, sub, True))
        for i in range(early, sub - 1):
            settle(i, i + 1, sub, True)
    else:
        loop(0, sub, lambda i: settle(i, 0, sub, False))

    for copy in stores[3:5]:
        copy.start()
    for copy in loads:
        copy.wait()

    step = 512
    cr = nw * sr

    def target(w, g):
        return b - core + g % 2, (core * nw + w) * plan.cpw + g // 2

    def is_self(w, g):
        tb, tv = target(w, g)
        return (tb == b) & (tv == v)

    def grad_copy(i, w, g):
        return remote(
            got.at[w, g, i], d_att.at[i, v], d_send.at[i, w, g], d_recv.at[i, v], target(w, g)
        )

    def grad_own(i, w, g):
        return pltpu.make_async_copy(got.at[w, g, i], d_att.at[i, v], d_local.at[i])

    def slope_at(n):
        return n % hpd, slice(n // hpd * cr, (n // hpd + 1) * cr)

    def keep_slope(f, slope):
        for n in range(step // LANES):
            h, at = slope_at(f // LANES + n)
            acc[h, at, :] = slope[:, n * LANES : (n + 1) * LANES]

    def kept_slope(f):
        places = [slope_at(f // LANES + n) for n in range(step // LANES)]
        return jnp.concatenate([acc[h, at, :] for h, at in places], axis=1)

    def tokens(n):
        i = lax.rem(n + sub - 1, sub)
        for w in range(nw):
            for g in range(groups):
                own = mine & (slot == w) & (group == g)

                @pl.when(own)
                def _():
                    att_own(i).wait()

                @pl.when(jnp.logical_not(own))
                def _():
                    arrived(got.at[w, g, i], a_recv.at[w, g, i])

        rows = rows16(i * cr, cr)
        if hpd == 1:
            parts = [got[:, g, i] + got[:, g + 1, i] for g in range(0, groups, 2)]
        else:
            parts = [got[:, g, i] for g in range(groups)]
        attended = jnp.concatenate([part.reshape(cr, pw) for part in parts], axis=1)
        att_s[rows, :] = attended
        first = x[:, i].reshape(cr, width).astype(F32) + mm(attended, wo_s[...]) + vec(bo)
        unit1, inv1 = norm_parts(first)
        middle = unit1 * vec(g1) + vec(s1)
        mid_low = middle.astype(LOW)
        mid_s[rows, :] = mid_low
        total = middle + vec(bd)

        def before(f):
            return mm(mid_low, wu_s[:, f : f + step]) + bu[f : f + step].reshape(1, -1).astype(F32)

        pre = before(0)
        for f in range(0, ff, step):
            ahead = before(f + step) if f + step < ff else None
            act, slope = gelu_and_slope(pre)
            act_low = act.astype(LOW)
            act_s[rows, f : f + step] = act_low
            keep_slope(f, slope)
            total = total + mm(act_low, wd_s[f : f + step, :])
            pre = ahead
        unit2, inv2 = norm_parts(total)
        result = (unit2 * vec(g2) + vec(s2)).astype(LOW).reshape(nw, sr, width)
        grad = cot_s[:, i].reshape(cr, width).astype(F32)
        cot_s[:, i] = result
        small[0:1, :] += sum_rows(grad * unit2)
        small[1:2, :] += sum_rows(grad)
        d_second = norm_back(unit2, inv2, grad * vec(g2))
        branch = d_second.astype(LOW)
        branch_s[rows, :] = branch
        small[2:3, :] += sum_rows(branch.astype(F32))
        d_middle = d_second

        def back(f):
            return mm_nt(branch, wd_s[f : f + step, :])

        d_act = back(0)
        for f in range(0, ff, step):
            ahead = back(f + step) if f + step < ff else None
            d_pre = (d_act * kept_slope(f)).astype(LOW)
            pre_s[rows, f : f + step] = d_pre
            at = 6 + f // step
            small[at : at + 1, :] += sum_rows(d_pre.astype(F32))
            d_middle = d_middle + mm_nt(d_pre, wu_s[:, f : f + step])
            d_act = ahead
        small[3:4, :] += sum_rows(d_middle * unit1)
        small[4:5, :] += sum_rows(d_middle)
        d_one = norm_back(unit1, inv1, d_middle * vec(g1))
        d_first[:, i] = d_one.reshape(nw, sr, width)
        d_out = d_one.astype(LOW)
        dout_s[rows, :] = d_out
        small[5:6, :] += sum_rows(d_out.astype(F32))
        d_attended = mm_nt(d_out, wo_s[...]).astype(LOW).reshape(nw, sr, width)
        for w in range(nw):
            for g in range(groups):
                at = (g // 2) * LANES if hpd == 1 else g * pw
                got[w, g, i] = d_attended[w, :, at : at + pw]

                @pl.when(is_self(w, g))
                def _():
                    grad_own(i, w, g).start()

                @pl.when(jnp.logical_not(is_self(w, g)))
                def _():
                    grad_copy(i, w, g).start()

    loop(0, sub, tokens)
    for copy in stores[5:]:
        copy.start()

    blocks = 2 * ff // step + 1
    spare = plan.piece - 3 * width

    half = width // 2

    def stage_copies(n):
        at = (n % 3) * width
        return [
            pltpu.make_async_copy(
                waug.at[:, (n % 2) * width + side * half : (n % 2) * width + (side + 1) * half],
                pieces.at[2 * (n // 3) + side, at : at + width, :],
                stage_sem.at[n % 2, side],
            )
            for side in range(2)
        ]

    def put(n, value):
        if n >= 2:
            for copy in stage_copies(n - 2):
                copy.wait()
        waug[:, (n % 2) * width : (n % 2 + 1) * width] = value.astype(LOW)
        for copy in stage_copies(n):
            copy.start()

    for f in range(ff // step):
        put(2 * f, mm_tn(mid_s[...], pre_s[:, f * step : (f + 1) * step]))
        put(2 * f + 1, mm_tn(act_s[:, f * step : (f + 1) * step], branch_s[...]))
    put(blocks - 1, mm_tn(att_s[...], dout_s[...]))
    for n in (blocks - 2, blocks - 1):
        for copy in stage_copies(n):
            copy.wait()
    if spare > 0:
        waug[:, 0:width] = jnp.zeros((width, width), LOW)
        for n in range(pieces.shape[0]):
            for at in range(0, spare, width):
                size = min(width, spare - at)
                pad = pltpu.make_async_copy(
                    waug.at[0:size, 0:half],
                    pieces.at[n, 3 * width + at : 3 * width + at + size, :],
                    stage_sem.at[0, 0],
                )
                pad.start()
                pad.wait()

    def take(n):
        i, s = n // nv, lax.rem(n, nv)

        @pl.when(jnp.logical_not((s == v) & mine))
        def _():
            arrived(d_att.at[i, s], d_recv.at[i, s])

    loop(0, sub * nv, take)

    def finish(i):
        for w in range(nw):
            for g in range(groups):

                @pl.when(is_self(w, g))
                def _():
                    grad_own(i, w, g).wait()

                @pl.when(jnp.logical_not(is_self(w, g)))
                def _():
                    grad_copy(i, w, g).wait_send()

        @pl.when(jnp.logical_not(mine))
        def _():
            att_copy(i, 0).wait_send()

        loop(1, nv, lambda o: att_copy(i, o).wait_send())

        @pl.when(mine)
        def _():
            loop(0, nv, lambda s: forward_copy(i, s).wait_send())

    loop(0, sub, finish)
    loop(0, sub * nv, end_out)
    for copy in stores:
        copy.wait()


class Sums:
    def __init__(
        self, plan, rows, source, sums, box1, half, box2, box3, box4, fin, pair_sems, many_sems
    ):
        self.plan, self.source, self.sums = plan, source, sums
        self.box1, self.half, self.box2, self.box3 = box1, half, box2, box3
        self.box4, self.fin = box4, fin
        self.s, self.m = pair_sems, many_sems
        b, v = lax.axis_index("batch"), lax.axis_index("var")
        self.b, self.v = b, v
        self.core, self.xs, self.lo, self.hi = lax.rem(b, 2), b // 2, lax.rem(v, 2), v // 2
        self.nh = plan.nv // 2
        self.half_rows = rows // 2
        self.quarter, self.eighth = rows // 4, rows // 8
        self.chunk = self.eighth // self.nh

    def mate(self, p, first):
        over_x = (p % 2 == 0) if first else (p % 2 == 1)
        db, dv = self.b + 2 - 4 * self.xs, self.v + 1 - 2 * self.lo
        return jnp.where(over_x, db, self.b), jnp.where(over_x, self.v, dv)

    def coords(self, p):
        even = p % 2 == 0
        return jnp.where(even, self.xs, self.lo), jnp.where(even, self.lo, self.xs)

    def pair(self, p, at, src, dst, device):
        return remote(src, dst, self.s.at[0, at, p], self.s.at[1, at, p], device)

    def core_copy(self, p):
        rows = rows16((1 - self.core) * self.half_rows, self.half_rows)
        device = (self.b + 1 - 2 * self.core, self.v)
        return self.pair(p, 0, self.source(p).at[rows, :], self.box1.at[p], device)

    def own_copy(self, p):
        rows = rows16(self.core * self.half_rows, self.half_rows)
        return pltpu.make_async_copy(
            self.source(p).at[rows, :], self.half.at[p], self.s.at[0, 6, p]
        )

    def first_copy(self, p):
        c1, _ = self.coords(p)
        rows = rows16((1 - c1) * self.quarter, self.quarter)
        return self.pair(p, 1, self.half.at[p, rows, :], self.box2.at[p], self.mate(p, True))

    def second_copy(self, p):
        c1, c2 = self.coords(p)
        rows = rows16(c1 * self.quarter + (1 - c2) * self.eighth, self.eighth)
        return self.pair(p, 2, self.half.at[p, rows, :], self.box3.at[p], self.mate(p, False))

    def peer(self, o):
        return lax.rem(self.hi + o, self.nh)

    def many_copy(self, p, o):
        d = self.peer(o)
        c1, c2 = self.coords(p)
        rows = rows16(c1 * self.quarter + c2 * self.eighth + d * self.chunk, self.chunk)
        return remote(
            self.half.at[p, rows, :], self.box4.at[p, self.hi],
            self.m.at[0, 0, p, o], self.m.at[1, 0, p, self.hi], (self.b, d * 2 + self.lo),
        )

    def region(self, p, start, size):
        return self.sums.at[p, rows16(self.core * self.half_rows + start, size), :]

    def chunk_at(self, p, who):
        c1, c2 = self.coords(p)
        start = c1 * self.quarter + c2 * self.eighth + who * self.chunk
        return self.region(p, start, self.chunk)

    def spread_copy(self, p, o):
        return remote(
            self.fin.at[p], self.chunk_at(p, self.hi),
            self.m.at[0, 1, p, o], self.m.at[1, 1, p, self.hi],
            (self.b, self.peer(o) * 2 + self.lo),
        )

    def keep_copy(self, p):
        return pltpu.make_async_copy(
            self.fin.at[p], self.chunk_at(p, self.hi), self.s.at[0, 7, p]
        )

    def back_second(self, p):
        c1, c2 = self.coords(p)
        at = self.region(p, c1 * self.quarter + c2 * self.eighth, self.eighth)
        return self.pair(p, 3, at, at, self.mate(p, False))

    def back_first(self, p):
        c1, _ = self.coords(p)
        at = self.region(p, c1 * self.quarter, self.quarter)
        return self.pair(p, 4, at, at, self.mate(p, True))

    def back_core(self, p):
        at = self.region(p, 0, self.half_rows)
        return self.pair(p, 5, at, at, (self.b + 1 - 2 * self.core, self.v))

    def came(self, p, at, ref):
        arrived(ref, self.s.at[1, at, p])

    def step0(self, p):
        self.core_copy(p).start()
        self.own_copy(p).start()

    def step1(self, p):
        self.own_copy(p).wait()
        self.came(p, 0, self.box1.at[p])
        self.half[p] = (self.half[p].astype(F32) + self.box1[p].astype(F32)).astype(LOW)
        self.first_copy(p).start()

    def add(self, p, start, size, other):
        rows = rows16(start, size)
        total = self.half[p, rows, :].astype(F32) + other.astype(F32)
        self.half[p, rows, :] = total.astype(LOW)

    def step2(self, p):
        c1, _ = self.coords(p)
        self.came(p, 1, self.box2.at[p])
        self.first_copy(p).wait_send()
        self.add(p, c1 * self.quarter, self.quarter, self.box2[p])
        self.second_copy(p).start()

    def step3(self, p):
        c1, c2 = self.coords(p)
        self.came(p, 2, self.box3.at[p])
        self.second_copy(p).wait_send()
        self.add(p, c1 * self.quarter + c2 * self.eighth, self.eighth, self.box3[p])
        loop(1, self.nh, lambda o: self.many_copy(p, o).start())

    def step4(self, p):
        def take(o):
            s = self.peer(o)
            arrived(self.box4.at[p, s], self.m.at[1, 0, p, s])

        loop(1, self.nh, take)
        c1, c2 = self.coords(p)
        rows = rows16(c1 * self.quarter + c2 * self.eighth + self.hi * self.chunk, self.chunk)
        total = self.half[p, rows, :].astype(F32)
        for o in range(1, self.nh):
            total = total + self.box4[p, self.peer(o)].astype(F32)
        self.fin[p] = total.astype(LOW)
        self.keep_copy(p).start()
        loop(1, self.nh, lambda o: self.spread_copy(p, o).start())

    def step5(self, p):
        def take(o):
            s = self.peer(o)
            arrived(self.chunk_at(p, s), self.m.at[1, 1, p, s])

        loop(1, self.nh, take)
        self.keep_copy(p).wait()
        self.back_second(p).start()

    def step6(self, p):
        c1, c2 = self.coords(p)
        self.came(p, 3, self.region(p, c1 * self.quarter + (1 - c2) * self.eighth, self.eighth))
        self.back_first(p).start()

    def step7(self, p):
        c1, _ = self.coords(p)
        self.came(p, 4, self.region(p, (1 - c1) * self.quarter, self.quarter))
        self.back_core(p).start()

    def step8(self, p):
        rows = rows16((1 - self.core) * self.half_rows, self.half_rows)
        self.came(p, 5, self.sums.at[p, rows, :])
        self.core_copy(p).wait_send()
        loop(1, self.nh, lambda o: self.many_copy(p, o).wait_send())
        loop(1, self.nh, lambda o: self.spread_copy(p, o).wait_send())
        self.back_second(p).wait_send()
        self.back_first(p).wait_send()
        self.back_core(p).wait_send()

    DUE = (0, 4, 10, 16, 22, 30, 34, 42, 46)
    LAG = 2

    def at(self, tile, count):
        steps = (
            self.step0, self.step1, self.step2, self.step3, self.step4,
            self.step5, self.step6, self.step7, self.step8,
        )
        @pl.when((tile & 1) == 0)
        def _():
            for due, step in reversed(tuple(zip(self.DUE, steps))):
                piece = (tile - due) >> 1

                @pl.when((piece >= 0) & (piece < count))
                def _():
                    step(piece)

    def end(self, count):
        return self.DUE[-1] + self.LAG * (count - 1) + 1


class ShortSums:
    def __init__(self, plan, source, sums, box1, half, box2, fin, pair_sems, many_sems):
        self.plan, self.source, self.sums = plan, source, sums
        self.box1, self.half, self.box2, self.fin = box1, half, box2, fin
        self.s, self.m = pair_sems, many_sems
        b, v = lax.axis_index("batch"), lax.axis_index("var")
        self.b, self.v, self.core = b, v, lax.rem(b, 2)
        self.peers = 2 * plan.nv
        self.me = (b // 2) * plan.nv + v
        self.half_rows = source.shape[1] // 2
        self.chunk = self.half_rows // self.peers

    def peer(self, o):
        return lax.rem(self.me + o, self.peers)

    def device(self, j):
        return (j // self.plan.nv) * 2 + self.core, lax.rem(j, self.plan.nv)

    def core_copy(self, p):
        rows = rows16((1 - self.core) * self.half_rows, self.half_rows)
        return remote(
            self.source.at[p, rows, :], self.box1.at[p], self.s.at[0, 0, p], self.s.at[1, 0, p],
            (self.b + 1 - 2 * self.core, self.v),
        )

    def many_copy(self, p, o):
        j = self.peer(o)
        return remote(
            self.half.at[p, rows16(j * self.chunk, self.chunk), :], self.box2.at[p, self.me],
            self.m.at[0, 0, p, o], self.m.at[1, 0, p, self.me], self.device(j),
        )

    def chunk_at(self, p, j):
        rows = rows16(self.core * self.half_rows + j * self.chunk, self.chunk)
        return self.sums.at[p, rows, :]

    def spread_copy(self, p, o):
        return remote(
            self.fin.at[p], self.chunk_at(p, self.me),
            self.m.at[0, 1, p, o], self.m.at[1, 1, p, self.me], self.device(self.peer(o)),
        )

    def keep_copy(self, p):
        return pltpu.make_async_copy(
            self.fin.at[p], self.chunk_at(p, self.me), self.s.at[0, 2, p]
        )

    def back_core(self, p):
        at = self.sums.at[p, rows16(self.core * self.half_rows, self.half_rows), :]
        return remote(
            at, at, self.s.at[0, 1, p], self.s.at[1, 1, p],
            (self.b + 1 - 2 * self.core, self.v),
        )

    def step0(self, p):
        self.core_copy(p).start()

    def step1(self, p):
        arrived(self.box1.at[p], self.s.at[1, 0, p])
        rows = rows16(self.core * self.half_rows, self.half_rows)
        total = self.source[p, rows, :].astype(F32) + self.box1[p].astype(F32)
        self.half[p] = total.astype(LOW)
        loop(1, self.peers, lambda o: self.many_copy(p, o).start())

    def step2(self, p):
        def take(o):
            j = self.peer(o)
            arrived(self.box2.at[p, j], self.m.at[1, 0, p, j])

        loop(1, self.peers, take)
        total = self.half[p, rows16(self.me * self.chunk, self.chunk), :].astype(F32)
        for o in range(1, self.peers):
            total = total + self.box2[p, self.peer(o)].astype(F32)
        self.fin[p] = total.astype(LOW)
        self.keep_copy(p).start()
        loop(1, self.peers, lambda o: self.spread_copy(p, o).start())

    def step3(self, p):
        def take(o):
            j = self.peer(o)
            arrived(self.chunk_at(p, j), self.m.at[1, 1, p, j])

        loop(1, self.peers, take)
        self.keep_copy(p).wait()
        self.back_core(p).start()

    def step4(self, p):
        rows = rows16((1 - self.core) * self.half_rows, self.half_rows)
        arrived(self.sums.at[p, rows, :], self.s.at[1, 1, p])
        self.core_copy(p).wait_send()
        loop(1, self.peers, lambda o: self.many_copy(p, o).wait_send())
        loop(1, self.peers, lambda o: self.spread_copy(p, o).wait_send())
        self.back_core(p).wait_send()


def backward_kernel(
    plan, count, qa_in, ka_in, va_in, att, d_att, xw, wq, wk, wv, d_first, ga, small,
    gi, sums, first_sums, last_sums, vectors,
    qa, ka, va,
    da, kt, dqt, dk, dv, dall, wcat, part, mate, own, final, dx, gacc, gb,
    bsum, box1, half, box2, box3, box4, fin, box1b, halfb, box2b, finb,
    ga0, box1c, halfc, box2c, box3c, box4c, finc,
    bias_mine, vec1, vec2, xs, firsts,
    p_send, p_recv, send, recv, local_sem, sa, ma, sb, mb, sc, mc, vs, vs2, load,
):
    nv, nw, hpd, hd = plan.nv, plan.nw, plan.hpd, plan.hd
    sub, sr, st, pairs = plan.sub, plan.sr, plan.st, plan.pairs
    slots, groups, pw, width = plan.slots, plan.groups, plan.pw, plan.width
    b, v, core, parity, slot, group = plan.here()
    mine = parity == core
    owner = b - core + parity
    base = plan.base(group)
    odds = [plan.odd(h, group) for h in range(hpd)]
    core_mate = (b + 1 - 2 * core, v)
    x_copy = pltpu.make_async_copy(xw, xs, load.at[0])
    first_copy = pltpu.make_async_copy(d_first, firsts, load.at[1])
    pair_copies = [
        [
            pltpu.make_async_copy(
                src.at[2 * pair : min(2 * pair + 2, hpd)],
                dst.at[2 * pair : min(2 * pair + 2, hpd)],
                load.at[2 + 3 * pair + n],
            )
            for n, (src, dst) in enumerate(((qa_in, qa), (ka_in, ka), (va_in, va)))
        ]
        for pair in range(pairs)
    ]
    for copies in pair_copies:
        for copy in copies:
            copy.start()
    x_copy.start()
    first_copy.start()
    greet(plan, b, v, core, across=True)
    tokens = Sums(
        plan, plan.piece, lambda p: ga.at[p], sums, box1, half, box2, box3, box4, fin, sa, ma
    )
    last = pairs - 1
    tail = ShortSums(plan, gb, last_sums, box1b, halfb, box2b, finb, sb, mb)
    opening = Sums(
        plan, ga0.shape[1], lambda p: ga0.at[p], first_sums,
        box1c, halfc, box2c, box3c, box4c, finc, sc, mc,
    )

    tile = lane_of((st, LANES))

    def prepare(i, pair):
        rows = rows16(i * st, st)
        for h in range(2 * pair, min(2 * pair + 2, hpd)):
            at = (h // 2) * LANES
            data = in_half(tile, odds[h], hd)
            column = extra_lane(tile, odds[h], hd)
            grad = d_att[i, :, :, at : at + LANES].reshape(st, LANES).astype(F32)
            prod = grad * att[i, :, :, at : at + LANES].reshape(st, LANES).astype(F32)
            delta = jnp.sum(jnp.where(data, prod, 0.0), axis=1, keepdims=True)
            high, mid, tail = (term.astype(F32) for term in three_parts(-delta))
            extra = jnp.where(column == 0, high, jnp.where(column == 1, mid, tail))
            da[h, rows, :] = jnp.where(
                data, grad, jnp.where((column >= 0) & (column < 3), extra, 0.0)
            ).astype(LOW)

    def open_pair(pair):
        for copy in pair_copies[pair]:
            copy.wait()
        for h in range(2 * pair, min(2 * pair + 2, hpd)):
            turned = jnp.transpose(ka[h])
            if hpd == 1:
                kt[h] = jnp.where(odds[h] == 1, turned[hd:], turned[:hd])
            else:
                kt[h] = turned[odds[h] * hd : (odds[h] + 1) * hd]
        loop(0, sub, lambda i: prepare(i, pair))

    for kind, ref in enumerate((wq, wk, wv)):
        wcat[:, kind * pw : (kind + 1) * pw] = ref[:, pl.ds(base, pw)]
    dk[...] = jnp.zeros_like(dk)
    dv[...] = jnp.zeros_like(dv)
    dqt[...] = jnp.zeros_like(dqt)
    gacc[...] = jnp.zeros_like(gacc)
    all_here(plan, across=True)
    tokens.step0(0)

    def attend(pair, qi, ki):
        rows, keys = pl.ds(pl.multiple_of(qi * st, st), st), pl.ds(pl.multiple_of(ki * st, st), st)
        key_parts, value_parts = [], []
        for h in range(2 * pair, min(2 * pair + 2, hpd)):
            q = qa[h, rows, :]
            d = da[h, rows, :]
            prob = jnp.exp(mm_nt(ka[h, keys, :], q))
            d_score = (prob * mm_nt(va[h, keys, :], d)).astype(LOW)
            value_parts.append(mm(prob.astype(LOW), d))
            key_parts.append(mm(d_score, q))
            dqt[pl.ds(pair * LANES + odds[h] * hd, hd), rows] += mm(kt[h, :, keys], d_score)
        if hpd == 1:
            key_parts.append(jnp.zeros_like(key_parts[0]))
            value_parts.append(jnp.zeros_like(value_parts[0]))
        first = in_half(tile, odds[2 * pair], hd)
        dv[pair, keys, :] += jnp.where(first, value_parts[0], value_parts[1])
        dk[pair, keys, :] += jnp.where(first, key_parts[0], key_parts[1])

    def gather_pair(pair, i):
        rows = rows16(i * st, st)
        at = pair * LANES
        dqt_block = dqt[at : at + LANES, pl.ds(pl.multiple_of(i * st, st), st)]
        dq = jnp.transpose(dqt_block)
        terms = (dq * (hd**-0.5), dk[pair, rows, :], dv[pair, rows, :])
        for kind, term in enumerate(terms):
            dall[rows, kind * pw + at : kind * pw + at + LANES] = term.astype(LOW)
        block = xs[rows, :]
        turned = (dqt_block * (hd**-0.5), jnp.transpose(terms[1]), jnp.transpose(terms[2]))
        for kind, term in enumerate(turned):
            gacc[kind * LANES : (kind + 1) * LANES, :] += mm(term.astype(LOW), block)
        for kind, row in ((0, 0), (2, 1)):
            bsum[row * 8 : row * 8 + 8, :] += fold_rows(terms[kind].astype(LOW).astype(F32))

    lanes = gb.shape[-1]

    def put_pair(pair, ref):
        if plan.piece > 3 * width or lanes > LANES:
            ref[...] = jnp.zeros_like(ref)
        at = base if hpd == 1 else pl.multiple_of(group * LANES, LANES)
        for kind in range(3):
            ref[0, kind * width : (kind + 1) * width, pl.ds(at, LANES)] = jnp.transpose(
                gacc[kind * LANES : (kind + 1) * LANES, :]
            ).astype(LOW)

    def put_vectors(ref, low):
        block = small[...].astype(LOW)
        for part in range(width // lanes):
            ref[0, low + 16 * part : low + 16 * part + 16, :] = block[
                :, part * lanes : (part + 1) * lanes
            ]

    x_copy.wait()

    bsum[...] = jnp.zeros_like(bsum)

    def put_bias(pair):
        at = base if hpd == 1 else pl.multiple_of(group * LANES, LANES)
        for row in range(2):
            bias_mine[2 * pair + row : 2 * pair + row + 1, pl.ds(at, LANES)] = jnp.sum(
                bsum[row * 8 : row * 8 + 8, :], axis=0, keepdims=True
            )
        bsum[...] = jnp.zeros_like(bsum)

    bias_mine[...] = jnp.zeros_like(bias_mine)
    for pair in range(pairs - 1):
        open_pair(pair)

        def square(t):
            tokens.at(pair * sub * sub + t + 1, count)
            attend(pair, t // sub, lax.rem(t, sub))

        loop(0, sub * sub, square)
        loop(0, sub, lambda i: gather_pair(pair, i))
        put_bias(pair)
        if pair == 0:
            put_pair(pair, ga0)
            put_vectors(ga0, 3 * width)
            opening.step0(0)
        gacc[...] = jnp.zeros_like(gacc)

    open_pair(last)
    before = last * sub * sub
    share = nv // groups
    mine_rows = share * sr

    def device_of(g):
        return b - core + g % 2, v - lax.rem(v, plan.cpw) + g // 2

    def part_copy(i, g):
        return remote(
            part.at[i, g * mine_rows : (g + 1) * mine_rows, :], mate.at[i, group],
            p_send.at[i, g], p_recv.at[i, group], device_of(g),
        )

    def send_parts(i):
        rows = rows16(i * st, st)
        total = mm_nt(dall[rows, :], wcat[...])
        part[i] = total.astype(LOW)
        own[i % 2] = total
        for g in range(groups):

            @pl.when(g != group)
            def _():
                part_copy(i, g).start()

    def final_copy(i, n):
        d = group * share + n
        return remote(
            final.at[i, n], dx.at[slot, i], send.at[i, n], recv.at[slot, i], (owner, d)
        )

    def is_own(n):
        return mine & (group * share + n == v)

    def own_copy(i, n):
        return pltpu.make_async_copy(final.at[i, n], dx.at[slot, i], local_sem.at[i])

    def send_final(i):
        total = own[i % 2, rows16(group * mine_rows, mine_rows), :]
        for g in range(groups):

            @pl.when(g != group)
            def _():
                arrived(mate.at[i, g], p_recv.at[i, g])

            @pl.when(g == group)
            def _():
                mate[i, g] = jnp.zeros((mine_rows, width), LOW)

        for g in range(groups):
            total = total + mate[i, g].astype(F32)
        final[i] = total.astype(LOW).reshape(share, sr, width)
        for n in range(share):

            @pl.when(is_own(n))
            def _():
                own_copy(i, n).start()

            @pl.when(jnp.logical_not(is_own(n)))
            def _():
                final_copy(i, n).start()

    def shrink(i):
        start = i * (2 * sub - i)

        def angle(t):
            done = start + t
            tokens.at(before + done + 1, count)
            if last > 0:
                for due, step in (
                    (1, opening.step1), (7, opening.step2), (11, opening.step3),
                    (16, opening.step4), (21, opening.step5),
                ):

                    @pl.when(done == due)
                    def _():
                        step(0)

            @pl.when((t == 1) & (i > 0))
            def _():
                send_final(i - 1)

            n = sub - i
            attend(
                last, jnp.where(t < n, i, i + 1 + t - n), jnp.where(t < n, i + t, i)
            )

        loop(0, 2 * (sub - i) - 1, angle)
        gather_pair(last, i)

        @pl.when(i == sub - 1)
        def _():
            put_pair(last, gb)
            if last == 0:
                put_vectors(gb, 3 * width)
            tail.step0(0)

        send_parts(i)

        @pl.when(i == sub - 1)
        def _():
            tail.step1(0)
            if sub > 1:
                send_final(sub - 2)

    loop(0, sub, shrink)
    tiles = before + sub * sub
    put_bias(last)
    core_vec = remote(bias_mine, vec1, vs.at[0], vs.at[1], core_mate)
    core_vec.start()
    send_final(sub - 1)
    arrived(vec1, vs.at[1])
    core_vec.wait_send()
    bias_mine[...] = bias_mine[...] + vec1[...]

    def vec_spread(o):
        return remote(
            bias_mine, vec2.at[tail.me], vs2.at[0, o], vs2.at[1, tail.me],
            tail.device(tail.peer(o)),
        )

    loop(1, 2 * nv, lambda o: vec_spread(o).start())
    vec2[tail.me] = bias_mine[...]
    first_copy.wait()

    def finish(i):
        for n in range(share):

            @pl.when(is_own(n))
            def _():
                own_copy(i, n).wait()

        for w in range(nw):
            self_sent = mine & (slot == w) & (v // share == group)

            @pl.when(jnp.logical_not(self_sent))
            def _():
                arrived(dx.at[w, i], recv.at[w, i])

        gi[:, i] = (firsts[:, i] + dx[:, i].astype(F32)).astype(LOW)

    if last > 0:
        opening.step6(0)
    tail.step2(0)
    loop(tiles + 1, max(tiles + 1, tokens.end(count)), lambda t: tokens.at(t, count))
    if last > 0:
        opening.step7(0)
    loop(0, sub - 1, finish)

    def vec_take(o):
        j = tail.peer(o)
        arrived(vec2.at[j], vs2.at[1, j])

    loop(1, 2 * nv, vec_take)
    total = vec2[0]
    for j in range(1, 2 * nv):
        total = total + vec2[j]
    vectors[...] = total
    loop(sub - 1, sub, finish)
    tail.step3(0)
    if last > 0:
        opening.step8(0)

    def close(i):
        for n in range(share):

            @pl.when(jnp.logical_not(is_own(n)))
            def _():
                final_copy(i, n).wait_send()

        for g in range(groups):

            @pl.when(g != group)
            def _():
                part_copy(i, g).wait_send()

    loop(0, sub, close)
    loop(1, 2 * nv, lambda o: vec_spread(o).wait_send())
    tail.step4(0)


def output_kernel(
    plan, ff, sums, first_sums, last_sums, vectors,
    gq, gk, gv, go, gu, gd, bq, bv, bo, g1, s1, bu, bd, g2, s2,
    block_in, first_in, last_in, block_out, wide_out, load, store,
):
    width = plan.width
    blocks = ff // width
    lanes = last_in.shape[-1]
    total = 2 * blocks + 1

    def block_loads(n):
        at = (n % 3) * width
        return [
            pltpu.make_async_copy(
                sums.at[2 * (n // 3) + side, at : at + width, :],
                block_in.at[n, :, side * (width // 2) : (side + 1) * (width // 2)],
                load.at[2 * n + side],
            )
            for side in range(2)
        ]

    def block_store(n):
        if n == 2 * blocks:
            dst = go
        elif n % 2:
            dst = gd.at[n // 2 * width : (n // 2 + 1) * width, :]
        else:
            dst = gu.at[:, n // 2 * width : (n // 2 + 1) * width]
        return pltpu.make_async_copy(block_out.at[n], dst, store.at[n])

    parts = [(first_sums, first_in), (last_sums, last_in)][2 - min(plan.pairs, 2) :]
    part_loads = [
        pltpu.make_async_copy(src, dst, load.at[2 * total + n]) for n, (src, dst) in enumerate(parts)
    ]
    wide_stores = [
        pltpu.make_async_copy(wide_out.at[n], dst, store.at[total + n])
        for n, dst in enumerate((gq, gk, gv))
    ]
    for n in range(total):
        for copy in block_loads(n):
            copy.start()
    for copy in part_loads:
        copy.start()
    for n in range(total):
        for copy in block_loads(n):
            copy.wait()
        block_out[n] = block_in[n].astype(F32)
        block_store(n).start()
    for copy in part_loads:
        copy.wait()
    groups = lanes // LANES
    for kind in range(3):
        for pair, (_, ref) in enumerate(parts):
            for group in range(groups):
                at = (group * plan.pairs + pair) * LANES
                wide_out[kind, :, at : at + LANES] = ref[
                    0, kind * width : (kind + 1) * width, group * LANES : (group + 1) * LANES
                ].astype(F32)
        wide_stores[kind].start()
    low = 3 * width
    ref = parts[0][1]
    rows = jnp.concatenate(
        [ref[0, low + 16 * n : low + 16 * n + 16, :] for n in range(width // lanes)], axis=1
    ).astype(F32)
    for n, ref in enumerate((g2, s2, bd, g1, s1, bo)):
        ref[...] = rows[n]
    for f in range(blocks):
        bu[f * width : (f + 1) * width] = rows[6 + f]
    for row, ref in enumerate((bq, bv)):
        for pair in range(plan.pairs):
            for group in range(groups):
                at = (group * plan.pairs + pair) * LANES
                ref[at : at + LANES] = vectors[2 * pair + row, group * LANES : (group + 1) * LANES]
    for n in range(total):
        block_store(n).wait()
    for copy in wide_stores:
        copy.wait()


def params(number):
    return pltpu.CompilerParams(
        vmem_limit_bytes=VMEM_BYTES, collective_id=number, has_side_effects=True
    )


def sum_scratch(plan, number, lanes, piece):
    nh = plan.nv // 2
    return [
        pltpu.VMEM((number, piece // 2, lanes), LOW),
        pltpu.VMEM((number, piece // 2, lanes), LOW),
        pltpu.VMEM((number, piece // 4, lanes), LOW),
        pltpu.VMEM((number, piece // 8, lanes), LOW),
        pltpu.VMEM((number, nh, piece // 8 // nh, lanes), LOW),
        pltpu.VMEM((number, piece // 8 // nh, lanes), LOW),
    ]


def short_scratch(plan, rows, lanes):
    peers = 2 * plan.nv
    return [
        pltpu.VMEM((1, rows // 2, lanes), LOW),
        pltpu.VMEM((1, rows // 2, lanes), LOW),
        pltpu.VMEM((1, peers, rows // 2 // peers, lanes), LOW),
        pltpu.VMEM((1, rows // 2 // peers, lanes), LOW),
    ]


def sum_sems(number, steps, peers):
    return [DMA((2, steps, number)), DMA((2, 2, number, peers))]


def body(
    plan,
    inputs, w_query, w_key, w_value, w_out, b_query, b_value, b_out, gain_one, shift_one,
    w_up, b_up, w_down, b_down, gain_two, shift_two, cotangent, valid_mask,
):
    nv, nw, width = plan.nv, plan.nw, plan.width
    slots, hpd, hd, pw, groups = plan.slots, plan.hpd, plan.hd, plan.pw, plan.groups
    sub, sr, st, pairs = plan.sub, plan.sr, plan.st, plan.pairs
    ff = w_up.shape[1]
    rows, cr = plan.rows, nw * sr
    piece = plan.piece
    shape = jax.ShapeDtypeStruct
    ANY = pl.BlockSpec(memory_space=pl.ANY)
    count = (2 * ff // width + 1) // 3 * 2

    heads = shape((hpd, slots, LANES), LOW)
    blocked = (nw, sub, sr, width)
    mask = valid_mask.reshape(nv, sub, sr).transpose(1, 0, 2).reshape(slots // LANES, LANES)
    qa, ka, va, xw, att, out, d_first, d_att, ga, small = pl.pallas_call(
        functools.partial(forward_kernel, plan, ff),
        out_shape=(
            heads,
            heads,
            heads,
            shape((sub, nv, sr, width), LOW),
            shape((sub, nv, sr, pw), LOW),
            shape(blocked, LOW),
            shape(blocked, F32),
            shape((sub, nv, sr, pw), LOW),
            shape((count, piece, width // 2), LOW),
            shape((16, width), F32),
        ),
        in_specs=[VM] * 7 + [ANY, ANY] + [VM] * 3 + [ANY, VM, ANY] + [VM] * 3,
        out_specs=(ANY,) * 7 + (VM, ANY, VM),
        scratch_shapes=[
            pltpu.VMEM((hpd, slots, LANES), LOW),
            pltpu.VMEM((hpd, slots, LANES), LOW),
            pltpu.VMEM((hpd, slots, LANES), LOW),
            pltpu.VMEM((sub, nv, sr, width), LOW),
            pltpu.VMEM((sub, nv, sr, pw), LOW),
            pltpu.VMEM(blocked, F32),
            pltpu.VMEM(blocked, LOW),
            pltpu.VMEM((width, width), LOW),
            pltpu.VMEM((width, ff), LOW),
            pltpu.VMEM((ff, width), LOW),
            pltpu.VMEM((width, max(3 * hpd * LANES, 2 * width)), LOW),
            pltpu.VMEM((slots, LANES), LOW),
            pltpu.VMEM((8, width), F32),
            pltpu.VMEM((hpd, max((sub - 1) * st, ff // LANES // hpd * cr), LANES), F32),
            pltpu.VMEM((nw, groups, sub, sr, pw), LOW),
            pltpu.VMEM((rows, width), LOW),
            pltpu.VMEM((rows, width), LOW),
            pltpu.VMEM((rows, ff), LOW),
            pltpu.VMEM((rows, ff), LOW),
            pltpu.VMEM((rows, width), LOW),
            pltpu.VMEM((rows, width), LOW),
            DMA((sub, nv)),
            DMA((sub, nv)),
            DMA((sub, nv)),
            DMA((sub, nv)),
            DMA((nw, groups, sub)),
            DMA((sub,)),
            DMA((sub, nw, groups)),
            DMA((sub, nv)),
            DMA((sub,)),
            DMA,
            DMA((2, 2)),
            DMA((4,)),
            DMA((7,)),
        ],
        compiler_params=params(1),
        name="forward_and_tokens",
    )(
        inputs.reshape(blocked), w_query, w_key, w_value, b_query, b_value, mask,
        cotangent.reshape(blocked), w_out, b_out, gain_one, shift_one,
        w_up, b_up, w_down, b_down, gain_two, shift_two,
    )

    share = nv // groups
    lanes = width // pairs
    unit = 16 * 4 * nv
    more = -(-(3 * width + 16 * width // lanes) // unit) * unit
    first_rows = more if pairs > 1 else unit
    last_rows = piece if pairs > 1 else more
    gi, sums, first_sums, last_sums, vectors = pl.pallas_call(
        functools.partial(backward_kernel, plan, count),
        out_shape=(
            shape(blocked, LOW),
            shape((count, piece, width // 2), LOW),
            shape((1, first_rows, lanes), LOW),
            shape((1, last_rows, lanes), LOW),
            shape((8, lanes), F32),
        ),
        in_specs=[ANY] * 3 + [VM] * 2 + [ANY] + [VM] * 3 + [ANY, ANY, VM],
        out_specs=(VM, ANY, ANY, ANY, VM),
        scratch_shapes=[
            pltpu.VMEM((hpd, slots, LANES), LOW),
            pltpu.VMEM((hpd, slots, LANES), LOW),
            pltpu.VMEM((hpd, slots, LANES), LOW),
            pltpu.VMEM((hpd, slots, LANES), LOW),
            pltpu.VMEM((hpd, hd, slots), LOW),
            pltpu.VMEM((pw, slots), F32),
            pltpu.VMEM((pairs, slots, LANES), F32),
            pltpu.VMEM((pairs, slots, LANES), F32),
            pltpu.VMEM((slots, 3 * pw), LOW),
            pltpu.VMEM((width, 3 * pw), LOW),
            pltpu.VMEM((sub, st, width), LOW),
            pltpu.VMEM((sub, groups, share * sr, width), LOW),
            pltpu.VMEM((2, st, width), F32),
            pltpu.VMEM((sub, share, sr, width), LOW),
            pltpu.VMEM((nw, sub, sr, width), LOW),
            pltpu.VMEM((3 * LANES, width), F32),
            pltpu.VMEM((1, last_rows, lanes), LOW),
            pltpu.VMEM((16, LANES), F32),
        ]
        + sum_scratch(plan, count, width // 2, piece)
        + short_scratch(plan, last_rows, lanes)
        + [pltpu.VMEM((1, first_rows, lanes), LOW)]
        + sum_scratch(plan, 1, lanes, first_rows)
        + [
            pltpu.VMEM((8, lanes), F32),
            pltpu.VMEM((8, lanes), F32),
            pltpu.VMEM((2 * nv, 8, lanes), F32),
            pltpu.VMEM((slots, width), LOW),
            pltpu.VMEM(blocked, F32),
            DMA((sub, groups)),
            DMA((sub, groups)),
            DMA((sub, share)),
            DMA((nw, sub)),
            DMA((sub,)),
        ]
        + sum_sems(count, 8, nv // 2)
        + sum_sems(1, 3, 2 * nv)
        + sum_sems(1, 8, nv // 2)
        + [DMA((2,)), DMA((2, 2 * nv)), DMA((2 + 3 * pairs,))],
        compiler_params=params(2),
        name="attention_backward",
    )(
        qa, ka, va, att, d_att, xw.reshape(slots, width), w_query, w_key, w_value, d_first,
        ga, small,
    )

    square = shape((width, width), F32)
    one = shape((width,), F32)
    total = 2 * ff // width + 1
    gq, gk, gv, go, gu, gd, bq, bv, bo, g1, s1, bu, bd, g2, s2 = pl.pallas_call(
        functools.partial(output_kernel, plan, ff),
        out_shape=(square,) * 4
        + (shape((width, ff), F32), shape((ff, width), F32))
        + (one,) * 5
        + (shape((ff,), F32),)
        + (one,) * 3,
        in_specs=[ANY] * 3 + [VM],
        out_specs=(ANY,) * 6 + (VM,) * 9,
        scratch_shapes=[
            pltpu.VMEM((total, width, width), LOW),
            pltpu.VMEM((1, first_rows, lanes), LOW),
            pltpu.VMEM((1, last_rows, lanes), LOW),
            pltpu.VMEM((total, width, width), F32),
            pltpu.VMEM((3, width, width), F32),
            DMA((2 * total + 2,)),
            DMA((total + 3,)),
        ],
        compiler_params=pltpu.CompilerParams(vmem_limit_bytes=VMEM_BYTES),
        name="outputs",
    )(sums, first_sums, last_sums, vectors)
    return (
        out.reshape(inputs.shape), gi.reshape(inputs.shape),
        gq, gk, gv, go, bq, bv, bo, g1, s1, gu, bu, gd, bd, g2, s2,
    )


def solution(mesh):
    data = P("batch", "var", None)

    def run(*args):
        plan = Plan(mesh, args[0].shape)
        return jax.shard_map(
            functools.partial(body, plan),
            mesh=mesh,
            in_specs=(data,) + (P(),) * 15 + (data, P()),
            out_specs=(data, data) + (P(),) * 15,
            check_vma=False,
        )(*args)

    return run
```
